256 devices in a mesh: pipe: 8 (over y, x_lo), dp: 32 (over x_hi, z, core).
Axes of the slice: x: 4 (x_hi: 2, x_lo: 2; x = x_hi * 2 + x_lo), y: 4, z: 8, core: 2. Of those that a mesh axis runs over, the one named last changes fastest.
Arguments:
- latents: bfloat16 [4, 32, 56, 1536], P(None, 'dp'), may hold values from -6 to 6
- out_grad: bfloat16 [4, 32, 56, 1536], P(None, 'dp'), may hold values from -0.0625 to 0.0625
- w_qkv: bfloat16 [8, 1536, 4608], P('pipe', 'dp'), may hold values from -0.15625 to 0.15625
- mod_table: float32 [8, 16, 3, 1536], P('pipe'), may hold values from -4 to 4
- timesteps: int32 [4, 32], P(None, 'dp'), may hold values from 0 to 15
- text_len: int32 [4, 32], P(None, 'dp'), may hold values from 1 to 16, as said below
Outputs:
- grad_qkv: float32 [8, 1536, 4608], P('pipe', 'dp')
The draws below stay inside these ranges and needn't reach their ends.
Inputs may be any that keep to these rules, and one draw needn't show every extreme that they name: `text_len`: some sample has all 16 text tokens live.
All inputs are finite; a program needn't handle non-finite values.
Results may differ from the reference program's by a relative error of at most 0.024.
Values may be sent and summed in bfloat16 or wider, within the bound.
No kernel may reach another device: no remote copies, remote signals or barrier semaphores. Data moves between devices by JAX's collectives and lax.ppermute only.
A program may use at most 128 MiB of HBM per device.

```python
import math
import jax
import jax.numpy as jnp
from jax import lax

D = 1536
HEADS = 12
HDIM = 128
IMG = 40
TXT = 16
MB = 4
NSTEP = 16
SEQ = 56
N_PIPE = 8
N_DP = 32


def draw_text_len(key, part):
    key = jax.random.fold_in(key, 7)
    first_key, second_key = jax.random.split(key)
    drawn = jax.random.randint(first_key, (MB * N_DP,), 1, TXT + 1)
    chosen = jax.random.randint(second_key, (), 0, MB * N_DP)
    filled = jnp.where(jnp.arange(MB * N_DP) == chosen, TXT, drawn)
    return filled.reshape(MB, N_DP).astype(jnp.int32)


def plant(values, own_key, smallest, top_value):
    index_at = [jax.random.randint(jax.random.fold_in(own_key, axis), (), 0, length) for axis, length in enumerate(values.shape)]
    longest = values.shape.index(max(values.shape))
    next_to = index_at[:longest] + [(index_at[longest] + 1) % values.shape[longest]] + index_at[longest + 1:]
    return values.at[tuple(index_at)].set(smallest).at[tuple(next_to)].set(top_value)


def with_spikes(entries, own_key, source, target, parts, factor):
    owner, partner = [(jnp.arange(entries.shape[dim]) // (entries.shape[dim] // parts)).reshape([-1 if axis == dim else 1 for axis in range(entries.ndim)]) for dim in (source, target)]
    chosen = jax.random.permutation(own_key, parts)[partner]
    strong = (owner == chosen) | (owner == (partner + parts // 2) % parts)
    return jnp.where(strong, factor * entries, entries)


def block_levels(rng, shape, cuts, smallest, high):
    level, own = 1.0, jax.random.fold_in(rng, 6)
    for axis_at, blocks in cuts:
        draws = jnp.exp(jax.random.uniform(jax.random.fold_in(own, axis_at), (blocks,), jnp.float32, smallest / len(cuts), high / len(cuts)))
        level = level * jnp.repeat(draws, shape[axis_at] // blocks).reshape([-1 if axis == axis_at else 1 for axis in range(len(shape))])
    return level


def gaussian(stream_key, extent, scale, most, pieces=(), kind=jnp.bfloat16):
    result = scale * jax.random.normal(stream_key, extent, jnp.float32)
    if pieces:
        result = result * block_levels(stream_key, extent, pieces, -0.22, 0.18)
    return jnp.clip(result, -most, most).astype(kind)


def noise_with(own_key, dims, deviation, most, cuts, heavy, kind=jnp.bfloat16):
    result = deviation * jax.random.normal(own_key, dims, jnp.float32)
    if cuts:
        result = result * block_levels(own_key, dims, cuts, -0.22, 0.18)
    return jnp.clip(with_spikes(result, jax.random.fold_in(own_key, 3), *heavy), -most, most).astype(kind)


def setup_inputs(seed: int = 0) -> dict:
    splits = jax.random.split(jax.random.key(seed), 7)
    return {
        "latents": noise_with(splits[0], (MB, N_DP, SEQ, D), 1.0, 6.0, ((1, 32),), (1, 3, 32, 2.75)),
        "out_grad": gaussian(splits[1], (MB, N_DP, SEQ, D), (MB * SEQ * N_DP) ** -0.5, 0.0625, ((1, 32),)),
        "w_qkv": gaussian(splits[2], (N_PIPE, D, 3 * D), D ** -0.5, 0.15625, ((0, 8), (1, 32))),
        "mod_table": gaussian(splits[3], (N_PIPE, NSTEP, 3, D), 0.7, 4.0, ((0, 8),), jnp.float32),
        "timesteps": plant(jax.random.randint(splits[4], (MB, N_DP), 0, NSTEP), jax.random.fold_in(splits[4], 1), 0, NSTEP - 1).astype(jnp.int32),
        "text_len": draw_text_len(jax.random.fold_in(splits[6], 71), 0),
    }


EPS = 1e-06

def modnorm(hidden, modulation):
    average = lax.optimization_barrier(jnp.mean(hidden, axis=-1, keepdims=True))
    centered = hidden - average
    variance = lax.optimization_barrier(jnp.mean(centered * centered, axis=-1, keepdims=True))
    return (1.0 + modulation[1]) * (centered * lax.rsqrt(variance + EPS)) + modulation[0]

def attend(projected, hidden, modulation, length):
    seq_len = hidden.shape[0]
    model_width = hidden.shape[1]
    queries = projected[:, :model_width].reshape(seq_len, HEADS, HDIM)
    key_rows = projected[:, model_width:2 * model_width].reshape(seq_len, HEADS, HDIM)
    values = projected[:, 2 * model_width:].reshape(seq_len, HEADS, HDIM)
    queries = queries * lax.rsqrt(lax.optimization_barrier(jnp.mean(queries * queries, axis=-1, keepdims=True)) + EPS)
    key_rows = key_rows * lax.rsqrt(lax.optimization_barrier(jnp.mean(key_rows * key_rows, axis=-1, keepdims=True)) + EPS)
    scores = jnp.einsum('qhc,khc->hqk', queries, key_rows) / math.sqrt(HDIM)
    position = jnp.arange(seq_len, dtype=jnp.int32)
    usable = ((position < IMG) | (position - IMG < length)).astype(jnp.float32)
    weights = jnp.exp(scores) * usable
    attention = weights / lax.optimization_barrier(jnp.sum(weights, axis=-1, keepdims=True))
    mixture = jnp.einsum('hqk,khc->qhc', attention, values).reshape(seq_len, model_width)
    return hidden + modulation[2] * mixture

def section_forward(hidden_in, weight_full, modulation, length):
    hidden = hidden_in.astype(jnp.float32)
    normed = modnorm(hidden, modulation).astype(jnp.bfloat16)
    projected = jnp.dot(normed, weight_full, preferred_element_type=jnp.float32)
    output = attend(projected, hidden, modulation, length).astype(jnp.bfloat16)
    return (output, normed, projected)

def section_backward(cotangent, projected, hidden_in, weight_full, modulation, length):
    hidden = hidden_in.astype(jnp.float32)
    _, pullback = jax.vjp(lambda proj, state: attend(proj, state, modulation, length), projected, hidden)
    proj_grad, direct_grad = pullback(cotangent.astype(jnp.float32))
    proj_low = proj_grad.astype(jnp.bfloat16)
    norm_grad = lax.dot_general(proj_low, weight_full, (((1,), (1,)), ((), ())), preferred_element_type=jnp.float32)
    _, norm_pull = jax.vjp(lambda state: modnorm(state, modulation), hidden)
    input_grad, = norm_pull(norm_grad)
    return ((direct_grad + input_grad).astype(jnp.bfloat16), proj_low)

def device_sums(normed, proj_low):
    left_rows = normed.reshape(MB, N_DP, SEQ, D).transpose(1, 0, 2, 3).reshape(N_DP, MB * SEQ, D)
    right_rows = proj_low.reshape(MB, N_DP, SEQ, 3 * D).transpose(1, 0, 2, 3).reshape(N_DP, MB * SEQ, 3 * D)

    def accumulate(total, pair):
        partial_sum = lax.dot_general(pair[0], pair[1], (((0,), (0,)), ((), ())), preferred_element_type=jnp.float32)
        rounded = lax.optimization_barrier(partial_sum.astype(jnp.bfloat16))
        return (total + rounded.astype(jnp.float32), None)
    total, _ = lax.scan(accumulate, jnp.zeros((D, 3 * D), jnp.float32), (left_rows, right_rows))
    return total

def reference(latents, out_grad, w_qkv, mod_table, timesteps, text_len):
    batch_size = MB * N_DP
    states = latents.reshape(batch_size, SEQ, D)
    levels = timesteps.reshape(batch_size)
    lengths = text_len.reshape(batch_size)
    saved = []
    for section_index in range(N_PIPE):
        modulation = mod_table[section_index][levels]
        output, normed, projected = jax.vmap(section_forward, in_axes=(0, None, 0, 0))(states, w_qkv[section_index], modulation, lengths)
        saved.append((states, normed, projected, modulation))
        states = output
    cotangent = out_grad.reshape(batch_size, SEQ, D)
    grads = [None] * N_PIPE
    for section_index in reversed(range(N_PIPE)):
        inputs, normed, projected, modulation = saved[section_index]
        cotangent, proj_low = jax.vmap(section_backward, in_axes=(0, 0, 0, None, 0, 0))(cotangent, projected, inputs, w_qkv[section_index], modulation, lengths)
        grads[section_index] = device_sums(normed, proj_low)
    return jnp.stack(grads)
```

```python
import functools
import math

import jax
import jax.numpy as jnp
from jax import lax
from jax.experimental import pallas as pl
from jax.experimental.pallas import tpu as pltpu
from jax.sharding import Mesh
from jax.sharding import PartitionSpec as P

IMG = 40
EPS = 1e-06
HDIM = 128
BLOCKS = 8
QUART = 4
PAIR = 2
F32 = jnp.float32
BF16 = jnp.bfloat16
VM = pl.BlockSpec(memory_space=pltpu.VMEM)
SM = pl.BlockSpec(memory_space=pltpu.SMEM)
ANY = pl.BlockSpec(memory_space=pl.ANY)


def place(scal, k):
    p = scal[2]
    j = lax.max((k - p + 2) // 2 - 1, 0)
    j = lax.min(j, BLOCKS // 2 - 1)
    return lax.rem(k + p, 2), j


def fetch_weights(scal, pieces, wscr, sem):
    c = scal[1]
    halves = wscr.shape[0]

    def start(own, other):
        for t in range(halves):
            pltpu.make_async_copy(own.at[:, t], wscr.at[t, :, c], sem).start()
            pltpu.make_async_copy(other.at[:, t], wscr.at[t, :, 1 - c], sem).start()

    if len(pieces) == 2:
        start(*pieces)
    else:

        @pl.when(scal[2] == 0)
        def _():
            start(*pieces[:2])

        @pl.when(scal[2] != 0)
        def _():
            start(*pieces[2:])


def await_weights(wscr, sem):
    pltpu.make_async_copy(wscr, wscr, sem).wait()


def half_weights(wscr, t):
    value = wscr[t]
    return value.reshape(value.shape[0] * value.shape[1] * value.shape[2], value.shape[3])


def standardize(hidden):
    average = jnp.mean(hidden, axis=-1, keepdims=True)
    centered = hidden - average
    variance = jnp.mean(centered * centered, axis=-1, keepdims=True)
    scale = lax.rsqrt(variance + EPS)
    return centered * scale, scale


def nt(a, b):
    return lax.dot_general(
        a.astype(BF16), b.astype(BF16), (((1,), (1,)), ((), ())), preferred_element_type=F32
    )


def nn(a, b):
    return lax.dot_general(
        a.astype(BF16), b.astype(BF16), (((1,), (0,)), ((), ())), preferred_element_type=F32
    )


def tn(a, b):
    return lax.dot_general(
        a.astype(BF16), b.astype(BF16), (((0,), (0,)), ((), ())), preferred_element_type=F32
    )


def unit(rows):
    scale = lax.rsqrt(jnp.mean(rows * rows, axis=-1, keepdims=True) + EPS)
    return rows * scale, scale


def weights_of(q, k, length):
    scores = nt(q, k) * (1.0 / math.sqrt(HDIM))
    position = lax.broadcasted_iota(jnp.int32, scores.shape, 1)
    usable = (position < IMG) | (position - IMG < length)
    weights = jnp.where(usable, jnp.exp(scores), 0.0)
    return weights / jnp.sum(weights, axis=-1, keepdims=True)


def forward_kernel(k, n_in, n_w, send, scal, *refs):
    ins, refs = refs[:n_in], refs[n_in:]
    mods, gates = refs[:2]
    pieces, refs = refs[2 : 2 + n_w], refs[2 + n_w :]
    if send:
        out_ref, refs = refs[0], refs[1:]
    hidden_ref, normed_ref, proj_ref, wscr, hs, sem = refs
    fetch_weights(scal, pieces, wscr, sem)
    y = scal[0]
    micro, j = place(scal, k)
    chunk = hs.shape[2]

    def from_whole(ref):
        for t in range(QUART):
            hs[t] = ref[:, t * chunk : (t + 1) * chunk]

    def from_chunks(parts):
        for d in range(QUART):
            hs[lax.rem(y + QUART - d, QUART)] = parts[d][...]

    if n_in == 1:
        from_whole(ins[0])
    elif n_in == QUART:
        from_chunks(ins)
    else:

        @pl.when(scal[2] == 0)
        def _():
            from_whole(ins[0])

        @pl.when(scal[2] != 0)
        def _():
            from_chunks(ins[1:])

    for t in range(QUART):
        hidden_ref[:, t * chunk : (t + 1) * chunk] = hs[t]
    rows, width = hidden_ref.shape
    seq = rows // PAIR
    normal, _ = standardize(hidden_ref[...].astype(F32))
    normal = normal.reshape(PAIR, seq, width)
    normed = jnp.concatenate(
        [
            (1.0 + mods[j, PAIR * micro + s, 1:2, :]) * normal[s]
            + mods[j, PAIR * micro + s, 0:1, :]
            for s in range(PAIR)
        ],
        axis=0,
    ).astype(BF16)
    normed_ref[...] = normed
    await_weights(wscr, sem)
    halves = wscr.shape[0]
    span = width // halves
    projected = nn(normed[:, :span], half_weights(wscr, 0))
    for t in range(1, halves):
        projected += nn(normed[:, t * span : (t + 1) * span], half_weights(wscr, t))
    proj_ref[...] = projected
    if not send:
        return
    own = hs[y].astype(F32)
    for s in range(PAIR):
        length = scal[3 + PAIR * micro + s]
        r = slice(s * seq, (s + 1) * seq)
        mixed = []
        for h in range(chunk // HDIM):
            lo = h * HDIM
            q, _ = unit(proj_ref[r, lo : lo + HDIM])
            key, _ = unit(proj_ref[r, chunk + lo : chunk + lo + HDIM])
            v = proj_ref[r, 2 * chunk + lo : 2 * chunk + lo + HDIM]
            mixed.append(nn(weights_of(q, key, length), v))
        mixture = jnp.concatenate(mixed, axis=1)
        gate = gates[j, PAIR * micro + s]
        hs_rows = own[r] + gate * mixture
        if s == 0:
            first = hs_rows
    out_ref[...] = jnp.concatenate([first, hs_rows], axis=0).astype(BF16)


def backward_kernel(k, n_in, n_w, send, scal, *refs):
    ins, refs = refs[:n_in], refs[n_in:]
    mods, gates, hidden_ref, proj_ref = refs[:4]
    pieces, refs = refs[4 : 4 + n_w], refs[4 + n_w :]
    outs, refs = refs[: QUART * send], refs[QUART * send :]
    low_ref, wscr, gs, dp, ds, sem = refs
    if send:
        fetch_weights(scal, pieces, wscr, sem)
    y = scal[0]
    micro, j = place(scal, k)
    rows, width = hidden_ref.shape
    chunk = width // QUART
    seq = rows // PAIR

    def total(parts):
        gs[...] = sum([part[...].astype(F32) for part in parts[1:]], parts[0][...].astype(F32))

    if n_in == 1:
        total(ins)
    elif n_in == QUART:
        total(ins)
    else:

        @pl.when(scal[2] != 0)
        def _():
            total(ins[:1])

        @pl.when(scal[2] == 0)
        def _():
            total(ins[1:])

    root = 1.0 / math.sqrt(HDIM)
    for s in range(PAIR):
        length = scal[3 + PAIR * micro + s]
        r = slice(s * seq, (s + 1) * seq)
        for h in range(chunk // HDIM):
            lo = h * HDIM
            c = slice(lo, lo + HDIM)
            gate = gates[j, PAIR * micro + s, :, c]
            dmix = gs[r, c] * gate
            q, rq = unit(proj_ref[r, lo : lo + HDIM])
            key, rk = unit(proj_ref[r, chunk + lo : chunk + lo + HDIM])
            v = proj_ref[r, 2 * chunk + lo : 2 * chunk + lo + HDIM]
            att = weights_of(q, key, length)
            datt = nt(dmix, v)
            dscore = att * (datt - jnp.sum(att * datt, axis=-1, keepdims=True)) * root
            dqn = nn(dscore, key)
            dkn = tn(dscore, q)
            dp[r, c] = rq * (dqn - q * jnp.mean(dqn * q, axis=-1, keepdims=True))
            dp[r, chunk + lo : chunk + lo + HDIM] = rk * (
                dkn - key * jnp.mean(dkn * key, axis=-1, keepdims=True)
            )
            dp[r, 2 * chunk + lo : 2 * chunk + lo + HDIM] = tn(att, dmix)
    low = dp[...].astype(BF16)
    low_ref[...] = low
    if not send:
        return
    normal, scale = standardize(hidden_ref[...].astype(F32))
    await_weights(wscr, sem)
    halves = wscr.shape[0]
    norm_grad = jnp.concatenate([nt(low, half_weights(wscr, t)) for t in range(halves)], axis=1)
    norm_grad = norm_grad.reshape(PAIR, seq, width)
    grad = jnp.concatenate(
        [(1.0 + mods[j, PAIR * micro + s, 1:2, :]) * norm_grad[s] for s in range(PAIR)], axis=0
    )
    back = scale * (
        grad
        - jnp.mean(grad, axis=-1, keepdims=True)
        - normal * jnp.mean(grad * normal, axis=-1, keepdims=True)
    )
    for t in range(QUART):
        ds[t] = back[:, t * chunk : (t + 1) * chunk]
    ds[y] = ds[y] + gs[...]
    for d in range(QUART):
        outs[d][...] = ds[lax.rem(y + d, QUART)].astype(BF16)


def weight_grad_kernel(scal, n0, n1, n2, g0, g1, g2, out, nscr, gscr, sems):
    c = scal[1]
    rows = n0.shape[0]

    def start(normed, grad):
        pltpu.make_async_copy(normed, nscr.at[0:rows], sems.at[0]).start()
        pltpu.make_async_copy(grad, gscr.at[0:rows], sems.at[1]).start()

    pltpu.make_async_copy(n1, nscr.at[rows : 2 * rows], sems.at[2]).start()
    pltpu.make_async_copy(g1, gscr.at[rows : 2 * rows], sems.at[3]).start()

    @pl.when(scal[2] == 0)
    def _():
        start(n0, g0)

    @pl.when(scal[2] != 0)
    def _():
        start(n2, g2)

    pltpu.make_async_copy(n0, nscr.at[0:rows], sems.at[0]).wait()
    pltpu.make_async_copy(g0, gscr.at[0:rows], sems.at[1]).wait()
    pltpu.make_async_copy(n1, nscr.at[rows : 2 * rows], sems.at[2]).wait()
    pltpu.make_async_copy(g1, gscr.at[rows : 2 * rows], sems.at[3]).wait()
    cores, depth, halves, share, _ = out.shape
    width = nscr.shape[1]
    per = 384
    groups = per // share
    right = gscr[...]
    for t in range(width // per):
        value = tn(nscr[:, t * per : (t + 1) * per], right).astype(BF16)
        for u in range(groups):
            at = t * groups + u
            core = at % cores
            half, z = divmod(at // cores, depth)
            where = lax.rem(core + c, cores)
            out[where, z, half] = value[u * share : (u + 1) * share]


def shards(latents, out_grad, w_qkv, mod_table, timesteps, text_len):
    y = lax.axis_index("y")
    p = lax.axis_index("xl")
    half = lax.axis_index("xh")
    core = lax.axis_index("c")
    halves = lax.axis_size("xh")
    depth = lax.axis_size("z")
    cores = lax.axis_size("c")
    count, _, seq, width = latents.shape
    share = w_qkv.shape[1]
    chunk = width // QUART
    cols = 3 * chunk
    rows = PAIR * seq
    nj = BLOCKS // 2
    levels = mod_table.shape[1]

    def swap(value, axis):
        return lax.ppermute(value, axis, [(0, 1), (1, 0)])

    quarters = w_qkv[0].reshape(share, 3, QUART, chunk)
    quarters = quarters.transpose(2, 0, 1, 3).reshape(QUART, share, cols)
    mine = lax.all_to_all(quarters, "y", 0, 0)
    if halves == 2:
        other = swap(mine, "xh")
        both = jnp.stack(
            [jnp.where(half == 0, mine, other), jnp.where(half == 0, other, mine)], axis=1
        )
    else:
        both = mine[:, None]
    pieces = []
    for j in range(nj):
        own = lax.all_gather(both[j], "z", axis=0)
        pieces.append((own, swap(own, "c")))

    onehot = (timesteps[:, 0][:, None] == jnp.arange(levels, dtype=jnp.int32)[None, :]).astype(F32)
    table, _ = lax.optimization_barrier((mod_table, mine))
    modulations = jnp.dot(
        onehot, table[0].reshape(levels, 3 * width), precision=lax.Precision.HIGHEST
    ).reshape(count, 3, width)
    mods = lax.all_gather(modulations, "y", axis=0)
    gates = lax.dynamic_slice_in_dim(mods[:, :, 2:3, :], y * chunk, chunk, axis=3)
    scal = jnp.concatenate(
        [jnp.stack([y, core, p]).astype(jnp.int32), text_len[:, 0].astype(jnp.int32)]
    )
    entering = latents.reshape(count // PAIR, rows, width)
    leaving = lax.dynamic_slice_in_dim(
        out_grad.reshape(count // PAIR, rows, width), y * chunk, chunk, axis=2
    )

    routes = [
        [
            (yy * 2 + pp, ((yy + d) % QUART) * 2 + (1 - pp))
            for yy in range(QUART)
            for pp in range(2)
        ]
        for d in range(QUART)
    ]

    def send(parts):
        return [lax.ppermute(parts[d], ("y", "xl"), routes[d]) for d in range(QUART)]

    wscr = pltpu.VMEM((halves, depth, cores, share, cols), BF16)
    params = pltpu.CompilerParams(vmem_limit_bytes=40 * 1024 * 1024)

    def held(k):
        first, second = min(k // 2, nj - 1), max((k - 1) // 2, 0)
        if first == second:
            return pieces[first]
        return pieces[first] + pieces[second]

    def shape(cols, kind):
        return jax.ShapeDtypeStruct((rows, cols), kind)

    steps = BLOCKS + 1
    saved = []
    received = None
    for k in range(steps):
        if k == 0:
            ins = [entering[0]]
        elif k == 1:
            ins = [entering[1]] + received
        else:
            ins = received
        weights = held(k)
        sending = k < steps - 1
        outs = [shape(width, BF16), shape(width, BF16), shape(cols, F32)]
        if sending:
            outs = [shape(chunk, BF16)] + outs
        result = pl.pallas_call(
            functools.partial(forward_kernel, k, len(ins), len(weights), sending),
            out_shape=outs,
            in_specs=[SM] + [VM] * (len(ins) + 2) + [ANY] * len(weights),
            out_specs=[VM] * len(outs),
            scratch_shapes=[wscr, pltpu.VMEM((QUART, rows, chunk), BF16), pltpu.SemaphoreType.DMA],
            compiler_params=params,
            name="forward_step",
        )(scal, *ins, mods, gates, *weights)
        if sending:
            received = send([result[0]] * QUART)
            result = result[1:]
        saved.append(result)

    lows = [None] * steps
    sums = [None] * nj
    received = None
    for k in reversed(range(steps)):
        if k == steps - 1:
            ins = [leaving[1]]
        elif k == steps - 2:
            ins = [leaving[0]] + received
        else:
            ins = received
        weights = held(k)
        sending = k > 0
        outs = [shape(chunk, BF16)] * (QUART * sending) + [shape(cols, BF16)]
        hidden, _, projected = saved[k]
        result = pl.pallas_call(
            functools.partial(backward_kernel, k, len(ins), len(weights), sending),
            out_shape=outs,
            in_specs=[SM] + [VM] * (len(ins) + 4) + [ANY] * len(weights),
            out_specs=[VM] * len(outs),
            scratch_shapes=[
                wscr,
                pltpu.VMEM((rows, chunk), F32),
                pltpu.VMEM((rows, cols), F32),
                pltpu.VMEM((QUART, rows, chunk), F32),
                pltpu.SemaphoreType.DMA,
            ],
            compiler_params=params,
            name="backward_step",
        )(scal, *ins, mods, gates, hidden, projected, *weights)
        lows[k] = result[-1]
        if sending:
            received = send(result[:-1])
        if k % 2 == 0 and k < steps - 1:
            j = k // 2
            partial = pl.pallas_call(
                weight_grad_kernel,
                out_shape=jax.ShapeDtypeStruct((cores, depth, halves, share, cols), BF16),
                in_specs=[SM] + [ANY] * 6,
                out_specs=VM,
                scratch_shapes=[
                    pltpu.VMEM((2 * rows, width), BF16),
                    pltpu.VMEM((2 * rows, cols), BF16),
                    pltpu.SemaphoreType.DMA((4,)),
                ],
                compiler_params=params,
                cost_estimate=pl.CostEstimate(
                    flops=4 * rows * width * cols,
                    bytes_accessed=4 * width * cols,
                    transcendentals=0,
                ),
                name="weight_grad",
            )(scal, *[saved[k + i][1] for i in range(3)], *[lows[k + i] for i in range(3)])
            chip = partial[0] + swap(partial[1], "c")
            ring = lax.psum_scatter(chip, "z", scatter_dimension=0)
            if halves == 2:
                there = lax.dynamic_index_in_dim(ring, 1 - half, 0, keepdims=False)
                here = lax.dynamic_index_in_dim(ring, half, 0, keepdims=False)
                sums[j] = (here.astype(F32) + swap(there, "xh").astype(F32)).astype(BF16)
            else:
                sums[j] = ring[0]
    grads = lax.all_to_all(jnp.stack(sums), "y", 0, 0)
    grads = grads.reshape(QUART, share, 3, chunk).transpose(1, 2, 0, 3)
    return grads.reshape(1, share, 3 * width).astype(F32)


def solution(mesh):
    fine = Mesh(mesh.devices.reshape(4, 2, 2, 8, 2), ("y", "xl", "xh", "z", "c"))
    pipe = ("y", "xl")
    dp = ("xh", "z", "c")
    return jax.shard_map(
        shards,
        mesh=fine,
        in_specs=(
            P(None, dp, None, None),
            P(None, dp, None, None),
            P(pipe, dp, None),
            P(pipe, None, None, None),
            P(None, dp),
            P(None, dp),
        ),
        out_specs=P(pipe, dp, None),
        check_vma=False,
    )
```

```python
import functools
import math

import jax
import jax.numpy as jnp
from jax import lax
from jax.experimental import pallas as pl
from jax.experimental.pallas import tpu as pltpu
from jax.sharding import Mesh
from jax.sharding import PartitionSpec as P

IMG = 40
EPS = 1e-06
HDIM = 128
BLOCKS = 8
QUART = 4
PAIR = 2
F32 = jnp.float32
BF16 = jnp.bfloat16
VMEM_LIMIT = 16 * 1024 * 1024
VM = pl.BlockSpec(memory_space=pltpu.VMEM)
SM = pl.BlockSpec(memory_space=pltpu.SMEM)
ANY = pl.BlockSpec(memory_space=pl.ANY)


def place(scal, k):
    p = scal[2]
    j = lax.max((k - p + 2) // 2 - 1, 0)
    j = lax.min(j, BLOCKS // 2 - 1)
    return lax.rem(k + p, 2), j, lax.rem(scal[0] + QUART - j, QUART)


def fetch_weights(scal, j, pieces, wscr, sem):
    c = scal[1]
    halves = wscr.shape[0]
    inner = lax.rem(j, 2)

    def start(own, other):
        for t in range(halves):
            where = lax.rem(t + scal[3], halves)
            pltpu.make_async_copy(own.at[:, inner, t], wscr.at[where, :, c], sem).start()
            pltpu.make_async_copy(other.at[:, inner, t], wscr.at[where, :, 1 - c], sem).start()

    if len(pieces) == 2:
        start(*pieces)
    else:

        @pl.when(scal[2] == 0)
        def _():
            start(*pieces[:2])

        @pl.when(scal[2] != 0)
        def _():
            start(*pieces[2:])


def await_weights(wscr, sem):
    pltpu.make_async_copy(wscr, wscr, sem).wait()


def half_weights(wscr, t):
    value = wscr[t]
    return value.reshape(value.shape[0] * value.shape[1] * value.shape[2], value.shape[3])


def standardize(hidden):
    average = jnp.mean(hidden, axis=-1, keepdims=True)
    centered = hidden - average
    variance = jnp.mean(centered * centered, axis=-1, keepdims=True)
    scale = lax.rsqrt(variance + EPS)
    return centered * scale, scale


def nt(a, b):
    return lax.dot_general(
        a.astype(BF16), b.astype(BF16), (((1,), (1,)), ((), ())), preferred_element_type=F32
    )


def nn(a, b):
    return lax.dot_general(
        a.astype(BF16), b.astype(BF16), (((1,), (0,)), ((), ())), preferred_element_type=F32
    )


def tn(a, b):
    return lax.dot_general(
        a.astype(BF16), b.astype(BF16), (((0,), (0,)), ((), ())), preferred_element_type=F32
    )


def unit(rows):
    scale = lax.rsqrt(jnp.mean(rows * rows, axis=-1, keepdims=True) + EPS)
    return rows * scale, scale


def weights_of(q, k, length):
    scores = nt(q, k) * (1.0 / math.sqrt(HDIM))
    position = lax.broadcasted_iota(jnp.int32, scores.shape, 1)
    usable = (position < IMG) | (position - IMG < length)
    weights = jnp.where(usable, jnp.exp(scores), 0.0)
    return weights / jnp.sum(weights, axis=-1, keepdims=True)


def load_hidden(scal, ins, hs):
    y = scal[0]
    chunk = hs.shape[2]

    def from_whole(ref):
        for t in range(QUART):
            hs[t] = ref[:, t * chunk : (t + 1) * chunk]

    def from_chunks(parts):
        for d in range(QUART):
            hs[lax.rem(y + QUART - d, QUART)] = parts[d][...]

    if len(ins) == 1:
        from_whole(ins[0])
    elif len(ins) == QUART:
        from_chunks(ins)
    else:

        @pl.when(scal[2] == 0)
        def _():
            from_whole(ins[0])

        @pl.when(scal[2] != 0)
        def _():
            from_chunks(ins[1:])

    return jnp.concatenate([hs[t].astype(F32) for t in range(QUART)], axis=1)


def forward_kernel(k, n_in, n_w, send, scal, *refs):
    ins, refs = refs[:n_in], refs[n_in:]
    mods, gates = refs[:2]
    pieces, refs = refs[2 : 2 + n_w], refs[2 + n_w :]
    if send:
        out_ref, refs = refs[0], refs[1:]
    normed_ref, proj_ref, wscr, hs, sem = refs
    y = scal[0]
    micro, j, slot = place(scal, k)
    fetch_weights(scal, j, pieces, wscr, sem)
    chunk = hs.shape[2]
    rows, width = normed_ref.shape
    seq = rows // PAIR
    normal, _ = standardize(load_hidden(scal, ins, hs))
    normal = normal.reshape(PAIR, seq, width)
    normed = jnp.concatenate(
        [
            (1.0 + mods[slot, PAIR * micro + s, 1:2, :]) * normal[s]
            + mods[slot, PAIR * micro + s, 0:1, :]
            for s in range(PAIR)
        ],
        axis=0,
    ).astype(BF16)
    normed_ref[...] = normed
    await_weights(wscr, sem)
    halves = wscr.shape[0]
    span = width // halves
    projected = nn(normed[:, :span], half_weights(wscr, 0))
    for t in range(1, halves):
        projected += nn(normed[:, t * span : (t + 1) * span], half_weights(wscr, t))
    proj_ref[...] = projected
    if not send:
        return
    own = hs[y].astype(F32)
    for s in range(PAIR):
        length = scal[4 + PAIR * micro + s]
        r = slice(s * seq, (s + 1) * seq)
        mixed = []
        for h in range(chunk // HDIM):
            lo = h * HDIM
            q, _ = unit(proj_ref[r, lo : lo + HDIM])
            key, _ = unit(proj_ref[r, chunk + lo : chunk + lo + HDIM])
            v = proj_ref[r, 2 * chunk + lo : 2 * chunk + lo + HDIM]
            mixed.append(nn(weights_of(q, key, length), v))
        mixture = jnp.concatenate(mixed, axis=1)
        gate = gates[slot, PAIR * micro + s]
        hs_rows = own[r] + gate * mixture
        if s == 0:
            first = hs_rows
    out_ref[...] = jnp.concatenate([first, hs_rows], axis=0).astype(BF16)


def backward_kernel(k, n_in, n_hid, n_w, send, scal, *refs):
    ins, refs = refs[:n_in], refs[n_in:]
    hidden, refs = refs[:n_hid], refs[n_hid:]
    mods, gates, proj_ref = refs[:3]
    pieces, refs = refs[3 : 3 + n_w], refs[3 + n_w :]
    outs, refs = refs[: QUART * send], refs[QUART * send :]
    low_ref, wscr, hs, gs, dp, ds, sem = refs
    y = scal[0]
    micro, j, slot = place(scal, k)
    if send:
        fetch_weights(scal, j, pieces, wscr, sem)
    rows, chunk = gs.shape
    width = chunk * QUART
    seq = rows // PAIR

    def total(parts):
        gs[...] = sum([part[...].astype(F32) for part in parts[1:]], parts[0][...].astype(F32))

    if n_in in (1, QUART):
        total(ins)
    else:

        @pl.when(scal[2] != 0)
        def _():
            total(ins[:1])

        @pl.when(scal[2] == 0)
        def _():
            total(ins[1:])

    root = 1.0 / math.sqrt(HDIM)
    for s in range(PAIR):
        length = scal[4 + PAIR * micro + s]
        r = slice(s * seq, (s + 1) * seq)
        for h in range(chunk // HDIM):
            lo = h * HDIM
            c = slice(lo, lo + HDIM)
            gate = gates[slot, PAIR * micro + s, :, c]
            dmix = gs[r, c] * gate
            q, rq = unit(proj_ref[r, lo : lo + HDIM])
            key, rk = unit(proj_ref[r, chunk + lo : chunk + lo + HDIM])
            v = proj_ref[r, 2 * chunk + lo : 2 * chunk + lo + HDIM]
            att = weights_of(q, key, length)
            datt = nt(dmix, v)
            dscore = att * (datt - jnp.sum(att * datt, axis=-1, keepdims=True)) * root
            dqn = nn(dscore, key)
            dkn = tn(dscore, q)
            dp[r, c] = rq * (dqn - q * jnp.mean(dqn * q, axis=-1, keepdims=True))
            dp[r, chunk + lo : chunk + lo + HDIM] = rk * (
                dkn - key * jnp.mean(dkn * key, axis=-1, keepdims=True)
            )
            dp[r, 2 * chunk + lo : 2 * chunk + lo + HDIM] = tn(att, dmix)
    low = dp[...].astype(BF16)
    low_ref[...] = low
    if not send:
        return
    normal, scale = standardize(load_hidden(scal, hidden, hs))
    await_weights(wscr, sem)
    halves = wscr.shape[0]
    norm_grad = jnp.concatenate([nt(low, half_weights(wscr, t)) for t in range(halves)], axis=1)
    norm_grad = norm_grad.reshape(PAIR, seq, width)
    grad = jnp.concatenate(
        [(1.0 + mods[slot, PAIR * micro + s, 1:2, :]) * norm_grad[s] for s in range(PAIR)], axis=0
    )
    back = scale * (
        grad
        - jnp.mean(grad, axis=-1, keepdims=True)
        - normal * jnp.mean(grad * normal, axis=-1, keepdims=True)
    )
    for t in range(QUART):
        ds[t] = back[:, t * chunk : (t + 1) * chunk]
    ds[y] = ds[y] + gs[...]
    for d in range(QUART):
        outs[d][...] = ds[lax.rem(y + d, QUART)].astype(BF16)


def weight_grad_kernel(scal, n0, n1, n2, g0, g1, g2, out, nscr, gscr, sems):
    c = scal[1]
    rows = n0.shape[0]

    def start(normed, grad):
        pltpu.make_async_copy(normed, nscr.at[0:rows], sems.at[0]).start()
        pltpu.make_async_copy(grad, gscr.at[0:rows], sems.at[1]).start()

    pltpu.make_async_copy(n1, nscr.at[rows : 2 * rows], sems.at[2]).start()
    pltpu.make_async_copy(g1, gscr.at[rows : 2 * rows], sems.at[3]).start()

    @pl.when(scal[2] == 0)
    def _():
        start(n0, g0)

    @pl.when(scal[2] != 0)
    def _():
        start(n2, g2)

    pltpu.make_async_copy(n0, nscr.at[0:rows], sems.at[0]).wait()
    pltpu.make_async_copy(g0, gscr.at[0:rows], sems.at[1]).wait()
    pltpu.make_async_copy(n1, nscr.at[rows : 2 * rows], sems.at[2]).wait()
    pltpu.make_async_copy(g1, gscr.at[rows : 2 * rows], sems.at[3]).wait()
    cores, depth, halves, share, _ = out.shape
    width = nscr.shape[1]
    per = 384
    groups = per // share
    right = gscr[...]
    for t in range(width // per):
        value = tn(nscr[:, t * per : (t + 1) * per], right).astype(BF16)
        for u in range(groups):
            at = t * groups + u
            core = at % cores
            half, z = divmod(at // cores, depth)
            where = lax.rem(core + c, cores)
            out[where, z, half] = value[u * share : (u + 1) * share]


def shards(latents, out_grad, w_qkv, mod_table, timesteps, text_len):
    y = lax.axis_index("y")
    p = lax.axis_index("xl")
    half = lax.axis_index("xh")
    core = lax.axis_index("c")
    halves = lax.axis_size("xh")
    depth = lax.axis_size("z")
    cores = lax.axis_size("c")
    count, _, seq, width = latents.shape
    share = w_qkv.shape[1]
    chunk = width // QUART
    cols = 3 * chunk
    rows = PAIR * seq
    nj = BLOCKS // 2
    levels = mod_table.shape[1]

    def swap(value, axis):
        return lax.ppermute(value, axis, [(0, 1), (1, 0)])

    turns = [
        [
            [
                (yy * halves + hh, ((yy + dy) % QUART) * halves + (hh + dx) % halves)
                for yy in range(QUART)
                for hh in range(halves)
            ]
            for dy in range(QUART)
        ]
        for dx in range(halves)
    ]

    def turn(value, dx, dy):
        if dx == 0 and dy == 0:
            return value
        return lax.ppermute(value, ("y", "xh"), turns[dx][dy])

    def pick(stack, index):
        return lax.dynamic_index_in_dim(stack, index, 0, keepdims=False)

    quarters = w_qkv[0].reshape(share, 3, QUART, chunk)
    quarters = quarters.transpose(2, 0, 1, 3).reshape(QUART, share, cols)
    leaves = [pick(quarters, lax.rem(y + dy, QUART)) for dy in range(QUART)]
    arrived = [
        jnp.stack([turn(leaves[dy], dx, dy) for dy in range(QUART)]) for dx in range(halves)
    ]
    pieces = []
    for g in range(nj // 2):
        part = jnp.stack(
            [
                jnp.stack(
                    [pick(arrived[dx], lax.rem(y + QUART - j, QUART)) for dx in range(halves)]
                )
                for j in (2 * g, 2 * g + 1)
            ]
        )
        own = lax.all_gather(part, "z", axis=0)
        pieces.append((own, swap(own, "c")))

    onehot = (timesteps[:, 0][:, None] == jnp.arange(levels, dtype=jnp.int32)[None, :]).astype(F32)
    table, _ = lax.optimization_barrier((mod_table, arrived[0]))
    modulations = jnp.dot(
        onehot, table[0].reshape(levels, 3 * width), precision=lax.Precision.HIGHEST
    ).reshape(count, 3, width)
    mods = jnp.stack(
        [modulations]
        + [
            lax.ppermute(modulations, "y", [(yy, (yy + dy) % QUART) for yy in range(QUART)])
            for dy in range(1, QUART)
        ]
    )
    gates = lax.dynamic_slice_in_dim(mods[:, :, 2:3, :], y * chunk, chunk, axis=3)
    scal = jnp.concatenate(
        [jnp.stack([y, core, p, half]).astype(jnp.int32), text_len[:, 0].astype(jnp.int32)]
    )
    entering = latents.reshape(count // PAIR, rows, width)
    leaving = lax.dynamic_slice_in_dim(
        out_grad.reshape(count // PAIR, rows, width), y * chunk, chunk, axis=2
    )

    routes = [
        [
            (yy * 2 + pp, ((yy + d) % QUART) * 2 + (1 - pp))
            for yy in range(QUART)
            for pp in range(2)
        ]
        for d in range(QUART)
    ]

    def send(parts):
        return [lax.ppermute(parts[d], ("y", "xl"), routes[d]) for d in range(QUART)]

    wscr = pltpu.VMEM((halves, depth, cores, share, cols), BF16)
    params = pltpu.CompilerParams(vmem_limit_bytes=VMEM_LIMIT)

    def held(k):
        first, second = min(k // 2, nj - 1), max((k - 1) // 2, 0)
        first, second = first // 2, second // 2
        if first == second:
            return pieces[first]
        return pieces[first] + pieces[second]

    def shape(cols, kind):
        return jax.ShapeDtypeStruct((rows, cols), kind)

    steps = BLOCKS + 1
    saved = []
    received = None
    for k in range(steps):
        if k == 0:
            ins = [entering[0]]
        elif k == 1:
            ins = [entering[1]] + received
        else:
            ins = received
        weights = held(k)
        sending = k < steps - 1
        outs = [shape(width, BF16), shape(cols, F32)]
        if sending:
            outs = [shape(chunk, BF16)] + outs
        result = pl.pallas_call(
            functools.partial(forward_kernel, k, len(ins), len(weights), sending),
            out_shape=outs,
            in_specs=[SM] + [VM] * (len(ins) + 2) + [ANY] * len(weights),
            out_specs=[VM] * len(outs),
            scratch_shapes=[wscr, pltpu.VMEM((QUART, rows, chunk), BF16), pltpu.SemaphoreType.DMA],
            compiler_params=params,
            name="forward_step",
        )(scal, *ins, mods, gates, *weights)
        if sending:
            received = send([result[0]] * QUART)
            result = result[1:]
        saved.append((ins, *result))

    lows = [None] * steps
    sums = [None] * nj
    received = None
    for k in reversed(range(steps)):
        if k == steps - 1:
            ins = [leaving[1]]
        elif k == steps - 2:
            ins = [leaving[0]] + received
        else:
            ins = received
        weights = held(k)
        sending = k > 0
        outs = [shape(chunk, BF16)] * (QUART * sending) + [shape(cols, BF16)]
        hidden, _, projected = saved[k]
        sources = len(ins) + len(hidden) + 3
        result = pl.pallas_call(
            functools.partial(
                backward_kernel, k, len(ins), len(hidden), len(weights), sending
            ),
            out_shape=outs,
            in_specs=[SM] + [VM] * sources + [ANY] * len(weights),
            out_specs=[VM] * len(outs),
            scratch_shapes=[
                wscr,
                pltpu.VMEM((QUART, rows, chunk), BF16),
                pltpu.VMEM((rows, chunk), F32),
                pltpu.VMEM((rows, cols), F32),
                pltpu.VMEM((QUART, rows, chunk), F32),
                pltpu.SemaphoreType.DMA,
            ],
            compiler_params=params,
            name="backward_step",
        )(scal, *ins, *hidden, mods, gates, projected, *weights)
        lows[k] = result[-1]
        if sending:
            received = send(result[:-1])
        if k % 2 == 0 and k < steps - 1:
            j = k // 2
            factors = [saved[k + i][1] for i in range(3)] + [lows[k + i] for i in range(3)]
            if sending:
                factors, received[0] = lax.optimization_barrier((factors, received[0]))
            partial = pl.pallas_call(
                weight_grad_kernel,
                out_shape=jax.ShapeDtypeStruct((cores, depth, halves, share, cols), BF16),
                in_specs=[SM] + [ANY] * 6,
                out_specs=VM,
                scratch_shapes=[
                    pltpu.VMEM((2 * rows, width), BF16),
                    pltpu.VMEM((2 * rows, cols), BF16),
                    pltpu.SemaphoreType.DMA((4,)),
                ],
                compiler_params=params,
                cost_estimate=pl.CostEstimate(
                    flops=4 * rows * width * cols,
                    bytes_accessed=4 * width * cols,
                    transcendentals=0,
                ),
                name="weight_grad",
            )(scal, *factors)
            chip = partial[0] + swap(partial[1], "c")
            sums[j] = lax.psum_scatter(chip, "z", scatter_dimension=0)
    sums = jnp.stack(sums)
    finals = []
    for dy in range(QUART):
        block = pick(sums, lax.rem(y + dy, QUART))
        here = [turn(pick(block, lax.rem(half + dx, halves)), dx, dy) for dx in range(halves)]
        finals.append(sum([part.astype(F32) for part in here]).reshape(share, 3, chunk))
    finals = jnp.stack(finals)
    grads = jnp.stack([pick(finals, lax.rem(y + QUART - q, QUART)) for q in range(QUART)], axis=2)
    return grads.reshape(1, share, 3 * width)


def solution(mesh):
    fine = Mesh(mesh.devices.reshape(4, 2, 2, 8, 2), ("y", "xl", "xh", "z", "c"))
    pipe = ("y", "xl")
    dp = ("xh", "z", "c")
    return jax.shard_map(
        shards,
        mesh=fine,
        in_specs=(
            P(None, dp, None, None),
            P(None, dp, None, None),
            P(pipe, dp, None),
            P(pipe, None, None, None),
            P(None, dp),
            P(None, dp),
        ),
        out_specs=P(pipe, dp, None),
        check_vma=False,
    )
```

```python
import functools
import math

import jax
import jax.numpy as jnp
from jax import lax
from jax.experimental import pallas as pl
from jax.experimental.pallas import tpu as pltpu
from jax.sharding import Mesh
from jax.sharding import PartitionSpec as P

IMG = 40
EPS = 1e-06
HDIM = 128
BLOCKS = 8
QUART = 4
PAIR = 2
F32 = jnp.float32
BF16 = jnp.bfloat16
VMEM_LIMIT = 16 * 1024 * 1024
VM = pl.BlockSpec(memory_space=pltpu.VMEM)
SM = pl.BlockSpec(memory_space=pltpu.SMEM)
ANY = pl.BlockSpec(memory_space=pl.ANY)


def place(scal, k):
    p = scal[2]
    j = lax.max((k - p + 2) // 2 - 1, 0)
    j = lax.min(j, BLOCKS // 2 - 1)
    return lax.rem(k + p, 2), j, lax.rem(scal[0] + QUART - j, QUART)


def fetch_weights(scal, j, pieces, wscr, sem):
    c = scal[1]
    halves = wscr.shape[0]
    inner = lax.rem(j, 2)

    def start(own, other):
        for t in range(halves):
            pltpu.make_async_copy(own.at[:, inner, t], wscr.at[t, :, c], sem).start()
            pltpu.make_async_copy(other.at[:, inner, t], wscr.at[t, :, 1 - c], sem).start()

    if len(pieces) == 2:
        start(*pieces)
    else:

        @pl.when(scal[2] == 0)
        def _():
            start(*pieces[:2])

        @pl.when(scal[2] != 0)
        def _():
            start(*pieces[2:])


def await_weights(wscr, sem):
    pltpu.make_async_copy(wscr, wscr, sem).wait()


def half_weights(wscr, t):
    value = wscr[t]
    return value.reshape(value.shape[0] * value.shape[1] * value.shape[2], value.shape[3])


def standardize(hidden):
    average = jnp.mean(hidden, axis=-1, keepdims=True)
    centered = hidden - average
    variance = jnp.mean(centered * centered, axis=-1, keepdims=True)
    scale = lax.rsqrt(variance + EPS)
    return centered * scale, scale


def nt(a, b):
    return lax.dot_general(
        a.astype(BF16), b.astype(BF16), (((1,), (1,)), ((), ())), preferred_element_type=F32
    )


def nn(a, b):
    return lax.dot_general(
        a.astype(BF16), b.astype(BF16), (((1,), (0,)), ((), ())), preferred_element_type=F32
    )


def tn(a, b):
    return lax.dot_general(
        a.astype(BF16), b.astype(BF16), (((0,), (0,)), ((), ())), preferred_element_type=F32
    )


def unit(rows):
    scale = lax.rsqrt(jnp.mean(rows * rows, axis=-1, keepdims=True) + EPS)
    return rows * scale, scale


def weights_of(q, k, length):
    scores = nt(q, k) * (1.0 / math.sqrt(HDIM))
    position = lax.broadcasted_iota(jnp.int32, scores.shape, 1)
    usable = (position < IMG) | (position - IMG < length)
    weights = jnp.where(usable, jnp.exp(scores), 0.0)
    return weights / jnp.sum(weights, axis=-1, keepdims=True)


def load_hidden(scal, ins, hs):
    y = scal[0]
    chunk = hs.shape[2]

    def from_whole(ref):
        for t in range(QUART):
            hs[t] = ref[:, t * chunk : (t + 1) * chunk]

    def from_chunks(parts):
        for d in range(QUART):
            hs[lax.rem(y + QUART - d, QUART)] = parts[d][...]

    if len(ins) == 1:
        from_whole(ins[0])
    elif len(ins) == QUART:
        from_chunks(ins)
    else:

        @pl.when(scal[2] == 0)
        def _():
            from_whole(ins[0])

        @pl.when(scal[2] != 0)
        def _():
            from_chunks(ins[1:])

    return jnp.concatenate([hs[t].astype(F32) for t in range(QUART)], axis=1)


def forward_kernel(k, n_in, n_w, send, scal, *refs):
    ins, refs = refs[:n_in], refs[n_in:]
    mods, gates = refs[:2]
    pieces, refs = refs[2 : 2 + n_w], refs[2 + n_w :]
    if send:
        out_ref, refs = refs[0], refs[1:]
    normed_out, proj_out, normed_ref, proj_ref, wscr, hs, sem, sems = refs
    normed_save = pltpu.make_async_copy(normed_ref, normed_out, sems.at[0])
    proj_save = pltpu.make_async_copy(proj_ref, proj_out, sems.at[1])
    y = scal[0]
    micro, j, slot = place(scal, k)
    fetch_weights(scal, j, pieces, wscr, sem)
    chunk = hs.shape[2]
    rows, width = normed_ref.shape
    seq = rows // PAIR
    normal, _ = standardize(load_hidden(scal, ins, hs))
    normal = normal.reshape(PAIR, seq, width)
    normed = jnp.concatenate(
        [
            (1.0 + mods[slot, PAIR * micro + s, 1:2, :]) * normal[s]
            + mods[slot, PAIR * micro + s, 0:1, :]
            for s in range(PAIR)
        ],
        axis=0,
    ).astype(BF16)
    normed_ref[...] = normed
    normed_save.start()
    await_weights(wscr, sem)
    halves = wscr.shape[0]
    span = width // halves
    projected = nn(normed[:, :span], half_weights(wscr, 0))
    for t in range(1, halves):
        projected += nn(normed[:, t * span : (t + 1) * span], half_weights(wscr, t))
    proj_ref[...] = projected
    proj_save.start()
    if not send:
        normed_save.wait()
        proj_save.wait()
        return
    own = hs[y].astype(F32)
    for s in range(PAIR):
        length = scal[3 + PAIR * micro + s]
        r = slice(s * seq, (s + 1) * seq)
        mixed = []
        for h in range(chunk // HDIM):
            lo = h * HDIM
            q, _ = unit(proj_ref[r, lo : lo + HDIM])
            key, _ = unit(proj_ref[r, chunk + lo : chunk + lo + HDIM])
            v = proj_ref[r, 2 * chunk + lo : 2 * chunk + lo + HDIM]
            mixed.append(nn(weights_of(q, key, length), v))
        mixture = jnp.concatenate(mixed, axis=1)
        gate = gates[slot, PAIR * micro + s]
        hs_rows = own[r] + gate * mixture
        if s == 0:
            first = hs_rows
    out_ref[...] = jnp.concatenate([first, hs_rows], axis=0).astype(BF16)
    normed_save.wait()
    proj_save.wait()


def backward_kernel(k, n_in, n_hid, n_w, send, scal, *refs):
    ins, refs = refs[:n_in], refs[n_in:]
    hidden, refs = refs[:n_hid], refs[n_hid:]
    mods, gates, proj_ref = refs[:3]
    pieces, refs = refs[3 : 3 + n_w], refs[3 + n_w :]
    outs, refs = refs[: QUART * send], refs[QUART * send :]
    low_out, low_ref, wscr, hs, gs, dp, ds, sem, low_sem = refs
    low_save = pltpu.make_async_copy(low_ref, low_out, low_sem)
    y = scal[0]
    micro, j, slot = place(scal, k)
    if send:
        fetch_weights(scal, j, pieces, wscr, sem)
    rows, chunk = gs.shape
    width = chunk * QUART
    seq = rows // PAIR

    def total(parts):
        gs[...] = sum([part[...].astype(F32) for part in parts[1:]], parts[0][...].astype(F32))

    if n_in in (1, QUART):
        total(ins)
    else:

        @pl.when(scal[2] != 0)
        def _():
            total(ins[:1])

        @pl.when(scal[2] == 0)
        def _():
            total(ins[1:])

    root = 1.0 / math.sqrt(HDIM)
    for s in range(PAIR):
        length = scal[3 + PAIR * micro + s]
        r = slice(s * seq, (s + 1) * seq)
        for h in range(chunk // HDIM):
            lo = h * HDIM
            c = slice(lo, lo + HDIM)
            gate = gates[slot, PAIR * micro + s, :, c]
            dmix = gs[r, c] * gate
            q, rq = unit(proj_ref[r, lo : lo + HDIM])
            key, rk = unit(proj_ref[r, chunk + lo : chunk + lo + HDIM])
            v = proj_ref[r, 2 * chunk + lo : 2 * chunk + lo + HDIM]
            att = weights_of(q, key, length)
            datt = nt(dmix, v)
            dscore = att * (datt - jnp.sum(att * datt, axis=-1, keepdims=True)) * root
            dqn = nn(dscore, key)
            dkn = tn(dscore, q)
            dp[r, c] = rq * (dqn - q * jnp.mean(dqn * q, axis=-1, keepdims=True))
            dp[r, chunk + lo : chunk + lo + HDIM] = rk * (
                dkn - key * jnp.mean(dkn * key, axis=-1, keepdims=True)
            )
            dp[r, 2 * chunk + lo : 2 * chunk + lo + HDIM] = tn(att, dmix)
    low = dp[...].astype(BF16)
    low_ref[...] = low
    low_save.start()
    if not send:
        low_save.wait()
        return
    normal, scale = standardize(load_hidden(scal, hidden, hs))
    await_weights(wscr, sem)
    halves = wscr.shape[0]
    norm_grad = jnp.concatenate([nt(low, half_weights(wscr, t)) for t in range(halves)], axis=1)
    norm_grad = norm_grad.reshape(PAIR, seq, width)
    grad = jnp.concatenate(
        [(1.0 + mods[slot, PAIR * micro + s, 1:2, :]) * norm_grad[s] for s in range(PAIR)], axis=0
    )
    back = scale * (
        grad
        - jnp.mean(grad, axis=-1, keepdims=True)
        - normal * jnp.mean(grad * normal, axis=-1, keepdims=True)
    )
    for t in range(QUART):
        ds[t] = back[:, t * chunk : (t + 1) * chunk]
    ds[y] = ds[y] + gs[...]
    for d in range(QUART):
        outs[d][...] = ds[lax.rem(y + d, QUART)].astype(BF16)
    low_save.wait()


def weight_grad_kernel(scal, n0, n1, n2, g0, g1, g2, out, nscr, gscr, sems):
    c = scal[1]
    rows = n0.shape[0]

    def start(normed, grad):
        pltpu.make_async_copy(normed, nscr.at[0:rows], sems.at[0]).start()
        pltpu.make_async_copy(grad, gscr.at[0:rows], sems.at[1]).start()

    pltpu.make_async_copy(n1, nscr.at[rows : 2 * rows], sems.at[2]).start()
    pltpu.make_async_copy(g1, gscr.at[rows : 2 * rows], sems.at[3]).start()

    @pl.when(scal[2] == 0)
    def _():
        start(n0, g0)

    @pl.when(scal[2] != 0)
    def _():
        start(n2, g2)

    pltpu.make_async_copy(n0, nscr.at[0:rows], sems.at[0]).wait()
    pltpu.make_async_copy(g0, gscr.at[0:rows], sems.at[1]).wait()
    pltpu.make_async_copy(n1, nscr.at[rows : 2 * rows], sems.at[2]).wait()
    pltpu.make_async_copy(g1, gscr.at[rows : 2 * rows], sems.at[3]).wait()
    cores, depth, halves, share, _ = out.shape
    width = nscr.shape[1]
    per = 384
    groups = per // share
    right = gscr[...]
    for t in range(width // per):
        value = tn(nscr[:, t * per : (t + 1) * per], right).astype(BF16)
        for u in range(groups):
            at = t * groups + u
            core = at % cores
            half, z = divmod(at // cores, depth)
            where = lax.rem(core + c, cores)
            out[where, z, half] = value[u * share : (u + 1) * share]


def shards(latents, out_grad, w_qkv, mod_table, timesteps, text_len):
    y = lax.axis_index("y")
    p = lax.axis_index("xl")
    core = lax.axis_index("c")
    halves = lax.axis_size("xh")
    depth = lax.axis_size("z")
    cores = lax.axis_size("c")
    count, _, seq, width = latents.shape
    share = w_qkv.shape[1]
    chunk = width // QUART
    cols = 3 * chunk
    rows = PAIR * seq
    nj = BLOCKS // 2
    levels = mod_table.shape[1]

    def swap(value, axis):
        return lax.ppermute(value, axis, [(0, 1), (1, 0)])

    quarters = w_qkv[0].reshape(share, 3, QUART, chunk).transpose(2, 0, 1, 3)
    quarters = quarters.reshape(QUART, 1, share, cols)
    quarters = jnp.broadcast_to(quarters, (QUART, halves, share, cols))
    quarters = quarters.reshape(QUART * halves, share, cols)
    both = lax.all_to_all(quarters, ("y", "xh"), 0, 0).reshape(nj, halves, share, cols)
    gathered = [lax.all_gather(both[2 * g : 2 * g + 2], "z", axis=0) for g in range(nj // 2)]

    onehot = (timesteps[:, 0][:, None] == jnp.arange(levels, dtype=jnp.int32)[None, :]).astype(F32)
    table, _ = lax.optimization_barrier((mod_table, both))
    modulations = jnp.dot(
        onehot, table[0].reshape(levels, 3 * width), precision=lax.Precision.HIGHEST
    ).reshape(count, 3, width)
    mods = jnp.stack(
        [modulations]
        + [
            lax.ppermute(modulations, "y", [(yy, (yy + dy) % QUART) for yy in range(QUART)])
            for dy in range(1, QUART)
        ]
    )
    first, mods = lax.optimization_barrier((gathered[0], mods))
    pieces = [(first, swap(first, "c"))]
    gates = lax.dynamic_slice_in_dim(mods[:, :, 2:3, :], y * chunk, chunk, axis=3)
    scal = jnp.concatenate(
        [jnp.stack([y, core, p]).astype(jnp.int32), text_len[:, 0].astype(jnp.int32)]
    )
    entering = latents.reshape(count // PAIR, rows, width)
    leaving = lax.dynamic_slice_in_dim(
        out_grad.reshape(count // PAIR, rows, width), y * chunk, chunk, axis=2
    )

    routes = [
        [
            (yy * 2 + pp, ((yy + d) % QUART) * 2 + (1 - pp))
            for yy in range(QUART)
            for pp in range(2)
        ]
        for d in range(QUART)
    ]

    def send(parts):
        return [lax.ppermute(parts[d], ("y", "xl"), routes[d]) for d in range(QUART)]

    wscr = pltpu.VMEM((halves, depth, cores, share, cols), BF16)
    params = pltpu.CompilerParams(vmem_limit_bytes=VMEM_LIMIT)

    def held(k):
        first, second = min(k // 2, nj - 1), max((k - 1) // 2, 0)
        first, second = first // 2, second // 2
        if first == second:
            return pieces[first]
        return pieces[first] + pieces[second]

    def shape(cols, kind):
        return jax.ShapeDtypeStruct((rows, cols), kind)

    steps = BLOCKS + 1
    saved = []
    received = None
    for k in range(steps):
        if k == 0:
            ins = [entering[0]]
        elif k == 1:
            ins = [entering[1]] + received
        else:
            ins = received
        weights = held(k)
        sending = k < steps - 1
        outs = [shape(width, BF16), shape(cols, F32)]
        if sending:
            outs = [shape(chunk, BF16)] + outs
        result = pl.pallas_call(
            functools.partial(forward_kernel, k, len(ins), len(weights), sending),
            out_shape=outs,
            in_specs=[SM] + [VM] * (len(ins) + 2) + [ANY] * len(weights),
            out_specs=[VM] * sending + [ANY] * 2,
            scratch_shapes=[
                pltpu.VMEM((rows, width), BF16),
                pltpu.VMEM((rows, cols), F32),
                wscr,
                pltpu.VMEM((QUART, rows, chunk), BF16),
                pltpu.SemaphoreType.DMA,
                pltpu.SemaphoreType.DMA((2,)),
            ],
            compiler_params=params,
            name="forward_step",
        )(scal, *ins, mods, gates, *weights)
        if sending:
            received = send([result[0]] * QUART)
            result = result[1:]
        if k == 2:
            second, _ = lax.optimization_barrier((gathered[1], received[0]))
            pieces.append((second, swap(second, "c")))
        saved.append((ins, *result))

    lows = [None] * steps
    chips = [None] * nj
    rings = [None] * (nj // 2)
    received = None
    for k in reversed(range(steps)):
        if k == steps - 1:
            ins = [leaving[1]]
        elif k == steps - 2:
            ins = [leaving[0]] + received
        else:
            ins = received
        weights = held(k)
        sending = k > 0
        outs = [shape(chunk, BF16)] * (QUART * sending) + [shape(cols, BF16)]
        hidden, _, projected = saved[k]
        sources = len(ins) + len(hidden) + 3
        result = pl.pallas_call(
            functools.partial(
                backward_kernel, k, len(ins), len(hidden), len(weights), sending
            ),
            out_shape=outs,
            in_specs=[SM] + [VM] * sources + [ANY] * len(weights),
            out_specs=[VM] * (len(outs) - 1) + [ANY],
            scratch_shapes=[
                pltpu.VMEM((rows, cols), BF16),
                wscr,
                pltpu.VMEM((QUART, rows, chunk), BF16),
                pltpu.VMEM((rows, chunk), F32),
                pltpu.VMEM((rows, cols), F32),
                pltpu.VMEM((QUART, rows, chunk), F32),
                pltpu.SemaphoreType.DMA,
                pltpu.SemaphoreType.DMA,
            ],
            compiler_params=params,
            name="backward_step",
        )(scal, *ins, *hidden, mods, gates, projected, *weights)
        lows[k] = result[-1]
        if sending:
            received = send(result[:-1])
        if k % 2 == 0 and k < steps - 1:
            j = k // 2
            factors = [saved[k + i][1] for i in range(3)] + [lows[k + i] for i in range(3)]
            if sending:
                factors, received[0] = lax.optimization_barrier((factors, received[0]))
            partial = pl.pallas_call(
                weight_grad_kernel,
                out_shape=jax.ShapeDtypeStruct((cores, depth, halves, share, cols), BF16),
                in_specs=[SM] + [ANY] * 6,
                out_specs=VM,
                scratch_shapes=[
                    pltpu.VMEM((2 * rows, width), BF16),
                    pltpu.VMEM((2 * rows, cols), BF16),
                    pltpu.SemaphoreType.DMA((4,)),
                ],
                compiler_params=params,
                cost_estimate=pl.CostEstimate(
                    flops=4 * rows * width * cols,
                    bytes_accessed=4 * width * cols,
                    transcendentals=0,
                ),
                name="weight_grad",
            )(scal, *factors)
            if sending:
                partial, received[1] = lax.optimization_barrier((partial, received[1]))
            chips[j] = (partial[0], swap(partial[1], "c"))
        if k in (0, 3):
            g = k // 3
            total = jnp.stack([chips[2 * g + i][0] + chips[2 * g + i][1] for i in range(2)], axis=1)
            total = total.reshape(depth, 2 * halves * share, cols)
            if sending:
                total, received[1] = lax.optimization_barrier((total, received[1]))
            else:
                total, _ = lax.optimization_barrier((total, rings[1]))
            rings[g] = lax.psum_scatter(total, "z", scatter_dimension=0)
    spread = jnp.stack(rings).reshape(nj * halves, share, cols)
    quarters = lax.all_to_all(spread, ("y", "xh"), 0, 0).reshape(QUART, halves, share, 3, chunk)
    grads = jnp.sum(quarters.astype(F32), axis=1).transpose(1, 2, 0, 3)
    return grads.reshape(1, share, 3 * width)


def solution(mesh):
    fine = Mesh(mesh.devices.reshape(4, 2, 2, 8, 2), ("y", "xl", "xh", "z", "c"))
    pipe = ("y", "xl")
    dp = ("xh", "z", "c")
    return jax.shard_map(
        shards,
        mesh=fine,
        in_specs=(
            P(None, dp, None, None),
            P(None, dp, None, None),
            P(pipe, dp, None),
            P(pipe, None, None, None),
            P(None, dp),
            P(None, dp),
        ),
        out_specs=P(pipe, dp, None),
        check_vma=False,
    )
```

```python
import functools
import math

import jax
import jax.numpy as jnp
from jax import lax
from jax.experimental import pallas as pl
from jax.experimental.pallas import tpu as pltpu
from jax.sharding import Mesh
from jax.sharding import PartitionSpec as P

IMG = 40
EPS = 1e-06
HDIM = 128
BLOCKS = 8
QUART = 4
PAIR = 2
F32 = jnp.float32
BF16 = jnp.bfloat16
VMEM_LIMIT = 16 * 1024 * 1024
VM = pl.BlockSpec(memory_space=pltpu.VMEM)
SM = pl.BlockSpec(memory_space=pltpu.SMEM)
HBM = pl.BlockSpec(memory_space=pltpu.HBM)


def place(scal, k):
    p = scal[2]
    j = lax.max((k - p + 2) // 2 - 1, 0)
    j = lax.min(j, BLOCKS // 2 - 1)
    return lax.rem(k + p, 2), j, lax.rem(scal[0] + QUART - j, QUART)


def fetch_weights(scal, j, pieces, wscr, sem):
    c = scal[1]
    halves = wscr.shape[0]
    inner = lax.rem(j, 2)

    def start(own, other):
        for t in range(halves):
            pltpu.make_async_copy(own.at[:, inner, t], wscr.at[t, :, c], sem).start()
            pltpu.make_async_copy(other.at[:, inner, t], wscr.at[t, :, 1 - c], sem).start()

    if len(pieces) == 2:
        start(*pieces)
    else:

        @pl.when(scal[2] == 0)
        def _():
            start(*pieces[:2])

        @pl.when(scal[2] != 0)
        def _():
            start(*pieces[2:])


def await_weights(wscr, sem):
    pltpu.make_async_copy(wscr, wscr, sem).wait()


def half_weights(wscr, t):
    value = wscr[t]
    return value.reshape(value.shape[0] * value.shape[1] * value.shape[2], value.shape[3])


def standardize(hidden):
    average = jnp.mean(hidden, axis=-1, keepdims=True)
    centered = hidden - average
    variance = jnp.mean(centered * centered, axis=-1, keepdims=True)
    scale = lax.rsqrt(variance + EPS)
    return centered * scale, scale


def nt(a, b):
    return lax.dot_general(
        a.astype(BF16), b.astype(BF16), (((1,), (1,)), ((), ())), preferred_element_type=F32
    )


def nn(a, b):
    return lax.dot_general(
        a.astype(BF16), b.astype(BF16), (((1,), (0,)), ((), ())), preferred_element_type=F32
    )


def tn(a, b):
    return lax.dot_general(
        a.astype(BF16), b.astype(BF16), (((0,), (0,)), ((), ())), preferred_element_type=F32
    )


def unit(rows):
    scale = lax.rsqrt(jnp.mean(rows * rows, axis=-1, keepdims=True) + EPS)
    return rows * scale, scale


def weights_of(q, k, length):
    scores = nt(q, k) * (1.0 / math.sqrt(HDIM))
    position = lax.broadcasted_iota(jnp.int32, scores.shape, 1)
    usable = (position < IMG) | (position - IMG < length)
    weights = jnp.where(usable, jnp.exp(scores), 0.0)
    return weights / jnp.sum(weights, axis=-1, keepdims=True)


def load_hidden(scal, ins, hs):
    y = scal[0]
    chunk = hs.shape[2]

    def from_whole(ref):
        for t in range(QUART):
            hs[t] = ref[:, t * chunk : (t + 1) * chunk]

    def from_chunks(parts):
        for d in range(QUART):
            hs[lax.rem(y + QUART - d, QUART)] = parts[d][...]

    if len(ins) == 1:
        from_whole(ins[0])
    elif len(ins) == QUART:
        from_chunks(ins)
    else:

        @pl.when(scal[2] == 0)
        def _():
            from_whole(ins[0])

        @pl.when(scal[2] != 0)
        def _():
            from_chunks(ins[1:])


def whole(hs):
    return jnp.concatenate([hs[t].astype(F32) for t in range(QUART)], axis=1)


def forward_kernel(k, n_in, n_w, send, scal, *refs):
    ins, refs = refs[:n_in], refs[n_in:]
    mods, gates = refs[:2]
    pieces, refs = refs[2 : 2 + n_w], refs[2 + n_w :]
    if send:
        out_ref, refs = refs[0], refs[1:]
    hidden_out, normed_out, proj_out, normed_ref, proj_ref, wscr, hs, sem, sems = refs
    hidden_save = pltpu.make_async_copy(hs, hidden_out, sems.at[2])
    normed_save = pltpu.make_async_copy(normed_ref, normed_out, sems.at[0])
    proj_save = pltpu.make_async_copy(proj_ref, proj_out, sems.at[1])
    y = scal[0]
    micro, j, slot = place(scal, k)
    fetch_weights(scal, j, pieces, wscr, sem)
    chunk = hs.shape[2]
    rows, width = normed_ref.shape
    seq = rows // PAIR
    load_hidden(scal, ins, hs)
    hidden_save.start()
    normal, _ = standardize(whole(hs))
    normal = normal.reshape(PAIR, seq, width)
    normed = jnp.concatenate(
        [
            (1.0 + mods[slot, PAIR * micro + s, 1:2, :]) * normal[s]
            + mods[slot, PAIR * micro + s, 0:1, :]
            for s in range(PAIR)
        ],
        axis=0,
    ).astype(BF16)
    normed_ref[...] = normed
    normed_save.start()
    await_weights(wscr, sem)
    halves = wscr.shape[0]
    span = width // halves
    projected = nn(normed[:, :span], half_weights(wscr, 0))
    for t in range(1, halves):
        projected += nn(normed[:, t * span : (t + 1) * span], half_weights(wscr, t))
    proj_ref[...] = projected
    proj_save.start()
    if not send:
        normed_save.wait()
        hidden_save.wait()
        proj_save.wait()
        return
    own = hs[y].astype(F32)
    for s in range(PAIR):
        length = scal[3 + PAIR * micro + s]
        r = slice(s * seq, (s + 1) * seq)
        mixed = []
        for h in range(chunk // HDIM):
            lo = h * HDIM
            q, _ = unit(proj_ref[r, lo : lo + HDIM])
            key, _ = unit(proj_ref[r, chunk + lo : chunk + lo + HDIM])
            v = proj_ref[r, 2 * chunk + lo : 2 * chunk + lo + HDIM]
            mixed.append(nn(weights_of(q, key, length), v))
        mixture = jnp.concatenate(mixed, axis=1)
        gate = gates[slot, PAIR * micro + s]
        hs_rows = own[r] + gate * mixture
        if s == 0:
            first = hs_rows
    out_ref[...] = jnp.concatenate([first, hs_rows], axis=0).astype(BF16)
    normed_save.wait()
    hidden_save.wait()
    proj_save.wait()


def backward_kernel(k, n_in, n_w, send, scal, *refs):
    ins, refs = refs[:n_in], refs[n_in:]
    mods, gates, hidden, projected = refs[:4]
    pieces, refs = refs[4 : 4 + n_w], refs[4 + n_w :]
    outs, refs = refs[: QUART * send], refs[QUART * send :]
    low_out, low_ref, proj_ref, wscr, hs, gs, dp, ds, sem, sems = refs
    low_save = pltpu.make_async_copy(low_ref, low_out, sems.at[0])
    proj_load = pltpu.make_async_copy(projected, proj_ref, sems.at[1])
    proj_load.start()
    y = scal[0]
    micro, j, slot = place(scal, k)
    if send:
        hidden_load = pltpu.make_async_copy(hidden, hs, sems.at[2])
        hidden_load.start()
        fetch_weights(scal, j, pieces, wscr, sem)
    rows, chunk = gs.shape
    width = chunk * QUART
    seq = rows // PAIR

    def total(parts):
        gs[...] = sum([part[...].astype(F32) for part in parts[1:]], parts[0][...].astype(F32))

    if n_in in (1, QUART):
        total(ins)
    else:

        @pl.when(scal[2] != 0)
        def _():
            total(ins[:1])

        @pl.when(scal[2] == 0)
        def _():
            total(ins[1:])

    proj_load.wait()
    root = 1.0 / math.sqrt(HDIM)
    for s in range(PAIR):
        length = scal[3 + PAIR * micro + s]
        r = slice(s * seq, (s + 1) * seq)
        for h in range(chunk // HDIM):
            lo = h * HDIM
            c = slice(lo, lo + HDIM)
            gate = gates[slot, PAIR * micro + s, :, c]
            dmix = gs[r, c] * gate
            q, rq = unit(proj_ref[r, lo : lo + HDIM])
            key, rk = unit(proj_ref[r, chunk + lo : chunk + lo + HDIM])
            v = proj_ref[r, 2 * chunk + lo : 2 * chunk + lo + HDIM]
            att = weights_of(q, key, length)
            datt = nt(dmix, v)
            dscore = att * (datt - jnp.sum(att * datt, axis=-1, keepdims=True)) * root
            dqn = nn(dscore, key)
            dkn = tn(dscore, q)
            dp[r, c] = rq * (dqn - q * jnp.mean(dqn * q, axis=-1, keepdims=True))
            dp[r, chunk + lo : chunk + lo + HDIM] = rk * (
                dkn - key * jnp.mean(dkn * key, axis=-1, keepdims=True)
            )
            dp[r, 2 * chunk + lo : 2 * chunk + lo + HDIM] = tn(att, dmix)
    low = dp[...].astype(BF16)
    low_ref[...] = low
    low_save.start()
    if not send:
        low_save.wait()
        return
    hidden_load.wait()
    normal, scale = standardize(whole(hs))
    await_weights(wscr, sem)
    halves = wscr.shape[0]
    norm_grad = jnp.concatenate([nt(low, half_weights(wscr, t)) for t in range(halves)], axis=1)
    norm_grad = norm_grad.reshape(PAIR, seq, width)
    grad = jnp.concatenate(
        [(1.0 + mods[slot, PAIR * micro + s, 1:2, :]) * norm_grad[s] for s in range(PAIR)], axis=0
    )
    back = scale * (
        grad
        - jnp.mean(grad, axis=-1, keepdims=True)
        - normal * jnp.mean(grad * normal, axis=-1, keepdims=True)
    )
    for t in range(QUART):
        ds[t] = back[:, t * chunk : (t + 1) * chunk]
    ds[y] = ds[y] + gs[...]
    for d in range(QUART):
        outs[d][...] = ds[lax.rem(y + d, QUART)].astype(BF16)
    low_save.wait()


def weight_grad_kernel(scal, n0, n1, n2, g0, g1, g2, out, nscr, gscr, held, sems):
    c = scal[1]
    rows = n0.shape[0]

    def start(normed, grad):
        pltpu.make_async_copy(normed, nscr.at[0:rows], sems.at[0]).start()
        pltpu.make_async_copy(grad, gscr.at[0:rows], sems.at[1]).start()

    pltpu.make_async_copy(n1, nscr.at[rows : 2 * rows], sems.at[2]).start()
    pltpu.make_async_copy(g1, gscr.at[rows : 2 * rows], sems.at[3]).start()

    @pl.when(scal[2] == 0)
    def _():
        start(n0, g0)

    @pl.when(scal[2] != 0)
    def _():
        start(n2, g2)

    pltpu.make_async_copy(n0, nscr.at[0:rows], sems.at[0]).wait()
    pltpu.make_async_copy(g0, gscr.at[0:rows], sems.at[1]).wait()
    pltpu.make_async_copy(n1, nscr.at[rows : 2 * rows], sems.at[2]).wait()
    pltpu.make_async_copy(g1, gscr.at[rows : 2 * rows], sems.at[3]).wait()
    share = out.shape[3]
    depth = out.shape[1]
    steps, cores, count = held.shape[:3]
    per = cores * count * share
    right = gscr[...]
    saves = []
    for t in range(steps):
        value = tn(nscr[:, t * per : (t + 1) * per], right).astype(BF16)
        half, z = divmod(t * count, depth)
        for core in range(cores):
            for u in range(count):
                at = (u * cores + core) * share
                held[t, core, u] = value[at : at + share]
            save = pltpu.make_async_copy(
                held.at[t, core],
                out.at[lax.rem(core + c, cores), z : z + count, half],
                sems.at[4 + t * cores + core],
            )
            save.start()
            saves.append(save)
    for save in saves:
        save.wait()


def shards(latents, out_grad, w_qkv, mod_table, timesteps, text_len):
    y = lax.axis_index("y")
    p = lax.rem(lax.axis_index("xl") + y, 2)
    half = lax.axis_index("xh")
    core = lax.axis_index("c")
    halves = lax.axis_size("xh")
    depth = lax.axis_size("z")
    cores = lax.axis_size("c")
    count, _, seq, width = latents.shape
    share = w_qkv.shape[1]
    chunk = width // QUART
    cols = 3 * chunk
    rows = PAIR * seq
    nj = BLOCKS // 2
    count_z = max(384 // (cores * share), 1)
    strips = width // (cores * count_z * share)
    levels = mod_table.shape[1]

    def swap(value, axis):
        return lax.ppermute(value, axis, [(0, 1), (1, 0)])

    fine = ("y", "xl", "xh")

    def route(dx, dy, back, group):
        pairs = []
        for yy in range(QUART):
            to = (yy + dy) % QUART
            if group is not None and to // 2 != group:
                continue
            for xx in range(2):
                there = (xx + (yy if back else to)) % 2
                for hh in range(halves):
                    pairs.append(
                        (
                            (yy * 2 + xx) * halves + hh,
                            (to * 2 + there) * halves + (hh + dx) % halves,
                        )
                    )
        return pairs

    def pick(stack, index):
        return lax.dynamic_index_in_dim(stack, index, 0, keepdims=False)

    quarters = w_qkv[0].reshape(share, 3, QUART, chunk).transpose(2, 0, 1, 3)
    quarters = quarters.reshape(QUART, share, cols)
    leaves = [pick(quarters, lax.rem(y + dy, QUART)) for dy in range(QUART)]
    arrived = [
        [lax.ppermute(leaves[dy], fine, route(dx, dy, False, None)) for dy in range(QUART)]
        for dx in range(halves)
    ]
    arrived = [jnp.stack(row) for row in arrived]
    gathered = []
    for g in range(nj // 2):
        part = []
        for j in (2 * g, 2 * g + 1):
            mine = [pick(arrived[dx], lax.rem(y + QUART - j, QUART)) for dx in range(halves)]
            if halves == 2:
                mine = [jnp.where(half == h, mine[0], mine[1]) for h in range(2)]
            part.append(jnp.stack(mine))
        gathered.append(lax.all_gather(jnp.stack(part), "z", axis=0))

    onehot = (timesteps[:, 0][:, None] == jnp.arange(levels, dtype=jnp.int32)[None, :]).astype(F32)
    table, _ = lax.optimization_barrier((mod_table, arrived[0]))
    modulations = jnp.dot(
        onehot, table[0].reshape(levels, 3 * width), precision=lax.Precision.HIGHEST
    ).reshape(count, 3, width)
    mods = jnp.stack(
        [lax.ppermute(modulations, fine, route(0, dy, False, None)) for dy in range(QUART)]
    )
    first, mods = lax.optimization_barrier((gathered[0], mods))
    pieces = [(first, swap(first, "c"))]
    gates = lax.dynamic_slice_in_dim(mods[:, :, 2:3, :], y * chunk, chunk, axis=3)
    scal = jnp.concatenate(
        [jnp.stack([y, core, p]).astype(jnp.int32), text_len[:, 0].astype(jnp.int32)]
    )
    entering = latents.reshape(count // PAIR, rows, width)
    leaving = lax.dynamic_slice_in_dim(
        out_grad.reshape(count // PAIR, rows, width), y * chunk, chunk, axis=2
    )

    routes = [
        [
            (yy * 2 + xx, ((yy + d) % QUART) * 2 + (1 + xx + d) % 2)
            for yy in range(QUART)
            for xx in range(2)
        ]
        for d in range(QUART)
    ]

    def send(parts):
        return [lax.ppermute(parts[d], ("y", "xl"), routes[d]) for d in range(QUART)]

    wscr = pltpu.VMEM((halves, depth, cores, share, cols), BF16)
    params = pltpu.CompilerParams(vmem_limit_bytes=VMEM_LIMIT)

    def held(k):
        first, second = min(k // 2, nj - 1), max((k - 1) // 2, 0)
        first, second = first // 2, second // 2
        if first == second:
            return pieces[first]
        return pieces[first] + pieces[second]

    def shape(cols, kind):
        return jax.ShapeDtypeStruct((rows, cols), kind)

    steps = BLOCKS + 1
    saved = []
    received = None
    for k in range(steps):
        if k == 0:
            ins = [entering[0]]
        elif k == 1:
            ins = [entering[1]] + received
        else:
            ins = received
        weights = held(k)
        sending = k < steps - 1
        state = jax.ShapeDtypeStruct((QUART, rows, chunk), BF16)
        outs = [state, shape(width, BF16), shape(cols, F32)]
        if sending:
            outs = [shape(chunk, BF16)] + outs
        result = pl.pallas_call(
            functools.partial(forward_kernel, k, len(ins), len(weights), sending),
            out_shape=outs,
            in_specs=[SM] + [VM] * (len(ins) + 2) + [HBM] * len(weights),
            out_specs=[VM] * sending + [HBM] * 3,
            scratch_shapes=[
                pltpu.VMEM((rows, width), BF16),
                pltpu.VMEM((rows, cols), F32),
                wscr,
                pltpu.VMEM((QUART, rows, chunk), BF16),
                pltpu.SemaphoreType.DMA,
                pltpu.SemaphoreType.DMA((3,)),
            ],
            compiler_params=params,
            name="forward_step",
        )(scal, *ins, mods, gates, *weights)
        if sending:
            received = send([result[0]] * QUART)
            result = result[1:]
        if k == 2:
            second, _ = lax.optimization_barrier((gathered[1], received[0]))
            pieces.append((second, swap(second, "c")))
        saved.append(result)

    lows = [None] * steps
    chips = [None] * nj
    rings = [None] * (nj // 2)
    received = None
    for k in reversed(range(steps)):
        if k == steps - 1:
            ins = [leaving[1]]
        elif k == steps - 2:
            ins = [leaving[0]] + received
        else:
            ins = received
        weights = held(k)
        sending = k > 0
        outs = [shape(chunk, BF16)] * (QUART * sending) + [shape(cols, BF16)]
        hidden, _, projected = saved[k]
        result = pl.pallas_call(
            functools.partial(backward_kernel, k, len(ins), len(weights), sending),
            out_shape=outs,
            in_specs=[SM] + [VM] * (len(ins) + 2) + [HBM] * (2 + len(weights)),
            out_specs=[VM] * (len(outs) - 1) + [HBM],
            scratch_shapes=[
                pltpu.VMEM((rows, cols), BF16),
                pltpu.VMEM((rows, cols), F32),
                wscr,
                pltpu.VMEM((QUART, rows, chunk), BF16),
                pltpu.VMEM((rows, chunk), F32),
                pltpu.VMEM((rows, cols), F32),
                pltpu.VMEM((QUART, rows, chunk), F32),
                pltpu.SemaphoreType.DMA,
                pltpu.SemaphoreType.DMA((3,)),
            ],
            compiler_params=params,
            name="backward_step",
        )(scal, *ins, mods, gates, hidden, projected, *weights)
        lows[k] = result[-1]
        if sending:
            received = send(result[:-1])
        if k % 2 == 0 and k < steps - 1:
            j = k // 2
            factors = [saved[k + i][1] for i in range(3)] + [lows[k + i] for i in range(3)]
            if sending:
                factors, received[0] = lax.optimization_barrier((factors, received[0]))
            partial = pl.pallas_call(
                weight_grad_kernel,
                out_shape=jax.ShapeDtypeStruct((cores, depth, halves, share, cols), BF16),
                in_specs=[SM] + [HBM] * 6,
                out_specs=HBM,
                scratch_shapes=[
                    pltpu.VMEM((2 * rows, width), BF16),
                    pltpu.VMEM((2 * rows, cols), BF16),
                    pltpu.VMEM((strips, cores, count_z, share, cols), BF16),
                    pltpu.SemaphoreType.DMA((4 + strips * cores,)),
                ],
                compiler_params=params,
                cost_estimate=pl.CostEstimate(
                    flops=4 * rows * width * cols,
                    bytes_accessed=4 * width * cols,
                    transcendentals=0,
                ),
                name="weight_grad",
            )(scal, *factors)
            if sending:
                partial, received[1] = lax.optimization_barrier((partial, received[1]))
            chips[j] = (partial[0], swap(partial[1], "c"))
        if k in (0, 3):
            g = k // 3
            total = jnp.concatenate(
                [
                    (chips[i][0] + chips[i][1]).reshape(depth, halves * share, cols)
                    for i in (2 * g, 2 * g + 1)
                ],
                axis=1,
            )
            if sending:
                total, received[1] = lax.optimization_barrier((total, received[1]))
            else:
                total, rings[1] = lax.optimization_barrier((total, rings[1]))
            rings[g] = lax.psum_scatter(total, "z", scatter_dimension=0)

    def hand_back(g):
        ring = rings[g].reshape(2 * halves, share, cols)
        parts = []
        for dy in range(QUART):
            for dx in range(halves):
                index = lax.rem(y + dy, 2) * halves + lax.rem(half + dx, halves)
                parts.append(lax.ppermute(pick(ring, index), fine, route(dx, dy, True, g)))
        return parts

    upper = hand_back(1)
    rings[0], upper = lax.optimization_barrier((rings[0], upper))
    lower = hand_back(0)
    finals = []
    for dy in range(QUART):
        near = slice(dy * halves, (dy + 1) * halves)
        parts = [part.astype(F32) for part in upper[near] + lower[near]]
        finals.append(sum(parts).reshape(share, 3, chunk))
    finals = jnp.stack(finals)
    grads = jnp.stack([pick(finals, lax.rem(y + QUART - q, QUART)) for q in range(QUART)], axis=2)
    return grads.reshape(1, share, 3 * width)


def solution(mesh):
    fine = Mesh(mesh.devices.reshape(4, 2, 2, 8, 2), ("y", "xl", "xh", "z", "c"))
    pipe = ("y", "xl")
    dp = ("xh", "z", "c")
    return jax.shard_map(
        shards,
        mesh=fine,
        in_specs=(
            P(None, dp, None, None),
            P(None, dp, None, None),
            P(pipe, dp, None),
            P(pipe, None, None, None),
            P(None, dp),
            P(None, dp),
        ),
        out_specs=P(pipe, dp, None),
        check_vma=False,
    )
```

```python
import functools
import math

import jax
import jax.numpy as jnp
from jax import lax
from jax.experimental import pallas as pl
from jax.experimental.pallas import tpu as pltpu
from jax.sharding import Mesh
from jax.sharding import PartitionSpec as P

IMG = 40
EPS = 1e-06
HDIM = 128
BLOCKS = 8
QUART = 4
PAIR = 2
F32 = jnp.float32
BF16 = jnp.bfloat16
VMEM_LIMIT = 16 * 1024 * 1024
VM = pl.BlockSpec(memory_space=pltpu.VMEM)
SM = pl.BlockSpec(memory_space=pltpu.SMEM)
HBM = pl.BlockSpec(memory_space=pltpu.HBM)


def place(scal, k):
    p = scal[2]
    j = lax.max((k - p + 2) // 2 - 1, 0)
    j = lax.min(j, BLOCKS // 2 - 1)
    return lax.rem(k + p, 2), j, lax.rem(scal[0] + QUART - j, QUART)


def fetch_weights(scal, j, pieces, wscr, sem):
    c = scal[1]
    halves = wscr.shape[0]
    inner = lax.rem(j, 2)

    def start(own, other):
        for t in range(halves):
            pltpu.make_async_copy(own.at[:, inner, t], wscr.at[t, :, c], sem).start()
            pltpu.make_async_copy(other.at[:, inner, t], wscr.at[t, :, 1 - c], sem).start()

    if len(pieces) == 2:
        start(*pieces)
    else:

        @pl.when(scal[2] == 0)
        def _():
            start(*pieces[:2])

        @pl.when(scal[2] != 0)
        def _():
            start(*pieces[2:])


def await_weights(wscr, sem):
    pltpu.make_async_copy(wscr, wscr, sem).wait()


def half_weights(wscr, t):
    value = wscr[t]
    return value.reshape(value.shape[0] * value.shape[1] * value.shape[2], value.shape[3])


def standardize(hidden):
    average = jnp.mean(hidden, axis=-1, keepdims=True)
    centered = hidden - average
    variance = jnp.mean(centered * centered, axis=-1, keepdims=True)
    scale = lax.rsqrt(variance + EPS)
    return centered * scale, scale


def nt(a, b):
    return lax.dot_general(
        a.astype(BF16), b.astype(BF16), (((1,), (1,)), ((), ())), preferred_element_type=F32
    )


def nn(a, b):
    return lax.dot_general(
        a.astype(BF16), b.astype(BF16), (((1,), (0,)), ((), ())), preferred_element_type=F32
    )


def tn(a, b):
    return lax.dot_general(
        a.astype(BF16), b.astype(BF16), (((0,), (0,)), ((), ())), preferred_element_type=F32
    )


def unit(rows):
    scale = lax.rsqrt(jnp.mean(rows * rows, axis=-1, keepdims=True) + EPS)
    return rows * scale, scale


def weights_of(q, k, length):
    scores = nt(q, k) * (1.0 / math.sqrt(HDIM))
    position = lax.broadcasted_iota(jnp.int32, scores.shape, 1)
    usable = (position < IMG) | (position - IMG < length)
    weights = jnp.where(usable, jnp.exp(scores), 0.0)
    return weights / jnp.sum(weights, axis=-1, keepdims=True)


def load_hidden(scal, ins, hs):
    y = scal[0]
    chunk = hs.shape[2]

    def from_whole(ref):
        for t in range(QUART):
            hs[t] = ref[:, t * chunk : (t + 1) * chunk]

    def from_chunks(parts):
        for d in range(QUART):
            hs[lax.rem(y + QUART - d, QUART)] = parts[d][...]

    if len(ins) == 1:
        from_whole(ins[0])
    elif len(ins) == QUART:
        from_chunks(ins)
    else:

        @pl.when(scal[2] == 0)
        def _():
            from_whole(ins[0])

        @pl.when(scal[2] != 0)
        def _():
            from_chunks(ins[1:])


def whole(hs):
    return jnp.concatenate([hs[t].astype(F32) for t in range(QUART)], axis=1)


def forward_kernel(k, n_in, n_w, send, scal, *refs):
    ins, refs = refs[:n_in], refs[n_in:]
    mods, gates = refs[:2]
    pieces, refs = refs[2 : 2 + n_w], refs[2 + n_w :]
    if send:
        out_ref, refs = refs[0], refs[1:]
    hidden_out, normed_out, proj_out, normed_ref, proj_ref, wscr, hs, sem, sems = refs
    hidden_save = pltpu.make_async_copy(hs, hidden_out, sems.at[2])
    normed_save = pltpu.make_async_copy(normed_ref, normed_out, sems.at[0])
    proj_save = pltpu.make_async_copy(proj_ref, proj_out, sems.at[1])
    y = scal[0]
    micro, j, slot = place(scal, k)
    fetch_weights(scal, j, pieces, wscr, sem)
    chunk = hs.shape[2]
    rows, width = normed_ref.shape
    seq = rows // PAIR
    load_hidden(scal, ins, hs)
    hidden_save.start()
    normal, _ = standardize(whole(hs))
    normal = normal.reshape(PAIR, seq, width)
    normed = jnp.concatenate(
        [
            (1.0 + mods[slot, PAIR * micro + s, 1:2, :]) * normal[s]
            + mods[slot, PAIR * micro + s, 0:1, :]
            for s in range(PAIR)
        ],
        axis=0,
    ).astype(BF16)
    normed_ref[...] = normed
    normed_save.start()
    await_weights(wscr, sem)
    halves = wscr.shape[0]
    span = width // halves
    projected = nn(normed[:, :span], half_weights(wscr, 0))
    for t in range(1, halves):
        projected += nn(normed[:, t * span : (t + 1) * span], half_weights(wscr, t))
    proj_ref[...] = projected
    proj_save.start()
    if not send:
        normed_save.wait()
        hidden_save.wait()
        proj_save.wait()
        return
    own = hs[y].astype(F32)
    for s in range(PAIR):
        length = scal[3 + PAIR * micro + s]
        r = slice(s * seq, (s + 1) * seq)
        mixed = []
        for h in range(chunk // HDIM):
            lo = h * HDIM
            q, _ = unit(proj_ref[r, lo : lo + HDIM])
            key, _ = unit(proj_ref[r, chunk + lo : chunk + lo + HDIM])
            v = proj_ref[r, 2 * chunk + lo : 2 * chunk + lo + HDIM]
            mixed.append(nn(weights_of(q, key, length), v))
        mixture = jnp.concatenate(mixed, axis=1)
        gate = gates[slot, PAIR * micro + s]
        hs_rows = own[r] + gate * mixture
        if s == 0:
            first = hs_rows
    out_ref[...] = jnp.concatenate([first, hs_rows], axis=0).astype(BF16)
    normed_save.wait()
    hidden_save.wait()
    proj_save.wait()


def backward_kernel(k, n_in, n_w, send, scal, *refs):
    ins, refs = refs[:n_in], refs[n_in:]
    mods, gates, hidden, projected = refs[:4]
    pieces, refs = refs[4 : 4 + n_w], refs[4 + n_w :]
    outs, refs = refs[: QUART * send], refs[QUART * send :]
    low_out, low_ref, proj_ref, wscr, hs, gs, dp, ds, sem, sems = refs
    low_save = pltpu.make_async_copy(low_ref, low_out, sems.at[0])
    proj_load = pltpu.make_async_copy(projected, proj_ref, sems.at[1])
    proj_load.start()
    y = scal[0]
    micro, j, slot = place(scal, k)
    if send:
        hidden_load = pltpu.make_async_copy(hidden, hs, sems.at[2])
        hidden_load.start()
        fetch_weights(scal, j, pieces, wscr, sem)
    rows, chunk = gs.shape
    width = chunk * QUART
    seq = rows // PAIR

    def total(parts):
        gs[...] = sum([part[...].astype(F32) for part in parts[1:]], parts[0][...].astype(F32))

    if n_in in (1, QUART):
        total(ins)
    else:

        @pl.when(scal[2] != 0)
        def _():
            total(ins[:1])

        @pl.when(scal[2] == 0)
        def _():
            total(ins[1:])

    proj_load.wait()
    root = 1.0 / math.sqrt(HDIM)
    for s in range(PAIR):
        length = scal[3 + PAIR * micro + s]
        r = slice(s * seq, (s + 1) * seq)
        for h in range(chunk // HDIM):
            lo = h * HDIM
            c = slice(lo, lo + HDIM)
            gate = gates[slot, PAIR * micro + s, :, c]
            dmix = gs[r, c] * gate
            q, rq = unit(proj_ref[r, lo : lo + HDIM])
            key, rk = unit(proj_ref[r, chunk + lo : chunk + lo + HDIM])
            v = proj_ref[r, 2 * chunk + lo : 2 * chunk + lo + HDIM]
            att = weights_of(q, key, length)
            datt = nt(dmix, v)
            dscore = att * (datt - jnp.sum(att * datt, axis=-1, keepdims=True)) * root
            dqn = nn(dscore, key)
            dkn = tn(dscore, q)
            dp[r, c] = rq * (dqn - q * jnp.mean(dqn * q, axis=-1, keepdims=True))
            dp[r, chunk + lo : chunk + lo + HDIM] = rk * (
                dkn - key * jnp.mean(dkn * key, axis=-1, keepdims=True)
            )
            dp[r, 2 * chunk + lo : 2 * chunk + lo + HDIM] = tn(att, dmix)
    low = dp[...].astype(BF16)
    low_ref[...] = low
    low_save.start()
    if not send:
        low_save.wait()
        return
    hidden_load.wait()
    normal, scale = standardize(whole(hs))
    await_weights(wscr, sem)
    halves = wscr.shape[0]
    norm_grad = jnp.concatenate([nt(low, half_weights(wscr, t)) for t in range(halves)], axis=1)
    norm_grad = norm_grad.reshape(PAIR, seq, width)
    grad = jnp.concatenate(
        [(1.0 + mods[slot, PAIR * micro + s, 1:2, :]) * norm_grad[s] for s in range(PAIR)], axis=0
    )
    back = scale * (
        grad
        - jnp.mean(grad, axis=-1, keepdims=True)
        - normal * jnp.mean(grad * normal, axis=-1, keepdims=True)
    )
    for t in range(QUART):
        ds[t] = back[:, t * chunk : (t + 1) * chunk]
    ds[y] = ds[y] + gs[...]
    for d in range(QUART):
        outs[d][...] = ds[lax.rem(y + d, QUART)].astype(BF16)
    low_save.wait()


def weight_grad_kernel(scal, n0, n1, n2, g0, g1, g2, out, nscr, gscr, held, sems):
    c = scal[1]
    rows = n0.shape[0]

    def start(normed, grad):
        pltpu.make_async_copy(normed, nscr.at[0:rows], sems.at[0]).start()
        pltpu.make_async_copy(grad, gscr.at[0:rows], sems.at[1]).start()

    pltpu.make_async_copy(n1, nscr.at[rows : 2 * rows], sems.at[2]).start()
    pltpu.make_async_copy(g1, gscr.at[rows : 2 * rows], sems.at[3]).start()

    @pl.when(scal[2] == 0)
    def _():
        start(n0, g0)

    @pl.when(scal[2] != 0)
    def _():
        start(n2, g2)

    pltpu.make_async_copy(n0, nscr.at[0:rows], sems.at[0]).wait()
    pltpu.make_async_copy(g0, gscr.at[0:rows], sems.at[1]).wait()
    pltpu.make_async_copy(n1, nscr.at[rows : 2 * rows], sems.at[2]).wait()
    pltpu.make_async_copy(g1, gscr.at[rows : 2 * rows], sems.at[3]).wait()
    share = out.shape[3]
    depth = out.shape[1]
    steps, cores, count = held.shape[:3]
    per = cores * count * share
    right = gscr[...]
    saves = []
    for t in range(steps):
        value = tn(nscr[:, t * per : (t + 1) * per], right).astype(BF16)
        half, z = divmod(t * count, depth)
        for core in range(cores):
            for u in range(count):
                at = (u * cores + core) * share
                held[t, core, u] = value[at : at + share]
            save = pltpu.make_async_copy(
                held.at[t, core],
                out.at[lax.rem(core + c, cores), z : z + count, half],
                sems.at[4 + t * cores + core],
            )
            save.start()
            saves.append(save)
    for save in saves:
        save.wait()


def shards(latents, out_grad, w_qkv, mod_table, timesteps, text_len):
    y = lax.axis_index("y")
    p = lax.rem(lax.axis_index("xl") + y, 2)
    half = lax.axis_index("xh")
    core = lax.axis_index("c")
    halves = lax.axis_size("xh")
    depth = lax.axis_size("z")
    cores = lax.axis_size("c")
    count, _, seq, width = latents.shape
    share = w_qkv.shape[1]
    chunk = width // QUART
    cols = 3 * chunk
    rows = PAIR * seq
    nj = BLOCKS // 2
    count_z = max(384 // (cores * share), 1)
    strips = width // (cores * count_z * share)
    levels = mod_table.shape[1]

    def swap(value, axis):
        return lax.ppermute(value, axis, [(0, 1), (1, 0)])

    fine = ("y", "xl")

    def route(dy, back, group):
        pairs = []
        for yy in range(QUART):
            to = (yy + dy) % QUART
            if group is not None and to // 2 != group:
                continue
            for xx in range(2):
                there = (xx + (yy if back else to)) % 2
                pairs.append((yy * 2 + xx, to * 2 + there))
        return pairs

    def pick(stack, index):
        return lax.dynamic_index_in_dim(stack, index, 0, keepdims=False)

    quarters = w_qkv[0].reshape(share, 3, QUART, chunk).transpose(2, 0, 1, 3)
    quarters = quarters.reshape(QUART, share, cols)
    leaves = [pick(quarters, lax.rem(y + dy, QUART)) for dy in range(QUART)]
    arrived = jnp.stack(
        [lax.ppermute(leaves[dy], fine, route(dy, False, None)) for dy in range(QUART)]
    )
    gathered = []
    for g in range(nj // 2):
        mine = jnp.stack(
            [pick(arrived, lax.rem(y + QUART - j, QUART)) for j in (2 * g, 2 * g + 1)]
        )
        if g > 0:
            mine, _ = lax.optimization_barrier((mine, part))
        if halves == 2:
            other = swap(mine, "xh")
            mine = [jnp.where(half == h, mine, other) for h in range(2)]
            part = jnp.stack(mine, axis=1)
        else:
            part = mine[:, None]
        gathered.append(lax.all_gather(part, "z", axis=0))

    onehot = (timesteps[:, 0][:, None] == jnp.arange(levels, dtype=jnp.int32)[None, :]).astype(F32)
    table, _ = lax.optimization_barrier((mod_table, arrived))
    modulations = jnp.dot(
        onehot, table[0].reshape(levels, 3 * width), precision=lax.Precision.HIGHEST
    ).reshape(count, 3, width)
    mods = jnp.stack(
        [lax.ppermute(modulations, fine, route(dy, False, None)) for dy in range(QUART)]
    )
    gates = lax.dynamic_slice_in_dim(mods[:, :, 2:3, :], y * chunk, chunk, axis=3)
    scal = jnp.concatenate(
        [jnp.stack([y, core, p]).astype(jnp.int32), text_len[:, 0].astype(jnp.int32)]
    )
    entering = latents.reshape(count // PAIR, rows, width)
    leaving = lax.dynamic_slice_in_dim(
        out_grad.reshape(count // PAIR, rows, width), y * chunk, chunk, axis=2
    )

    first, mods, gates, entering = lax.optimization_barrier((gathered[0], mods, gates, entering))
    pieces = [(first, swap(first, "c"))]
    routes = [
        [
            (yy * 2 + xx, ((yy + d) % QUART) * 2 + (1 + xx + d) % 2)
            for yy in range(QUART)
            for xx in range(2)
        ]
        for d in range(QUART)
    ]

    def send(parts):
        return [lax.ppermute(parts[d], ("y", "xl"), routes[d]) for d in range(QUART)]

    wscr = pltpu.VMEM((halves, depth, cores, share, cols), BF16)
    params = pltpu.CompilerParams(vmem_limit_bytes=VMEM_LIMIT)

    def held(k):
        first, second = min(k // 2, nj - 1), max((k - 1) // 2, 0)
        first, second = first // 2, second // 2
        if first == second:
            return pieces[first]
        return pieces[first] + pieces[second]

    def shape(cols, kind):
        return jax.ShapeDtypeStruct((rows, cols), kind)

    def kept(dims, kind):
        return pltpu.HBM(dims, kind)

    def pinned(values):
        return [pltpu.with_memory_space_constraint(value, pltpu.HBM) for value in values]

    steps = BLOCKS + 1
    saved = []
    received = None
    for k in range(steps):
        if k == 0:
            ins = [entering[0]]
        elif k == 1:
            ins = [entering[1]] + received
        else:
            ins = received
        weights = held(k)
        sending = k < steps - 1
        outs = [
            kept((QUART, rows, chunk), BF16),
            kept((rows, width), BF16),
            kept((rows, cols), F32),
        ]
        if sending:
            outs = [shape(chunk, BF16)] + outs
        result = pl.pallas_call(
            functools.partial(forward_kernel, k, len(ins), len(weights), sending),
            out_shape=outs,
            in_specs=[SM] + [VM] * (len(ins) + 2) + [HBM] * len(weights),
            out_specs=[VM] * sending + [HBM] * 3,
            scratch_shapes=[
                pltpu.VMEM((rows, width), BF16),
                pltpu.VMEM((rows, cols), F32),
                wscr,
                pltpu.VMEM((QUART, rows, chunk), BF16),
                pltpu.SemaphoreType.DMA,
                pltpu.SemaphoreType.DMA((3,)),
            ],
            compiler_params=params,
            name="forward_step",
        )(scal, *ins, mods, gates, *pinned(weights))
        if sending:
            received = send([result[0]] * QUART)
            result = result[1:]
        if k == 3:
            second, _ = lax.optimization_barrier((gathered[1], result[1]))
            pieces.append((second, swap(second, "c")))
        saved.append(result)

    lows = [None] * steps
    chips = [None] * nj
    rings = [None] * (nj // 2)
    received = None
    for k in reversed(range(steps)):
        if k == steps - 1:
            ins = [leaving[1]]
        elif k == steps - 2:
            ins = [leaving[0]] + received
        else:
            ins = received
        weights = held(k)
        sending = k > 0
        outs = [shape(chunk, BF16)] * (QUART * sending) + [kept((rows, cols), BF16)]
        hidden, _, projected = saved[k]
        result = pl.pallas_call(
            functools.partial(backward_kernel, k, len(ins), len(weights), sending),
            out_shape=outs,
            in_specs=[SM] + [VM] * (len(ins) + 2) + [HBM] * (2 + len(weights)),
            out_specs=[VM] * (len(outs) - 1) + [HBM],
            scratch_shapes=[
                pltpu.VMEM((rows, cols), BF16),
                pltpu.VMEM((rows, cols), F32),
                wscr,
                pltpu.VMEM((QUART, rows, chunk), BF16),
                pltpu.VMEM((rows, chunk), F32),
                pltpu.VMEM((rows, cols), F32),
                pltpu.VMEM((QUART, rows, chunk), F32),
                pltpu.SemaphoreType.DMA,
                pltpu.SemaphoreType.DMA((3,)),
            ],
            compiler_params=params,
            name="backward_step",
        )(scal, *ins, mods, gates, *pinned([hidden, projected, *weights]))
        lows[k] = result[-1]
        if sending:
            received = send(result[:-1])
        if k % 2 == 0 and k < steps - 1:
            j = k // 2
            factors = [saved[k + i][1] for i in range(3)] + [lows[k + i] for i in range(3)]
            if sending:
                factors, received[0] = lax.optimization_barrier((factors, received[0]))
            partial = pl.pallas_call(
                weight_grad_kernel,
                out_shape=kept((cores, depth, halves, share, cols), BF16),
                in_specs=[SM] + [HBM] * 6,
                out_specs=HBM,
                scratch_shapes=[
                    pltpu.VMEM((2 * rows, width), BF16),
                    pltpu.VMEM((2 * rows, cols), BF16),
                    pltpu.VMEM((strips, cores, count_z, share, cols), BF16),
                    pltpu.SemaphoreType.DMA((4 + strips * cores,)),
                ],
                compiler_params=params,
                cost_estimate=pl.CostEstimate(
                    flops=4 * rows * width * cols,
                    bytes_accessed=4 * width * cols,
                    transcendentals=0,
                ),
                name="weight_grad",
            )(scal, *pinned(factors))
            if sending:
                partial, received[1] = lax.optimization_barrier((partial, received[1]))
            chips[j] = partial
        if k in (1, 3, 5):
            j = (k + 1) // 2
            chips[j], _ = lax.optimization_barrier((chips[j], lows[k]))
        if k in (0, 1, 3, 5):
            j = (k + 1) // 2
            chips[j] = (chips[j][0], swap(chips[j][1], "c"))
        if k == 4:
            keep, received[1] = lax.optimization_barrier((chips[3][1], received[1]))
            chips[3] = (chips[3][0], keep)
        if k in (0, 2):
            g = k // 2
            total = jnp.concatenate(
                [
                    (chips[i][0] + chips[i][1]).reshape(depth, halves * share, cols)
                    for i in (2 * g, 2 * g + 1)
                ],
                axis=1,
            )
            if sending:
                total, received[1] = lax.optimization_barrier((total, received[1]))
            else:
                total, rings[1] = lax.optimization_barrier((total, rings[1]))
            rings[g] = lax.psum_scatter(total, "z", scatter_dimension=0)

    def hand_back(g):
        ring = rings[g].reshape(2, halves, share, cols)
        ours = lax.dynamic_index_in_dim(ring, half, 1, keepdims=False)
        if halves == 2:
            theirs = swap(lax.dynamic_index_in_dim(ring, 1 - half, 1, keepdims=False), "xh")
            ours = (ours.astype(F32) + theirs.astype(F32)).astype(BF16)
        return [
            lax.ppermute(pick(ours, lax.rem(y + dy, 2)), fine, route(dy, True, g))
            for dy in range(QUART)
        ]

    upper = hand_back(1)
    rings[0], upper = lax.optimization_barrier((rings[0], upper))
    lower = hand_back(0)
    finals = [
        (upper[dy].astype(F32) + lower[dy].astype(F32)).reshape(share, 3, chunk)
        for dy in range(QUART)
    ]
    finals = jnp.stack(finals)
    grads = jnp.stack([pick(finals, lax.rem(y + QUART - q, QUART)) for q in range(QUART)], axis=2)
    return grads.reshape(1, share, 3 * width)


def solution(mesh):
    fine = Mesh(mesh.devices.reshape(4, 2, 2, 8, 2), ("y", "xl", "xh", "z", "c"))
    pipe = ("y", "xl")
    dp = ("xh", "z", "c")
    return jax.shard_map(
        shards,
        mesh=fine,
        in_specs=(
            P(None, dp, None, None),
            P(None, dp, None, None),
            P(pipe, dp, None),
            P(pipe, None, None, None),
            P(None, dp),
            P(None, dp),
        ),
        out_specs=P(pipe, dp, None),
        check_vma=False,
    )
```

```python
import functools
import math

import jax
import jax.numpy as jnp
from jax import lax
from jax.experimental import pallas as pl
from jax.experimental.pallas import tpu as pltpu
from jax.sharding import Mesh
from jax.sharding import PartitionSpec as P

IMG = 40
EPS = 1e-06
HDIM = 128
BLOCKS = 8
QUART = 4
PAIR = 2
F32 = jnp.float32
BF16 = jnp.bfloat16
VMEM_LIMIT = 16 * 1024 * 1024
VM = pl.BlockSpec(memory_space=pltpu.VMEM)
SM = pl.BlockSpec(memory_space=pltpu.SMEM)
HBM = pl.BlockSpec(memory_space=pltpu.HBM)


def place(scal, k):
    p = scal[2]
    j = lax.max((k - p + 2) // 2 - 1, 0)
    j = lax.min(j, BLOCKS // 2 - 1)
    return lax.rem(k + p, 2), j, lax.rem(scal[0] + QUART - j, QUART)


def fetch_weights(scal, j, pieces, wscr, sem):
    c = scal[1]
    halves = wscr.shape[0]
    inner = lax.rem(j, 2)

    def start(own, other):
        for t in range(halves):
            pltpu.make_async_copy(own.at[:, inner, t], wscr.at[t, :, c], sem.at[t]).start()
            pltpu.make_async_copy(other.at[:, inner, t], wscr.at[t, :, 1 - c], sem.at[t]).start()

    if len(pieces) == 2:
        start(*pieces)
    else:

        @pl.when(scal[2] == 0)
        def _():
            start(*pieces[:2])

        @pl.when(scal[2] != 0)
        def _():
            start(*pieces[2:])


def half_weights(wscr, sem, t):
    pltpu.make_async_copy(wscr.at[t], wscr.at[t], sem.at[t]).wait()
    value = wscr[t]
    return value.reshape(value.shape[0] * value.shape[1] * value.shape[2], value.shape[3])


def standardize(hidden):
    average = jnp.mean(hidden, axis=-1, keepdims=True)
    centered = hidden - average
    variance = jnp.mean(centered * centered, axis=-1, keepdims=True)
    scale = lax.rsqrt(variance + EPS)
    return centered * scale, scale


def nt(a, b):
    return lax.dot_general(
        a.astype(BF16), b.astype(BF16), (((1,), (1,)), ((), ())), preferred_element_type=F32
    )


def nn(a, b):
    return lax.dot_general(
        a.astype(BF16), b.astype(BF16), (((1,), (0,)), ((), ())), preferred_element_type=F32
    )


def tn(a, b):
    return lax.dot_general(
        a.astype(BF16), b.astype(BF16), (((0,), (0,)), ((), ())), preferred_element_type=F32
    )


def unit(rows):
    scale = lax.rsqrt(jnp.mean(rows * rows, axis=-1, keepdims=True) + EPS)
    return rows * scale, scale


def weights_of(q, k, length):
    scores = nt(q, k) * (1.0 / math.sqrt(HDIM))
    position = lax.broadcasted_iota(jnp.int32, scores.shape, 1)
    usable = (position < IMG) | (position - IMG < length)
    weights = jnp.where(usable, jnp.exp(scores), 0.0)
    return weights / jnp.sum(weights, axis=-1, keepdims=True)


def load_hidden(scal, ins, hs):
    y = scal[0]
    chunk = hs.shape[2]

    def from_whole(ref):
        for t in range(QUART):
            hs[t] = ref[:, t * chunk : (t + 1) * chunk]

    def from_chunks(parts):
        for d in range(QUART):
            hs[lax.rem(y + QUART - d, QUART)] = parts[d][...]

    if len(ins) == 1:
        from_whole(ins[0])
    elif len(ins) == QUART:
        from_chunks(ins)
    else:

        @pl.when(scal[2] == 0)
        def _():
            from_whole(ins[0])

        @pl.when(scal[2] != 0)
        def _():
            from_chunks(ins[1:])


def whole(hs):
    return jnp.concatenate([hs[t].astype(F32) for t in range(QUART)], axis=1)


def forward_kernel(k, n_in, n_w, send, scal, *refs):
    ins, refs = refs[:n_in], refs[n_in:]
    mods, gates = refs[:2]
    pieces, refs = refs[2 : 2 + n_w], refs[2 + n_w :]
    if send:
        out_ref, refs = refs[0], refs[1:]
    hidden_out, normed_out, proj_out, normed_ref, proj_ref, wscr, hs, sem, sems = refs
    hidden_save = pltpu.make_async_copy(hs, hidden_out, sems.at[2])
    normed_save = pltpu.make_async_copy(normed_ref, normed_out, sems.at[0])
    proj_save = pltpu.make_async_copy(proj_ref, proj_out, sems.at[1])
    y = scal[0]
    micro, j, slot = place(scal, k)
    fetch_weights(scal, j, pieces, wscr, sem)
    chunk = hs.shape[2]
    rows, width = normed_ref.shape
    seq = rows // PAIR
    load_hidden(scal, ins, hs)
    hidden_save.start()
    normal, _ = standardize(whole(hs))
    normal = normal.reshape(PAIR, seq, width)
    normed = jnp.concatenate(
        [
            (1.0 + mods[slot, PAIR * micro + s, 1:2, :]) * normal[s]
            + mods[slot, PAIR * micro + s, 0:1, :]
            for s in range(PAIR)
        ],
        axis=0,
    ).astype(BF16)
    normed_ref[...] = normed
    normed_save.start()
    halves = wscr.shape[0]
    span = width // halves
    projected = nn(normed[:, :span], half_weights(wscr, sem, 0))
    for t in range(1, halves):
        projected += nn(normed[:, t * span : (t + 1) * span], half_weights(wscr, sem, t))
    proj_ref[...] = projected
    proj_save.start()
    if not send:
        normed_save.wait()
        hidden_save.wait()
        proj_save.wait()
        return
    own = hs[y].astype(F32)
    for s in range(PAIR):
        length = scal[3 + PAIR * micro + s]
        r = slice(s * seq, (s + 1) * seq)
        mixed = []
        for h in range(chunk // HDIM):
            lo = h * HDIM
            q, _ = unit(proj_ref[r, lo : lo + HDIM])
            key, _ = unit(proj_ref[r, chunk + lo : chunk + lo + HDIM])
            v = proj_ref[r, 2 * chunk + lo : 2 * chunk + lo + HDIM]
            mixed.append(nn(weights_of(q, key, length), v))
        mixture = jnp.concatenate(mixed, axis=1)
        gate = gates[slot, PAIR * micro + s]
        hs_rows = own[r] + gate * mixture
        if s == 0:
            first = hs_rows
    out_ref[...] = jnp.concatenate([first, hs_rows], axis=0).astype(BF16)
    normed_save.wait()
    hidden_save.wait()
    proj_save.wait()


def backward_kernel(k, n_in, n_w, send, scal, *refs):
    ins, refs = refs[:n_in], refs[n_in:]
    mods, gates, proj_ref, hidden = refs[:4]
    pieces, refs = refs[4 : 4 + n_w], refs[4 + n_w :]
    outs, refs = refs[: QUART * send], refs[QUART * send :]
    low_out, low_ref, wscr, hs, gs, dp, ds, sem, sems = refs
    low_save = pltpu.make_async_copy(low_ref, low_out, sems.at[0])
    y = scal[0]
    micro, j, slot = place(scal, k)
    if send:
        hidden_load = pltpu.make_async_copy(hidden, hs, sems.at[2])
        hidden_load.start()
        fetch_weights(scal, j, pieces, wscr, sem)
    rows, chunk = gs.shape
    width = chunk * QUART
    seq = rows // PAIR

    def total(parts):
        gs[...] = sum([part[...].astype(F32) for part in parts[1:]], parts[0][...].astype(F32))

    if n_in in (1, QUART):
        total(ins)
    else:

        @pl.when(scal[2] != 0)
        def _():
            total(ins[:1])

        @pl.when(scal[2] == 0)
        def _():
            total(ins[1:])

    root = 1.0 / math.sqrt(HDIM)
    for s in range(PAIR):
        length = scal[3 + PAIR * micro + s]
        r = slice(s * seq, (s + 1) * seq)
        for h in range(chunk // HDIM):
            lo = h * HDIM
            c = slice(lo, lo + HDIM)
            gate = gates[slot, PAIR * micro + s, :, c]
            dmix = gs[r, c] * gate
            q, rq = unit(proj_ref[r, lo : lo + HDIM])
            key, rk = unit(proj_ref[r, chunk + lo : chunk + lo + HDIM])
            v = proj_ref[r, 2 * chunk + lo : 2 * chunk + lo + HDIM]
            att = weights_of(q, key, length)
            datt = nt(dmix, v)
            dscore = att * (datt - jnp.sum(att * datt, axis=-1, keepdims=True)) * root
            dqn = nn(dscore, key)
            dkn = tn(dscore, q)
            dp[r, c] = rq * (dqn - q * jnp.mean(dqn * q, axis=-1, keepdims=True))
            dp[r, chunk + lo : chunk + lo + HDIM] = rk * (
                dkn - key * jnp.mean(dkn * key, axis=-1, keepdims=True)
            )
            dp[r, 2 * chunk + lo : 2 * chunk + lo + HDIM] = tn(att, dmix)
    low = dp[...].astype(BF16)
    low_ref[...] = low
    low_save.start()
    if not send:
        low_save.wait()
        return
    hidden_load.wait()
    normal, scale = standardize(whole(hs))
    halves = wscr.shape[0]
    norm_grad = jnp.concatenate([nt(low, half_weights(wscr, sem, t)) for t in range(halves)], axis=1)
    norm_grad = norm_grad.reshape(PAIR, seq, width)
    grad = jnp.concatenate(
        [(1.0 + mods[slot, PAIR * micro + s, 1:2, :]) * norm_grad[s] for s in range(PAIR)], axis=0
    )
    back = scale * (
        grad
        - jnp.mean(grad, axis=-1, keepdims=True)
        - normal * jnp.mean(grad * normal, axis=-1, keepdims=True)
    )
    for t in range(QUART):
        ds[t] = back[:, t * chunk : (t + 1) * chunk]
    ds[y] = ds[y] + gs[...]
    for d in range(QUART):
        outs[d][...] = ds[lax.rem(y + d, QUART)].astype(BF16)
    low_save.wait()


def weight_grad_kernel(scal, n0, n1, n2, g0, g1, g2, near, far, nscr, gscr, held, sems):
    c = scal[1]
    rows = n0.shape[0]

    def start(normed, grad):
        pltpu.make_async_copy(normed, nscr.at[0:rows], sems.at[0]).start()
        pltpu.make_async_copy(grad, gscr.at[0:rows], sems.at[1]).start()

    pltpu.make_async_copy(n1, nscr.at[rows : 2 * rows], sems.at[2]).start()
    pltpu.make_async_copy(g1, gscr.at[rows : 2 * rows], sems.at[3]).start()

    @pl.when(scal[2] == 0)
    def _():
        start(n0, g0)

    @pl.when(scal[2] != 0)
    def _():
        start(n2, g2)

    pltpu.make_async_copy(n0, nscr.at[0:rows], sems.at[0]).wait()
    pltpu.make_async_copy(g0, gscr.at[0:rows], sems.at[1]).wait()
    pltpu.make_async_copy(n1, nscr.at[rows : 2 * rows], sems.at[2]).wait()
    pltpu.make_async_copy(g1, gscr.at[rows : 2 * rows], sems.at[3]).wait()
    share = near.shape[2]
    depth = near.shape[0]
    steps, cores, count = held.shape[:3]
    per = cores * count * share
    right = gscr[...]
    saves = []
    for t in range(steps):
        value = tn(nscr[:, t * per : (t + 1) * per], right).astype(BF16)
        half, z = divmod(t * count, depth)
        for core in range(cores):
            for u in range(count):
                at = (u * cores + core) * share
                held[t, core, u] = value[at : at + share]
            sem = sems.at[4 + t * cores + core]

            def save(out):
                return pltpu.make_async_copy(held.at[t, core], out.at[z : z + count, half], sem)

            @pl.when(c == core)
            def _():
                save(near).start()

            @pl.when(c != core)
            def _():
                save(far).start()

            saves.append(save(near))
    for save in saves:
        save.wait()


def assemble_kernel(scal, *refs):
    parts, (out, held) = refs[: 2 * QUART], refs[2 * QUART :]
    y = scal[0]
    chunk = out.shape[1] // (3 * QUART)
    for dy in range(QUART):
        total = parts[dy][...].astype(F32) + parts[QUART + dy][...].astype(F32)
        held[lax.rem(y + QUART - dy, QUART)] = total
    for q in range(QUART):
        for i in range(3):
            at = (i * QUART + q) * chunk
            out[:, at : at + chunk] = held[q][:, i * chunk : (i + 1) * chunk]


def shards(latents, out_grad, w_qkv, mod_table, timesteps, text_len):
    y = lax.axis_index("y")
    p = lax.rem(lax.axis_index("xl") + y, 2)
    half = lax.axis_index("xh")
    core = lax.axis_index("c")
    halves = lax.axis_size("xh")
    depth = lax.axis_size("z")
    cores = lax.axis_size("c")
    count, _, seq, width = latents.shape
    share = w_qkv.shape[1]
    chunk = width // QUART
    cols = 3 * chunk
    rows = PAIR * seq
    nj = BLOCKS // 2
    count_z = max(384 // (cores * share), 1)
    strips = width // (cores * count_z * share)
    levels = mod_table.shape[1]

    def swap(value, axis):
        return lax.ppermute(value, axis, [(0, 1), (1, 0)])

    fine = ("y", "xl")

    def route(dy, back, group):
        pairs = []
        for yy in range(QUART):
            to = (yy + dy) % QUART
            if group is not None and to // 2 != group:
                continue
            for xx in range(2):
                there = (xx + (yy if back else to)) % 2
                pairs.append((yy * 2 + xx, to * 2 + there))
        return pairs

    def pick(stack, index):
        return lax.dynamic_index_in_dim(stack, index, 0, keepdims=False)

    quarters = w_qkv[0].reshape(share, 3, QUART, chunk).transpose(2, 0, 1, 3)
    quarters = quarters.reshape(QUART, share, cols)
    leaves = [pick(quarters, lax.rem(y + dy, QUART)) for dy in range(QUART)]
    arrived = jnp.stack(
        [lax.ppermute(leaves[dy], fine, route(dy, False, None)) for dy in range(QUART)]
    )
    gathered = []
    for g in range(nj // 2):
        mine = jnp.stack(
            [pick(arrived, lax.rem(y + QUART - j, QUART)) for j in (2 * g, 2 * g + 1)]
        )
        if g > 0:
            mine, _ = lax.optimization_barrier((mine, part))
        if halves == 2:
            other = swap(mine, "xh")
            mine = [jnp.where(half == h, mine, other) for h in range(2)]
            part = jnp.stack(mine, axis=1)
        else:
            part = mine[:, None]
        gathered.append(lax.all_gather(part, "z", axis=0))

    onehot = (timesteps[:, 0][:, None] == jnp.arange(levels, dtype=jnp.int32)[None, :]).astype(F32)
    table, _ = lax.optimization_barrier((mod_table, arrived))
    modulations = jnp.dot(
        onehot, table[0].reshape(levels, 3 * width), precision=lax.Precision.HIGHEST
    ).reshape(count, 3, width)
    mods = jnp.stack(
        [lax.ppermute(modulations, fine, route(dy, False, None)) for dy in range(QUART)]
    )
    gates = lax.dynamic_slice_in_dim(mods[:, :, 2:3, :], y * chunk, chunk, axis=3)
    scal = jnp.concatenate(
        [jnp.stack([y, core, p]).astype(jnp.int32), text_len[:, 0].astype(jnp.int32)]
    )
    entering = latents.reshape(count // PAIR, rows, width)
    leaving = lax.dynamic_slice_in_dim(
        out_grad.reshape(count // PAIR, rows, width), y * chunk, chunk, axis=2
    )

    first, mods, gates, entering = lax.optimization_barrier((gathered[0], mods, gates, entering))
    pieces = [(first, swap(first, "c"))]
    routes = [
        [
            (yy * 2 + xx, ((yy + d) % QUART) * 2 + (1 + xx + d) % 2)
            for yy in range(QUART)
            for xx in range(2)
        ]
        for d in range(QUART)
    ]

    def send(parts):
        return [lax.ppermute(parts[d], ("y", "xl"), routes[d]) for d in range(QUART)]

    wscr = pltpu.VMEM((halves, depth, cores, share, cols), BF16)
    params = pltpu.CompilerParams(vmem_limit_bytes=VMEM_LIMIT)

    def held(k):
        first, second = min(k // 2, nj - 1), max((k - 1) // 2, 0)
        first, second = first // 2, second // 2
        if first == second:
            return pieces[first]
        return pieces[first] + pieces[second]

    def shape(cols, kind):
        return jax.ShapeDtypeStruct((rows, cols), kind)

    def kept(dims, kind):
        return pltpu.HBM(dims, kind)

    def pinned(values):
        return [pltpu.with_memory_space_constraint(value, pltpu.HBM) for value in values]

    steps = BLOCKS + 1
    saved = []
    received = None
    for k in range(steps):
        if k == 0:
            ins = [entering[0]]
        elif k == 1:
            ins = [entering[1]] + received
        else:
            ins = received
        weights = held(k)
        sending = k < steps - 1
        outs = [
            kept((QUART, rows, chunk), BF16),
            kept((rows, width), BF16),
            kept((rows, cols), F32),
        ]
        if sending:
            outs = [shape(chunk, BF16)] + outs
        result = pl.pallas_call(
            functools.partial(forward_kernel, k, len(ins), len(weights), sending),
            out_shape=outs,
            in_specs=[SM] + [VM] * (len(ins) + 2) + [HBM] * len(weights),
            out_specs=[VM] * sending + [HBM] * 3,
            scratch_shapes=[
                pltpu.VMEM((rows, width), BF16),
                pltpu.VMEM((rows, cols), F32),
                wscr,
                pltpu.VMEM((QUART, rows, chunk), BF16),
                pltpu.SemaphoreType.DMA((halves,)),
                pltpu.SemaphoreType.DMA((3,)),
            ],
            compiler_params=params,
            name="forward_step",
        )(scal, *ins, mods, gates, *pinned(weights))
        if sending:
            received = send([result[0]] * QUART)
            result = result[1:]
        if k == 3:
            second, _ = lax.optimization_barrier((gathered[1], result[1]))
            pieces.append((second, swap(second, "c")))
        saved.append(result)

    lows = [None] * steps
    chips = [None] * nj
    rings = [None] * (nj // 2)
    received = None
    for k in reversed(range(steps)):
        if k == steps - 1:
            ins = [leaving[1]]
        elif k == steps - 2:
            ins = [leaving[0]] + received
        else:
            ins = received
        weights = held(k)
        sending = k > 0
        outs = [shape(chunk, BF16)] * (QUART * sending) + [kept((rows, cols), BF16)]
        hidden, _, projected = saved[k]
        result = pl.pallas_call(
            functools.partial(backward_kernel, k, len(ins), len(weights), sending),
            out_shape=outs,
            in_specs=[SM] + [VM] * (len(ins) + 3) + [HBM] * (1 + len(weights)),
            out_specs=[VM] * (len(outs) - 1) + [HBM],
            scratch_shapes=[
                pltpu.VMEM((rows, cols), BF16),
                wscr,
                pltpu.VMEM((QUART, rows, chunk), BF16),
                pltpu.VMEM((rows, chunk), F32),
                pltpu.VMEM((rows, cols), F32),
                pltpu.VMEM((QUART, rows, chunk), F32),
                pltpu.SemaphoreType.DMA((halves,)),
                pltpu.SemaphoreType.DMA((3,)),
            ],
            compiler_params=params,
            name="backward_step",
        )(scal, *ins, mods, gates, projected, *pinned([hidden, *weights]))
        lows[k] = result[-1]
        if sending:
            received = send(result[:-1])
        if k % 2 == 0 and k < steps - 1:
            j = k // 2
            factors = [saved[k + i][1] for i in range(3)] + [lows[k + i] for i in range(3)]
            if sending:
                factors, received[0] = lax.optimization_barrier((factors, received[0]))
            partial = pl.pallas_call(
                weight_grad_kernel,
                out_shape=[kept((depth, halves, share, cols), BF16)] * cores,
                in_specs=[SM] + [HBM] * 6,
                out_specs=[HBM] * cores,
                scratch_shapes=[
                    pltpu.VMEM((2 * rows, width), BF16),
                    pltpu.VMEM((2 * rows, cols), BF16),
                    pltpu.VMEM((strips, cores, count_z, share, cols), BF16),
                    pltpu.SemaphoreType.DMA((4 + strips * cores,)),
                ],
                compiler_params=params,
                cost_estimate=pl.CostEstimate(
                    flops=4 * rows * width * cols,
                    bytes_accessed=4 * width * cols,
                    transcendentals=0,
                ),
                name="weight_grad",
            )(scal, *pinned(factors))
            if sending:
                partial, received[1] = lax.optimization_barrier((partial, received[1]))
            chips[j] = partial
        if k in (1, 3, 5):
            j = (k + 1) // 2
            chips[j], _ = lax.optimization_barrier((chips[j], lows[k]))
        if k in (0, 1, 3, 5):
            j = (k + 1) // 2
            chips[j] = (chips[j][0], swap(chips[j][1], "c"))
        if k == 4 and sending:
            keep, received[1] = lax.optimization_barrier((chips[3][1], received[1]))
            chips[3] = (chips[3][0], keep)
        if k in (0, 3):
            g = k // 3
            total = jnp.concatenate(
                [
                    (chips[i][0] + chips[i][1]).reshape(depth, halves * share, cols)
                    for i in (2 * g, 2 * g + 1)
                ],
                axis=1,
            )
            if sending:
                total, received[1] = lax.optimization_barrier((total, received[1]))
            else:
                total, rings[1] = lax.optimization_barrier((total, rings[1]))
            rings[g] = lax.psum_scatter(total, "z", scatter_dimension=0)

    def hand_back(g):
        ring = rings[g].reshape(2, halves, share, cols)
        ours = lax.dynamic_index_in_dim(ring, half, 1, keepdims=False)
        if halves == 2:
            theirs = swap(lax.dynamic_index_in_dim(ring, 1 - half, 1, keepdims=False), "xh")
            ours = (ours.astype(F32) + theirs.astype(F32)).astype(BF16)
        return [
            lax.ppermute(pick(ours, lax.rem(y + dy, 2)), fine, route(dy, True, g))
            for dy in range(QUART)
        ]

    upper = hand_back(1)
    rings[0], upper = lax.optimization_barrier((rings[0], upper))
    lower = hand_back(0)
    grads = pl.pallas_call(
        assemble_kernel,
        out_shape=jax.ShapeDtypeStruct((share, 3 * width), F32),
        in_specs=[SM] + [VM] * (2 * QUART),
        out_specs=VM,
        scratch_shapes=[pltpu.VMEM((QUART, share, cols), F32)],
        compiler_params=params,
        name="assemble",
    )(scal, *upper, *lower)
    return grads[None]


def solution(mesh):
    fine = Mesh(mesh.devices.reshape(4, 2, 2, 8, 2), ("y", "xl", "xh", "z", "c"))
    pipe = ("y", "xl")
    dp = ("xh", "z", "c")
    return jax.shard_map(
        shards,
        mesh=fine,
        in_specs=(
            P(None, dp, None, None),
            P(None, dp, None, None),
            P(pipe, dp, None),
            P(pipe, None, None, None),
            P(None, dp),
            P(None, dp),
        ),
        out_specs=P(pipe, dp, None),
        check_vma=False,
    )
```

```python
import functools
import math

import jax
import jax.numpy as jnp
from jax import lax
from jax.experimental import pallas as pl
from jax.experimental.pallas import tpu as pltpu
from jax.sharding import Mesh
from jax.sharding import PartitionSpec as P

IMG = 40
EPS = 1e-06
HDIM = 128
BLOCKS = 8
QUART = 4
PAIR = 2
F32 = jnp.float32
BF16 = jnp.bfloat16
VMEM_LIMIT = 16 * 1024 * 1024
VM = pl.BlockSpec(memory_space=pltpu.VMEM)
SM = pl.BlockSpec(memory_space=pltpu.SMEM)
HBM = pl.BlockSpec(memory_space=pltpu.HBM)


def place(scal, k):
    p = scal[2]
    j = lax.max((k - p + 2) // 2 - 1, 0)
    j = lax.min(j, BLOCKS // 2 - 1)
    return lax.rem(k + p, 2), j, lax.rem(scal[0] + QUART - j, QUART)


def fetch_weights(scal, j, pieces, wscr, sem):
    c = scal[1]
    halves = wscr.shape[0]
    inner = lax.rem(j, 2)

    def start(own, other):
        for t in range(halves):
            for z in range(wscr.shape[1]):
                for core, source in ((c, own), (1 - c, other)):
                    pltpu.make_async_copy(
                        source.at[z, inner, t], wscr.at[t, z, core], sem.at[t]
                    ).start()

    if len(pieces) == 2:
        start(*pieces)
    else:

        @pl.when(scal[2] == 0)
        def _():
            start(*pieces[:2])

        @pl.when(scal[2] != 0)
        def _():
            start(*pieces[2:])


def half_weights(wscr, sem, t):
    pltpu.make_async_copy(wscr.at[t], wscr.at[t], sem.at[t]).wait()
    value = wscr[t]
    return value.reshape(value.shape[0] * value.shape[1] * value.shape[2], value.shape[3])


def standardize(hidden):
    average = jnp.mean(hidden, axis=-1, keepdims=True)
    centered = hidden - average
    variance = jnp.mean(centered * centered, axis=-1, keepdims=True)
    scale = lax.rsqrt(variance + EPS)
    return centered * scale, scale


def nt(a, b):
    return lax.dot_general(
        a.astype(BF16), b.astype(BF16), (((1,), (1,)), ((), ())), preferred_element_type=F32
    )


def nn(a, b):
    return lax.dot_general(
        a.astype(BF16), b.astype(BF16), (((1,), (0,)), ((), ())), preferred_element_type=F32
    )


def tn(a, b):
    return lax.dot_general(
        a.astype(BF16), b.astype(BF16), (((0,), (0,)), ((), ())), preferred_element_type=F32
    )


def unit(rows):
    scale = lax.rsqrt(jnp.mean(rows * rows, axis=-1, keepdims=True) + EPS)
    return rows * scale, scale


def weights_of(q, k, length):
    scores = nt(q, k) * (1.0 / math.sqrt(HDIM))
    position = lax.broadcasted_iota(jnp.int32, scores.shape, 1)
    usable = (position < IMG) | (position - IMG < length)
    weights = jnp.where(usable, jnp.exp(scores), 0.0)
    return weights / jnp.sum(weights, axis=-1, keepdims=True)


def load_hidden(scal, ins, hs):
    y = scal[0]
    chunk = hs.shape[2]

    def from_whole(ref):
        for t in range(QUART):
            hs[t] = ref[:, t * chunk : (t + 1) * chunk]

    def from_chunks(parts):
        for d in range(QUART):
            hs[lax.rem(y + QUART - d, QUART)] = parts[d][...]

    if len(ins) == 1:
        from_whole(ins[0])
    elif len(ins) == QUART:
        from_chunks(ins)
    else:

        @pl.when(scal[2] == 0)
        def _():
            from_whole(ins[0])

        @pl.when(scal[2] != 0)
        def _():
            from_chunks(ins[1:])


def whole(hs):
    return jnp.concatenate([hs[t].astype(F32) for t in range(QUART)], axis=1)


def forward_kernel(k, n_in, n_w, send, scal, *refs):
    ins, refs = refs[:n_in], refs[n_in:]
    mods, gates = refs[:2]
    pieces, refs = refs[2 : 2 + n_w], refs[2 + n_w :]
    if send:
        out_ref, refs = refs[0], refs[1:]
    hidden_out, normed_out, proj_out, normed_ref, proj_ref, wscr, hs, sem, sems = refs
    hidden_save = pltpu.make_async_copy(hs, hidden_out, sems.at[2])
    normed_save = pltpu.make_async_copy(normed_ref, normed_out, sems.at[0])
    proj_save = pltpu.make_async_copy(proj_ref, proj_out, sems.at[1])
    y = scal[0]
    micro, j, slot = place(scal, k)
    fetch_weights(scal, j, pieces, wscr, sem)
    chunk = hs.shape[2]
    rows, width = normed_ref.shape
    seq = rows // PAIR
    load_hidden(scal, ins, hs)
    hidden_save.start()
    normal, _ = standardize(whole(hs))
    normal = normal.reshape(PAIR, seq, width)
    normed = jnp.concatenate(
        [
            (1.0 + mods[slot, PAIR * micro + s, 1:2, :]) * normal[s]
            + mods[slot, PAIR * micro + s, 0:1, :]
            for s in range(PAIR)
        ],
        axis=0,
    ).astype(BF16)
    normed_ref[...] = normed
    normed_save.start()
    halves = wscr.shape[0]
    span = width // halves
    projected = nn(normed[:, :span], half_weights(wscr, sem, 0))
    for t in range(1, halves):
        projected += nn(normed[:, t * span : (t + 1) * span], half_weights(wscr, sem, t))
    proj_ref[...] = projected
    proj_save.start()
    if not send:
        normed_save.wait()
        hidden_save.wait()
        proj_save.wait()
        return
    own = hs[y].astype(F32)
    for s in range(PAIR):
        length = scal[3 + PAIR * micro + s]
        r = slice(s * seq, (s + 1) * seq)
        mixed = []
        for h in range(chunk // HDIM):
            lo = h * HDIM
            q, _ = unit(proj_ref[r, lo : lo + HDIM])
            key, _ = unit(proj_ref[r, chunk + lo : chunk + lo + HDIM])
            v = proj_ref[r, 2 * chunk + lo : 2 * chunk + lo + HDIM]
            mixed.append(nn(weights_of(q, key, length), v))
        mixture = jnp.concatenate(mixed, axis=1)
        gate = gates[slot, PAIR * micro + s]
        hs_rows = own[r] + gate * mixture
        if s == 0:
            first = hs_rows
    out_ref[...] = jnp.concatenate([first, hs_rows], axis=0).astype(BF16)
    normed_save.wait()
    hidden_save.wait()
    proj_save.wait()


def backward_kernel(k, n_in, n_w, send, scal, *refs):
    ins, refs = refs[:n_in], refs[n_in:]
    mods, gates, proj_ref, hidden = refs[:4]
    pieces, refs = refs[4 : 4 + n_w], refs[4 + n_w :]
    outs, refs = refs[: QUART * send], refs[QUART * send :]
    low_out, low_ref, wscr, hs, gs, dp, ds, sem, sems = refs
    low_save = pltpu.make_async_copy(low_ref, low_out, sems.at[0])
    y = scal[0]
    micro, j, slot = place(scal, k)
    if send:
        hidden_load = pltpu.make_async_copy(hidden, hs, sems.at[2])
        hidden_load.start()
        fetch_weights(scal, j, pieces, wscr, sem)
    rows, chunk = gs.shape
    width = chunk * QUART
    seq = rows // PAIR

    def total(parts):
        gs[...] = sum([part[...].astype(F32) for part in parts[1:]], parts[0][...].astype(F32))

    if n_in in (1, QUART):
        total(ins)
    else:

        @pl.when(scal[2] != 0)
        def _():
            total(ins[:1])

        @pl.when(scal[2] == 0)
        def _():
            total(ins[1:])

    root = 1.0 / math.sqrt(HDIM)
    for s in range(PAIR):
        length = scal[3 + PAIR * micro + s]
        r = slice(s * seq, (s + 1) * seq)
        for h in range(chunk // HDIM):
            lo = h * HDIM
            c = slice(lo, lo + HDIM)
            gate = gates[slot, PAIR * micro + s, :, c]
            dmix = gs[r, c] * gate
            q, rq = unit(proj_ref[r, lo : lo + HDIM])
            key, rk = unit(proj_ref[r, chunk + lo : chunk + lo + HDIM])
            v = proj_ref[r, 2 * chunk + lo : 2 * chunk + lo + HDIM]
            att = weights_of(q, key, length)
            datt = nt(dmix, v)
            dscore = att * (datt - jnp.sum(att * datt, axis=-1, keepdims=True)) * root
            dqn = nn(dscore, key)
            dkn = tn(dscore, q)
            dp[r, c] = rq * (dqn - q * jnp.mean(dqn * q, axis=-1, keepdims=True))
            dp[r, chunk + lo : chunk + lo + HDIM] = rk * (
                dkn - key * jnp.mean(dkn * key, axis=-1, keepdims=True)
            )
            dp[r, 2 * chunk + lo : 2 * chunk + lo + HDIM] = tn(att, dmix)
    low = dp[...].astype(BF16)
    low_ref[...] = low
    low_save.start()
    if not send:
        low_save.wait()
        return
    hidden_load.wait()
    normal, scale = standardize(whole(hs))
    halves = wscr.shape[0]
    norm_grad = jnp.concatenate([nt(low, half_weights(wscr, sem, t)) for t in range(halves)], axis=1)
    norm_grad = norm_grad.reshape(PAIR, seq, width)
    grad = jnp.concatenate(
        [(1.0 + mods[slot, PAIR * micro + s, 1:2, :]) * norm_grad[s] for s in range(PAIR)], axis=0
    )
    back = scale * (
        grad
        - jnp.mean(grad, axis=-1, keepdims=True)
        - normal * jnp.mean(grad * normal, axis=-1, keepdims=True)
    )
    for t in range(QUART):
        ds[t] = back[:, t * chunk : (t + 1) * chunk]
    ds[y] = ds[y] + gs[...]
    for d in range(QUART):
        outs[d][...] = ds[lax.rem(y + d, QUART)].astype(BF16)
    low_save.wait()


def weight_grad_kernel(scal, n0, n1, n2, g0, g1, g2, near, far, nscr, gscr, held, sems):
    c = scal[1]
    rows = n0.shape[0]

    def start(normed, grad):
        pltpu.make_async_copy(normed, nscr.at[0:rows], sems.at[0]).start()
        pltpu.make_async_copy(grad, gscr.at[0:rows], sems.at[1]).start()

    pltpu.make_async_copy(n1, nscr.at[rows : 2 * rows], sems.at[2]).start()
    pltpu.make_async_copy(g1, gscr.at[rows : 2 * rows], sems.at[3]).start()

    @pl.when(scal[2] == 0)
    def _():
        start(n0, g0)

    @pl.when(scal[2] != 0)
    def _():
        start(n2, g2)

    pltpu.make_async_copy(n0, nscr.at[0:rows], sems.at[0]).wait()
    pltpu.make_async_copy(g0, gscr.at[0:rows], sems.at[1]).wait()
    pltpu.make_async_copy(n1, nscr.at[rows : 2 * rows], sems.at[2]).wait()
    pltpu.make_async_copy(g1, gscr.at[rows : 2 * rows], sems.at[3]).wait()
    share = near.shape[2]
    depth = near.shape[0]
    steps, cores, count = held.shape[:3]
    per = cores * count * share
    right = gscr[...]
    saves = []
    for t in range(steps):
        value = tn(nscr[:, t * per : (t + 1) * per], right).astype(BF16)
        half, z = divmod(t * count, depth)
        for core in range(cores):
            for u in range(count):
                at = (u * cores + core) * share
                held[t, core, u] = value[at : at + share]
            sem = sems.at[4 + t * cores + core]

            def save(out):
                return pltpu.make_async_copy(held.at[t, core], out.at[z : z + count, half], sem)

            @pl.when(c == core)
            def _():
                save(near).start()

            @pl.when(c != core)
            def _():
                save(far).start()

            saves.append(save(near))
    for save in saves:
        save.wait()


def assemble_kernel(scal, *refs):
    parts, (out, held) = refs[: 2 * QUART], refs[2 * QUART :]
    y = scal[0]
    chunk = out.shape[1] // (3 * QUART)
    for dy in range(QUART):
        total = parts[dy][...].astype(F32) + parts[QUART + dy][...].astype(F32)
        held[lax.rem(y + QUART - dy, QUART)] = total
    for q in range(QUART):
        for i in range(3):
            at = (i * QUART + q) * chunk
            out[:, at : at + chunk] = held[q][:, i * chunk : (i + 1) * chunk]


def shards(latents, out_grad, w_qkv, mod_table, timesteps, text_len):
    y = lax.axis_index("y")
    p = lax.rem(lax.axis_index("xl") + y, 2)
    half = lax.axis_index("xh")
    core = lax.axis_index("c")
    halves = lax.axis_size("xh")
    depth = lax.axis_size("z")
    cores = lax.axis_size("c")
    count, _, seq, width = latents.shape
    share = w_qkv.shape[1]
    chunk = width // QUART
    cols = 3 * chunk
    rows = PAIR * seq
    nj = BLOCKS // 2
    count_z = max(384 // (cores * share), 1)
    strips = width // (cores * count_z * share)
    levels = mod_table.shape[1]

    def swap(value, axis):
        return lax.ppermute(value, axis, [(0, 1), (1, 0)])

    fine = ("y", "xl")

    def route(dy, back, group):
        pairs = []
        for yy in range(QUART):
            to = (yy + dy) % QUART
            if group is not None and to // 2 != group:
                continue
            for xx in range(2):
                there = (xx + (yy if back else to)) % 2
                pairs.append((yy * 2 + xx, to * 2 + there))
        return pairs

    def pick(stack, index):
        return lax.dynamic_index_in_dim(stack, index, 0, keepdims=False)

    quarters = w_qkv[0].reshape(share, 3, QUART, chunk).transpose(2, 0, 1, 3)
    quarters = quarters.reshape(QUART, share, cols)
    leaves = [pick(quarters, lax.rem(y + dy, QUART)) for dy in range(QUART)]
    arrived = jnp.stack(
        [lax.ppermute(leaves[dy], fine, route(dy, False, None)) for dy in range(QUART)]
    )
    gathered = []
    for g in range(nj // 2):
        mine = jnp.stack(
            [pick(arrived, lax.rem(y + QUART - j, QUART)) for j in (2 * g, 2 * g + 1)]
        )
        if g > 0:
            mine, _ = lax.optimization_barrier((mine, part))
        if halves == 2:
            other = swap(mine, "xh")
            mine = [jnp.where(half == h, mine, other) for h in range(2)]
            part = jnp.stack(mine, axis=1)
        else:
            part = mine[:, None]
        gathered.append(lax.all_gather(part, "z", axis=0))

    onehot = (timesteps[:, 0][:, None] == jnp.arange(levels, dtype=jnp.int32)[None, :]).astype(F32)
    table, _ = lax.optimization_barrier((mod_table, arrived))
    modulations = jnp.dot(
        onehot, table[0].reshape(levels, 3 * width), precision=lax.Precision.HIGHEST
    ).reshape(count, 3, width)
    mods = jnp.stack(
        [lax.ppermute(modulations, fine, route(dy, False, None)) for dy in range(QUART)]
    )
    gates = lax.dynamic_slice_in_dim(mods[:, :, 2:3, :], y * chunk, chunk, axis=3)
    scal = jnp.concatenate(
        [jnp.stack([y, core, p]).astype(jnp.int32), text_len[:, 0].astype(jnp.int32)]
    )
    entering = latents.reshape(count // PAIR, rows, width)
    leaving = lax.dynamic_slice_in_dim(
        out_grad.reshape(count // PAIR, rows, width), y * chunk, chunk, axis=2
    )

    first, mods, gates, entering = lax.optimization_barrier((gathered[0], mods, gates, entering))
    pieces = [(first, swap(first, "c"))]
    routes = [
        [
            (yy * 2 + xx, ((yy + d) % QUART) * 2 + (1 + xx + d) % 2)
            for yy in range(QUART)
            for xx in range(2)
        ]
        for d in range(QUART)
    ]

    def send(parts):
        return [lax.ppermute(parts[d], ("y", "xl"), routes[d]) for d in range(QUART)]

    wscr = pltpu.VMEM((halves, depth, cores, share, cols), BF16)
    params = pltpu.CompilerParams(vmem_limit_bytes=VMEM_LIMIT)

    def held(k):
        first, second = min(k // 2, nj - 1), max((k - 1) // 2, 0)
        first, second = first // 2, second // 2
        if first == second:
            return pieces[first]
        return pieces[first] + pieces[second]

    def shape(cols, kind):
        return jax.ShapeDtypeStruct((rows, cols), kind)

    def kept(dims, kind):
        return pltpu.HBM(dims, kind)

    def pinned(values):
        return [pltpu.with_memory_space_constraint(value, pltpu.HBM) for value in values]

    steps = BLOCKS + 1
    saved = []
    received = None
    for k in range(steps):
        if k == 0:
            ins = [entering[0]]
        elif k == 1:
            ins = [entering[1]] + received
        else:
            ins = received
        weights = held(k)
        sending = k < steps - 1
        outs = [
            kept((QUART, rows, chunk), BF16),
            kept((rows, width), BF16),
            kept((rows, cols), F32),
        ]
        if sending:
            outs = [shape(chunk, BF16)] + outs
        result = pl.pallas_call(
            functools.partial(forward_kernel, k, len(ins), len(weights), sending),
            out_shape=outs,
            in_specs=[SM] + [VM] * (len(ins) + 2) + [HBM] * len(weights),
            out_specs=[VM] * sending + [HBM] * 3,
            scratch_shapes=[
                pltpu.VMEM((rows, width), BF16),
                pltpu.VMEM((rows, cols), F32),
                wscr,
                pltpu.VMEM((QUART, rows, chunk), BF16),
                pltpu.SemaphoreType.DMA((halves,)),
                pltpu.SemaphoreType.DMA((3,)),
            ],
            compiler_params=params,
            name="forward_step",
        )(scal, *ins, mods, gates, *pinned(weights))
        if sending:
            received = send([result[0]] * QUART)
            result = result[1:]
        if k == 3:
            second, _ = lax.optimization_barrier((gathered[1], result[1]))
            pieces.append((second, swap(second, "c")))
        saved.append(result)

    lows = [None] * steps
    chips = [None] * nj
    rings = [None] * (nj // 2)
    received = None
    for k in reversed(range(steps)):
        if k == steps - 1:
            ins = [leaving[1]]
        elif k == steps - 2:
            ins = [leaving[0]] + received
        else:
            ins = received
        weights = held(k)
        sending = k > 0
        outs = [shape(chunk, BF16)] * (QUART * sending) + [kept((rows, cols), BF16)]
        hidden, _, projected = saved[k]
        result = pl.pallas_call(
            functools.partial(backward_kernel, k, len(ins), len(weights), sending),
            out_shape=outs,
            in_specs=[SM] + [VM] * (len(ins) + 3) + [HBM] * (1 + len(weights)),
            out_specs=[VM] * (len(outs) - 1) + [HBM],
            scratch_shapes=[
                pltpu.VMEM((rows, cols), BF16),
                wscr,
                pltpu.VMEM((QUART, rows, chunk), BF16),
                pltpu.VMEM((rows, chunk), F32),
                pltpu.VMEM((rows, cols), F32),
                pltpu.VMEM((QUART, rows, chunk), F32),
                pltpu.SemaphoreType.DMA((halves,)),
                pltpu.SemaphoreType.DMA((3,)),
            ],
            compiler_params=params,
            name="backward_step",
        )(scal, *ins, mods, gates, projected, *pinned([hidden, *weights]))
        lows[k] = result[-1]
        if sending:
            received = send(result[:-1])
        if k % 2 == 0 and k < steps - 1:
            j = k // 2
            factors = [saved[k + i][1] for i in range(3)] + [lows[k + i] for i in range(3)]
            if sending:
                factors, received[0] = lax.optimization_barrier((factors, received[0]))
            partial = pl.pallas_call(
                weight_grad_kernel,
                out_shape=[kept((depth, halves, share, cols), BF16)] * cores,
                in_specs=[SM] + [HBM] * 6,
                out_specs=[HBM] * cores,
                scratch_shapes=[
                    pltpu.VMEM((2 * rows, width), BF16),
                    pltpu.VMEM((2 * rows, cols), BF16),
                    pltpu.VMEM((strips, cores, count_z, share, cols), BF16),
                    pltpu.SemaphoreType.DMA((4 + strips * cores,)),
                ],
                compiler_params=params,
                cost_estimate=pl.CostEstimate(
                    flops=4 * rows * width * cols,
                    bytes_accessed=4 * width * cols,
                    transcendentals=0,
                ),
                name="weight_grad",
            )(scal, *pinned(factors))
            if sending:
                partial, received[1] = lax.optimization_barrier((partial, received[1]))
            chips[j] = partial
        if k in (1, 3, 5):
            j = (k + 1) // 2
            chips[j], _ = lax.optimization_barrier((chips[j], lows[k]))
        if k in (0, 1, 3, 5):
            j = (k + 1) // 2
            chips[j] = (chips[j][0], swap(chips[j][1], "c"))
        if k == 4 and sending:
            keep, received[1] = lax.optimization_barrier((chips[3][1], received[1]))
            chips[3] = (chips[3][0], keep)
        if k in (0, 3):
            g = k // 3
            total = jnp.concatenate(
                [
                    (chips[i][0] + chips[i][1]).reshape(depth, halves * share, cols)
                    for i in (2 * g, 2 * g + 1)
                ],
                axis=1,
            )
            if sending:
                total, received[1] = lax.optimization_barrier((total, received[1]))
            else:
                total, rings[1] = lax.optimization_barrier((total, rings[1]))
            rings[g] = lax.psum_scatter(total, "z", scatter_dimension=0)

    def hand_back(g):
        ring = rings[g].reshape(2, halves, share, cols)
        ours = lax.dynamic_index_in_dim(ring, half, 1, keepdims=False)
        if halves == 2:
            theirs = swap(lax.dynamic_index_in_dim(ring, 1 - half, 1, keepdims=False), "xh")
            ours = (ours.astype(F32) + theirs.astype(F32)).astype(BF16)
        return [
            lax.ppermute(pick(ours, lax.rem(y + dy, 2)), fine, route(dy, True, g))
            for dy in range(QUART)
        ]

    upper = hand_back(1)
    rings[0], upper = lax.optimization_barrier((rings[0], upper))
    lower = hand_back(0)
    grads = pl.pallas_call(
        assemble_kernel,
        out_shape=jax.ShapeDtypeStruct((share, 3 * width), F32),
        in_specs=[SM] + [VM] * (2 * QUART),
        out_specs=VM,
        scratch_shapes=[pltpu.VMEM((QUART, share, cols), F32)],
        compiler_params=params,
        name="assemble",
    )(scal, *upper, *lower)
    return grads[None]


def solution(mesh):
    fine = Mesh(mesh.devices.reshape(4, 2, 2, 8, 2), ("y", "xl", "xh", "z", "c"))
    pipe = ("y", "xl")
    dp = ("xh", "z", "c")
    return jax.shard_map(
        shards,
        mesh=fine,
        in_specs=(
            P(None, dp, None, None),
            P(None, dp, None, None),
            P(pipe, dp, None),
            P(pipe, None, None, None),
            P(None, dp),
            P(None, dp),
        ),
        out_specs=P(pipe, dp, None),
        check_vma=False,
    )
```

```python
import functools
import math

import jax
import jax.numpy as jnp
from jax import lax
from jax.experimental import pallas as pl
from jax.experimental.pallas import tpu as pltpu
from jax.sharding import Mesh
from jax.sharding import PartitionSpec as P

IMG = 40
EPS = 1e-06
HDIM = 128
BLOCKS = 8
QUART = 4
PAIR = 2
F32 = jnp.float32
BF16 = jnp.bfloat16
VMEM_LIMIT = 16 * 1024 * 1024
VM = pl.BlockSpec(memory_space=pltpu.VMEM)
SM = pl.BlockSpec(memory_space=pltpu.SMEM)
HBM = pl.BlockSpec(memory_space=pltpu.HBM)


def place(scal, k):
    p = scal[2]
    j = lax.max((k - p + 2) // 2 - 1, 0)
    j = lax.min(j, BLOCKS // 2 - 1)
    return lax.rem(k + p, 2), j, lax.rem(scal[0] + QUART - j, QUART)


def fetch_weights(scal, j, pieces, wscr, sem):
    c = scal[1]
    halves = wscr.shape[0]
    inner = lax.rem(j, 2)

    def start(own, other):
        for t in range(halves):
            pltpu.make_async_copy(own.at[:, inner, t], wscr.at[t, :, c], sem.at[t]).start()
            pltpu.make_async_copy(other.at[:, inner, t], wscr.at[t, :, 1 - c], sem.at[t]).start()

    if len(pieces) == 2:
        start(*pieces)
    else:

        @pl.when(scal[2] == 0)
        def _():
            start(*pieces[:2])

        @pl.when(scal[2] != 0)
        def _():
            start(*pieces[2:])


def half_weights(wscr, sem, t):
    if sem is not None:
        pltpu.make_async_copy(wscr.at[t], wscr.at[t], sem.at[t]).wait()
    value = wscr[t]
    return value.reshape(value.shape[0] * value.shape[1] * value.shape[2], value.shape[3])


def standardize(hidden):
    average = jnp.mean(hidden, axis=-1, keepdims=True)
    centered = hidden - average
    variance = jnp.mean(centered * centered, axis=-1, keepdims=True)
    scale = lax.rsqrt(variance + EPS)
    return centered * scale, scale


def nt(a, b):
    return lax.dot_general(
        a.astype(BF16), b.astype(BF16), (((1,), (1,)), ((), ())), preferred_element_type=F32
    )


def nn(a, b):
    return lax.dot_general(
        a.astype(BF16), b.astype(BF16), (((1,), (0,)), ((), ())), preferred_element_type=F32
    )


def tn(a, b):
    return lax.dot_general(
        a.astype(BF16), b.astype(BF16), (((0,), (0,)), ((), ())), preferred_element_type=F32
    )


def unit(rows):
    scale = lax.rsqrt(jnp.mean(rows * rows, axis=-1, keepdims=True) + EPS)
    return rows * scale, scale


def weights_of(q, k, length):
    scores = nt(q, k) * (1.0 / math.sqrt(HDIM))
    position = lax.broadcasted_iota(jnp.int32, scores.shape, 1)
    usable = (position < IMG) | (position - IMG < length)
    weights = jnp.where(usable, jnp.exp(scores), 0.0)
    return weights / jnp.sum(weights, axis=-1, keepdims=True)


def load_hidden(scal, ins, hs):
    y = scal[0]
    chunk = hs.shape[2]

    def from_whole(ref):
        for t in range(QUART):
            hs[t] = ref[:, t * chunk : (t + 1) * chunk]

    def from_chunks(parts):
        for d in range(QUART):
            hs[lax.rem(y + QUART - d, QUART)] = parts[d][...]

    if len(ins) == 1:
        from_whole(ins[0])
    elif len(ins) == QUART:
        from_chunks(ins)
    else:

        @pl.when(scal[2] == 0)
        def _():
            from_whole(ins[0])

        @pl.when(scal[2] != 0)
        def _():
            from_chunks(ins[1:])


def whole(hs):
    return jnp.concatenate([hs[t].astype(F32) for t in range(QUART)], axis=1)


def load_kernel(k, scal, *refs):
    pieces, (out, sem) = refs[:-2], refs[-2:]
    fetch_weights(scal, place(scal, k)[1], pieces, out, sem)
    for t in range(out.shape[0]):
        pltpu.make_async_copy(out.at[t], out.at[t], sem.at[t]).wait()


def forward_kernel(k, n_in, n_w, loaded, send, scal, *refs):
    ins, refs = refs[:n_in], refs[n_in:]
    mods, gates = refs[:2]
    pieces, refs = refs[2 : 2 + n_w], refs[2 + n_w :]
    if send:
        out_ref, refs = refs[0], refs[1:]
    hidden_out, normed_out, proj_out, normed_ref, proj_ref, hs, sems = refs[:7]
    wscr, sem = (pieces[0], None) if loaded else refs[7:]
    hidden_save = pltpu.make_async_copy(hs, hidden_out, sems.at[2])
    normed_save = pltpu.make_async_copy(normed_ref, normed_out, sems.at[0])
    proj_save = pltpu.make_async_copy(proj_ref, proj_out, sems.at[1])
    y = scal[0]
    micro, j, slot = place(scal, k)
    if not loaded:
        fetch_weights(scal, j, pieces, wscr, sem)
    chunk = hs.shape[2]
    rows, width = normed_ref.shape
    seq = rows // PAIR
    load_hidden(scal, ins, hs)
    hidden_save.start()
    normal, _ = standardize(whole(hs))
    normal = normal.reshape(PAIR, seq, width)
    normed = jnp.concatenate(
        [
            (1.0 + mods[slot, PAIR * micro + s, 1:2, :]) * normal[s]
            + mods[slot, PAIR * micro + s, 0:1, :]
            for s in range(PAIR)
        ],
        axis=0,
    ).astype(BF16)
    normed_ref[...] = normed
    normed_save.start()
    halves = wscr.shape[0]
    span = width // halves
    projected = nn(normed[:, :span], half_weights(wscr, sem, 0))
    for t in range(1, halves):
        projected += nn(normed[:, t * span : (t + 1) * span], half_weights(wscr, sem, t))
    proj_ref[...] = projected
    proj_save.start()
    if not send:
        normed_save.wait()
        hidden_save.wait()
        proj_save.wait()
        return
    own = hs[y].astype(F32)
    for s in range(PAIR):
        length = scal[3 + PAIR * micro + s]
        r = slice(s * seq, (s + 1) * seq)
        mixed = []
        for h in range(chunk // HDIM):
            lo = h * HDIM
            q, _ = unit(proj_ref[r, lo : lo + HDIM])
            key, _ = unit(proj_ref[r, chunk + lo : chunk + lo + HDIM])
            v = proj_ref[r, 2 * chunk + lo : 2 * chunk + lo + HDIM]
            mixed.append(nn(weights_of(q, key, length), v))
        mixture = jnp.concatenate(mixed, axis=1)
        gate = gates[slot, PAIR * micro + s]
        hs_rows = own[r] + gate * mixture
        if s == 0:
            first = hs_rows
    out_ref[...] = jnp.concatenate([first, hs_rows], axis=0).astype(BF16)
    normed_save.wait()
    hidden_save.wait()
    proj_save.wait()


def backward_kernel(k, n_in, n_w, send, scal, *refs):
    ins, refs = refs[:n_in], refs[n_in:]
    mods, gates, proj_ref, hidden = refs[:4]
    pieces, refs = refs[4 : 4 + n_w], refs[4 + n_w :]
    outs, refs = refs[: QUART * send], refs[QUART * send :]
    low_out, low_ref, wscr, hs, gs, dp, ds, sem, sems = refs
    low_save = pltpu.make_async_copy(low_ref, low_out, sems.at[0])
    y = scal[0]
    micro, j, slot = place(scal, k)
    if send:
        hidden_load = pltpu.make_async_copy(hidden, hs, sems.at[2])
        hidden_load.start()
        fetch_weights(scal, j, pieces, wscr, sem)
    rows, chunk = gs.shape
    width = chunk * QUART
    seq = rows // PAIR

    def total(parts):
        gs[...] = sum([part[...].astype(F32) for part in parts[1:]], parts[0][...].astype(F32))

    if n_in in (1, QUART):
        total(ins)
    else:

        @pl.when(scal[2] != 0)
        def _():
            total(ins[:1])

        @pl.when(scal[2] == 0)
        def _():
            total(ins[1:])

    root = 1.0 / math.sqrt(HDIM)
    for s in range(PAIR):
        length = scal[3 + PAIR * micro + s]
        r = slice(s * seq, (s + 1) * seq)
        for h in range(chunk // HDIM):
            lo = h * HDIM
            c = slice(lo, lo + HDIM)
            gate = gates[slot, PAIR * micro + s, :, c]
            dmix = gs[r, c] * gate
            q, rq = unit(proj_ref[r, lo : lo + HDIM])
            key, rk = unit(proj_ref[r, chunk + lo : chunk + lo + HDIM])
            v = proj_ref[r, 2 * chunk + lo : 2 * chunk + lo + HDIM]
            att = weights_of(q, key, length)
            datt = nt(dmix, v)
            dscore = att * (datt - jnp.sum(att * datt, axis=-1, keepdims=True)) * root
            dqn = nn(dscore, key)
            dkn = tn(dscore, q)
            dp[r, c] = rq * (dqn - q * jnp.mean(dqn * q, axis=-1, keepdims=True))
            dp[r, chunk + lo : chunk + lo + HDIM] = rk * (
                dkn - key * jnp.mean(dkn * key, axis=-1, keepdims=True)
            )
            dp[r, 2 * chunk + lo : 2 * chunk + lo + HDIM] = tn(att, dmix)
    low = dp[...].astype(BF16)
    low_ref[...] = low
    low_save.start()
    if not send:
        low_save.wait()
        return
    hidden_load.wait()
    normal, scale = standardize(whole(hs))
    halves = wscr.shape[0]
    norm_grad = jnp.concatenate([nt(low, half_weights(wscr, sem, t)) for t in range(halves)], axis=1)
    norm_grad = norm_grad.reshape(PAIR, seq, width)
    grad = jnp.concatenate(
        [(1.0 + mods[slot, PAIR * micro + s, 1:2, :]) * norm_grad[s] for s in range(PAIR)], axis=0
    )
    back = scale * (
        grad
        - jnp.mean(grad, axis=-1, keepdims=True)
        - normal * jnp.mean(grad * normal, axis=-1, keepdims=True)
    )
    for t in range(QUART):
        ds[t] = back[:, t * chunk : (t + 1) * chunk]
    ds[y] = ds[y] + gs[...]
    for d in range(QUART):
        outs[d][...] = ds[lax.rem(y + d, QUART)].astype(BF16)
    low_save.wait()


def weight_grad_kernel(scal, n0, n1, n2, g0, g1, g2, near, far, nscr, gscr, held, sems):
    c = scal[1]
    rows = n0.shape[0]

    def start(normed, grad):
        pltpu.make_async_copy(normed, nscr.at[0:rows], sems.at[0]).start()
        pltpu.make_async_copy(grad, gscr.at[0:rows], sems.at[1]).start()

    pltpu.make_async_copy(n1, nscr.at[rows : 2 * rows], sems.at[2]).start()
    pltpu.make_async_copy(g1, gscr.at[rows : 2 * rows], sems.at[3]).start()

    @pl.when(scal[2] == 0)
    def _():
        start(n0, g0)

    @pl.when(scal[2] != 0)
    def _():
        start(n2, g2)

    pltpu.make_async_copy(n0, nscr.at[0:rows], sems.at[0]).wait()
    pltpu.make_async_copy(g0, gscr.at[0:rows], sems.at[1]).wait()
    pltpu.make_async_copy(n1, nscr.at[rows : 2 * rows], sems.at[2]).wait()
    pltpu.make_async_copy(g1, gscr.at[rows : 2 * rows], sems.at[3]).wait()
    share = near.shape[2]
    depth = near.shape[0]
    steps, cores, count = held.shape[:3]
    per = cores * count * share
    right = gscr[...]
    saves = []
    for t in range(steps):
        value = tn(nscr[:, t * per : (t + 1) * per], right).astype(BF16)
        half, z = divmod(t * count, depth)
        for core in range(cores):
            for u in range(count):
                at = (u * cores + core) * share
                held[t, core, u] = value[at : at + share]
            sem = sems.at[4 + t * cores + core]

            def save(out):
                return pltpu.make_async_copy(held.at[t, core], out.at[z : z + count, half], sem)

            @pl.when(c == core)
            def _():
                save(near).start()

            @pl.when(c != core)
            def _():
                save(far).start()

            saves.append(save(near))
    for save in saves:
        save.wait()


def assemble_kernel(scal, *refs):
    parts, (out, held) = refs[: 2 * QUART], refs[2 * QUART :]
    y = scal[0]
    chunk = out.shape[1] // (3 * QUART)
    for dy in range(QUART):
        total = parts[dy][...].astype(F32) + parts[QUART + dy][...].astype(F32)
        held[lax.rem(y + QUART - dy, QUART)] = total
    for q in range(QUART):
        for i in range(3):
            at = (i * QUART + q) * chunk
            out[:, at : at + chunk] = held[q][:, i * chunk : (i + 1) * chunk]


def shards(latents, out_grad, w_qkv, mod_table, timesteps, text_len):
    y = lax.axis_index("y")
    p = lax.rem(lax.axis_index("xl") + y, 2)
    half = lax.axis_index("xh")
    core = lax.axis_index("c")
    halves = lax.axis_size("xh")
    depth = lax.axis_size("z")
    cores = lax.axis_size("c")
    count, _, seq, width = latents.shape
    share = w_qkv.shape[1]
    chunk = width // QUART
    cols = 3 * chunk
    rows = PAIR * seq
    nj = BLOCKS // 2
    count_z = max(384 // (cores * share), 1)
    strips = width // (cores * count_z * share)
    levels = mod_table.shape[1]

    def swap(value, axis):
        return lax.ppermute(value, axis, [(0, 1), (1, 0)])

    fine = ("y", "xl")

    def route(dy, back, group):
        pairs = []
        for yy in range(QUART):
            to = (yy + dy) % QUART
            if group is not None and to // 2 != group:
                continue
            for xx in range(2):
                there = (xx + (yy if back else to)) % 2
                pairs.append((yy * 2 + xx, to * 2 + there))
        return pairs

    def pick(stack, index):
        return lax.dynamic_index_in_dim(stack, index, 0, keepdims=False)

    quarters = w_qkv[0].reshape(share, 3, QUART, chunk).transpose(2, 0, 1, 3)
    quarters = quarters.reshape(QUART, share, cols)
    leaves = [pick(quarters, lax.rem(y + dy, QUART)) for dy in range(QUART)]
    arrived = jnp.stack(
        [lax.ppermute(leaves[dy], fine, route(dy, False, None)) for dy in range(QUART)]
    )
    gathered = []
    for g in range(nj // 2):
        mine = jnp.stack(
            [pick(arrived, lax.rem(y + QUART - j, QUART)) for j in (2 * g, 2 * g + 1)]
        )
        if g > 0:
            mine, _ = lax.optimization_barrier((mine, part))
        if halves == 2:
            other = swap(mine, "xh")
            mine = [jnp.where(half == h, mine, other) for h in range(2)]
            part = jnp.stack(mine, axis=1)
        else:
            part = mine[:, None]
        gathered.append(lax.all_gather(part, "z", axis=0))

    onehot = (timesteps[:, 0][:, None] == jnp.arange(levels, dtype=jnp.int32)[None, :]).astype(F32)
    table, _ = lax.optimization_barrier((mod_table, arrived))
    modulations = jnp.dot(
        onehot, table[0].reshape(levels, 3 * width), precision=lax.Precision.HIGHEST
    ).reshape(count, 3, width)
    mods = jnp.stack(
        [lax.ppermute(modulations, fine, route(dy, False, None)) for dy in range(QUART)]
    )
    gates = lax.dynamic_slice_in_dim(mods[:, :, 2:3, :], y * chunk, chunk, axis=3)
    scal = jnp.concatenate(
        [jnp.stack([y, core, p]).astype(jnp.int32), text_len[:, 0].astype(jnp.int32)]
    )
    entering = latents.reshape(count // PAIR, rows, width)
    leaving = lax.dynamic_slice_in_dim(
        out_grad.reshape(count // PAIR, rows, width), y * chunk, chunk, axis=2
    )

    first, mods, gates, entering = lax.optimization_barrier((gathered[0], mods, gates, entering))
    pieces = [(first, swap(first, "c"))]
    routes = [
        [
            (yy * 2 + xx, ((yy + d) % QUART) * 2 + (1 + xx + d) % 2)
            for yy in range(QUART)
            for xx in range(2)
        ]
        for d in range(QUART)
    ]

    def send(parts):
        return [lax.ppermute(parts[d], ("y", "xl"), routes[d]) for d in range(QUART)]

    wscr = pltpu.VMEM((halves, depth, cores, share, cols), BF16)
    params = pltpu.CompilerParams(vmem_limit_bytes=VMEM_LIMIT)

    def held(k):
        first, second = min(k // 2, nj - 1), max((k - 1) // 2, 0)
        first, second = first // 2, second // 2
        if first == second:
            return pieces[first]
        return pieces[first] + pieces[second]

    def shape(cols, kind):
        return jax.ShapeDtypeStruct((rows, cols), kind)

    def kept(dims, kind):
        return pltpu.HBM(dims, kind)

    def pinned(values):
        return [pltpu.with_memory_space_constraint(value, pltpu.HBM) for value in values]

    steps = BLOCKS + 1
    saved = []
    received = None
    for k in range(steps):
        if k == 0:
            ins = [entering[0]]
        elif k == 1:
            ins = [entering[1]] + received
        else:
            ins = received
        loaded = k > 0
        weights = [ready] if loaded else pinned(held(k))
        sending = k < steps - 1
        outs = [
            kept((QUART, rows, chunk), BF16),
            kept((rows, width), BF16),
            kept((rows, cols), F32),
        ]
        if sending:
            outs = [shape(chunk, BF16)] + outs
        result = pl.pallas_call(
            functools.partial(forward_kernel, k, len(ins), len(weights), loaded, sending),
            out_shape=outs,
            in_specs=[SM] + [VM] * (len(ins) + 2) + [VM if loaded else HBM] * len(weights),
            out_specs=[VM] * sending + [HBM] * 3,
            scratch_shapes=[
                pltpu.VMEM((rows, width), BF16),
                pltpu.VMEM((rows, cols), F32),
                pltpu.VMEM((QUART, rows, chunk), BF16),
                pltpu.SemaphoreType.DMA((3,)),
            ]
            + ([] if loaded else [wscr, pltpu.SemaphoreType.DMA((halves,))]),
            compiler_params=params,
            name="forward_step",
        )(scal, *ins, mods, gates, *weights)
        if sending:
            received = send([result[0]] * QUART)
            result = result[1:]
        if k == 3:
            second, _ = lax.optimization_barrier((gathered[1], result[1]))
            pieces.append((second, swap(second, "c")))
        if sending:
            upcoming, received[0] = lax.optimization_barrier((list(held(k + 1)), received[0]))
            ready = pl.pallas_call(
                functools.partial(load_kernel, k + 1),
                out_shape=pltpu.VMEM((halves, depth, cores, share, cols), BF16),
                in_specs=[SM] + [HBM] * len(upcoming),
                out_specs=VM,
                scratch_shapes=[pltpu.SemaphoreType.DMA((halves,))],
                compiler_params=params,
                name="load_weights",
            )(scal, *pinned(upcoming))
        saved.append(result)

    lows = [None] * steps
    chips = [None] * nj
    rings = [None] * (nj // 2)
    received = None
    for k in reversed(range(steps)):
        if k == steps - 1:
            ins = [leaving[1]]
        elif k == steps - 2:
            ins = [leaving[0]] + received
        else:
            ins = received
        weights = held(k)
        sending = k > 0
        outs = [shape(chunk, BF16)] * (QUART * sending) + [kept((rows, cols), BF16)]
        hidden, _, projected = saved[k]
        result = pl.pallas_call(
            functools.partial(backward_kernel, k, len(ins), len(weights), sending),
            out_shape=outs,
            in_specs=[SM] + [VM] * (len(ins) + 3) + [HBM] * (1 + len(weights)),
            out_specs=[VM] * (len(outs) - 1) + [HBM],
            scratch_shapes=[
                pltpu.VMEM((rows, cols), BF16),
                wscr,
                pltpu.VMEM((QUART, rows, chunk), BF16),
                pltpu.VMEM((rows, chunk), F32),
                pltpu.VMEM((rows, cols), F32),
                pltpu.VMEM((QUART, rows, chunk), F32),
                pltpu.SemaphoreType.DMA((halves,)),
                pltpu.SemaphoreType.DMA((3,)),
            ],
            compiler_params=params,
            name="backward_step",
        )(scal, *ins, mods, gates, projected, *pinned([hidden, *weights]))
        lows[k] = result[-1]
        if sending:
            received = send(result[:-1])
        if k % 2 == 0 and k < steps - 1:
            j = k // 2
            factors = [saved[k + i][1] for i in range(3)] + [lows[k + i] for i in range(3)]
            if sending:
                factors, received[0] = lax.optimization_barrier((factors, received[0]))
            partial = pl.pallas_call(
                weight_grad_kernel,
                out_shape=[kept((depth, halves, share, cols), BF16)] * cores,
                in_specs=[SM] + [HBM] * 6,
                out_specs=[HBM] * cores,
                scratch_shapes=[
                    pltpu.VMEM((2 * rows, width), BF16),
                    pltpu.VMEM((2 * rows, cols), BF16),
                    pltpu.VMEM((strips, cores, count_z, share, cols), BF16),
                    pltpu.SemaphoreType.DMA((4 + strips * cores,)),
                ],
                compiler_params=params,
                cost_estimate=pl.CostEstimate(
                    flops=4 * rows * width * cols,
                    bytes_accessed=4 * width * cols,
                    transcendentals=0,
                ),
                name="weight_grad",
            )(scal, *pinned(factors))
            if sending:
                partial, received[1] = lax.optimization_barrier((partial, received[1]))
            chips[j] = partial
        if k in (1, 3, 5):
            j = (k + 1) // 2
            chips[j], _ = lax.optimization_barrier((chips[j], lows[k]))
        if k in (0, 1, 3, 5):
            j = (k + 1) // 2
            chips[j] = (chips[j][0], swap(chips[j][1], "c"))
        if k == 4 and sending:
            keep, received[1] = lax.optimization_barrier((chips[3][1], received[1]))
            chips[3] = (chips[3][0], keep)
        if k in (0, 3):
            g = k // 3
            total = jnp.concatenate(
                [
                    (chips[i][0] + chips[i][1]).reshape(depth, halves * share, cols)
                    for i in (2 * g, 2 * g + 1)
                ],
                axis=1,
            )
            if sending:
                total, received[1] = lax.optimization_barrier((total, received[1]))
            else:
                total, rings[1] = lax.optimization_barrier((total, rings[1]))
            rings[g] = lax.psum_scatter(total, "z", scatter_dimension=0)

    def hand_back(g):
        ring = rings[g].reshape(2, halves, share, cols)
        ours = lax.dynamic_index_in_dim(ring, half, 1, keepdims=False)
        if halves == 2:
            theirs = swap(lax.dynamic_index_in_dim(ring, 1 - half, 1, keepdims=False), "xh")
            ours = (ours.astype(F32) + theirs.astype(F32)).astype(BF16)
        return [
            lax.ppermute(pick(ours, lax.rem(y + dy, 2)), fine, route(dy, True, g))
            for dy in range(QUART)
        ]

    upper = hand_back(1)
    rings[0], upper = lax.optimization_barrier((rings[0], upper))
    lower = hand_back(0)
    grads = pl.pallas_call(
        assemble_kernel,
        out_shape=jax.ShapeDtypeStruct((share, 3 * width), F32),
        in_specs=[SM] + [VM] * (2 * QUART),
        out_specs=VM,
        scratch_shapes=[pltpu.VMEM((QUART, share, cols), F32)],
        compiler_params=params,
        name="assemble",
    )(scal, *upper, *lower)
    return grads[None]


def solution(mesh):
    fine = Mesh(mesh.devices.reshape(4, 2, 2, 8, 2), ("y", "xl", "xh", "z", "c"))
    pipe = ("y", "xl")
    dp = ("xh", "z", "c")
    return jax.shard_map(
        shards,
        mesh=fine,
        in_specs=(
            P(None, dp, None, None),
            P(None, dp, None, None),
            P(pipe, dp, None),
            P(pipe, None, None, None),
            P(None, dp),
            P(None, dp),
        ),
        out_specs=P(pipe, dp, None),
        check_vma=False,
    )
```

```python
import functools
import math

import jax
import jax.numpy as jnp
from jax import lax
from jax.experimental import pallas as pl
from jax.experimental.pallas import tpu as pltpu
from jax.sharding import Mesh
from jax.sharding import PartitionSpec as P

IMG = 40
EPS = 1e-06
HDIM = 128
BLOCKS = 8
QUART = 4
PAIR = 2
F32 = jnp.float32
BF16 = jnp.bfloat16
VMEM_LIMIT = 16 * 1024 * 1024
VM = pl.BlockSpec(memory_space=pltpu.VMEM)
SM = pl.BlockSpec(memory_space=pltpu.SMEM)
HBM = pl.BlockSpec(memory_space=pltpu.HBM)


def place(scal, k):
    p = scal[2]
    j = lax.max((k - p + 2) // 2 - 1, 0)
    j = lax.min(j, BLOCKS // 2 - 1)
    return lax.rem(k + p, 2), j, lax.rem(scal[0] + QUART - j, QUART)


def fetch_weights(scal, j, pieces, wscr, sem):
    c = scal[1]
    halves = wscr.shape[0]
    inner = lax.rem(j, 2)

    def start(own, other):
        for t in range(halves):
            pltpu.make_async_copy(own.at[:, inner, t], wscr.at[t, :, c], sem.at[t]).start()
            pltpu.make_async_copy(other.at[:, inner, t], wscr.at[t, :, 1 - c], sem.at[t]).start()

    if len(pieces) == 2:
        start(*pieces)
    else:

        @pl.when(scal[2] == 0)
        def _():
            start(*pieces[:2])

        @pl.when(scal[2] != 0)
        def _():
            start(*pieces[2:])


def half_weights(wscr, sem, t):
    if sem is not None:
        pltpu.make_async_copy(wscr.at[t], wscr.at[t], sem.at[t]).wait()
    value = wscr[t]
    return value.reshape(value.shape[0] * value.shape[1] * value.shape[2], value.shape[3])


def standardize(hidden):
    average = jnp.mean(hidden, axis=-1, keepdims=True)
    centered = hidden - average
    variance = jnp.mean(centered * centered, axis=-1, keepdims=True)
    scale = lax.rsqrt(variance + EPS)
    return centered * scale, scale


def nt(a, b):
    return lax.dot_general(
        a.astype(BF16), b.astype(BF16), (((1,), (1,)), ((), ())), preferred_element_type=F32
    )


def nn(a, b):
    return lax.dot_general(
        a.astype(BF16), b.astype(BF16), (((1,), (0,)), ((), ())), preferred_element_type=F32
    )


def tn(a, b):
    return lax.dot_general(
        a.astype(BF16), b.astype(BF16), (((0,), (0,)), ((), ())), preferred_element_type=F32
    )


def unit(rows):
    scale = lax.rsqrt(jnp.mean(rows * rows, axis=-1, keepdims=True) + EPS)
    return rows * scale, scale


def weights_of(q, k, length):
    scores = nt(q, k) * (1.0 / math.sqrt(HDIM))
    position = lax.broadcasted_iota(jnp.int32, scores.shape, 1)
    usable = (position < IMG) | (position - IMG < length)
    weights = jnp.where(usable, jnp.exp(scores), 0.0)
    return weights / jnp.sum(weights, axis=-1, keepdims=True)


def load_hidden(scal, ins, hs):
    y = scal[0]
    chunk = hs.shape[2]

    def from_whole(ref):
        for t in range(QUART):
            hs[t] = ref[:, t * chunk : (t + 1) * chunk]

    def from_chunks(parts):
        for d in range(QUART):
            hs[lax.rem(y + QUART - d, QUART)] = parts[d][...]

    if len(ins) == 1:
        from_whole(ins[0])
    elif len(ins) == QUART:
        from_chunks(ins)
    else:

        @pl.when(scal[2] == 0)
        def _():
            from_whole(ins[0])

        @pl.when(scal[2] != 0)
        def _():
            from_chunks(ins[1:])


def whole(hs):
    return jnp.concatenate([hs[t].astype(F32) for t in range(QUART)], axis=1)


def load_kernel(k, scal, *refs):
    pieces, (out, sem) = refs[:-2], refs[-2:]
    fetch_weights(scal, place(scal, k)[1], pieces, out, sem)
    for t in range(out.shape[0]):
        pltpu.make_async_copy(out.at[t], out.at[t], sem.at[t]).wait()


def forward_kernel(k, n_in, n_w, loaded, send, scal, *refs):
    ins, refs = refs[:n_in], refs[n_in:]
    mods, gates = refs[:2]
    pieces, refs = refs[2 : 2 + n_w], refs[2 + n_w :]
    if send:
        out_ref, refs = refs[0], refs[1:]
    hidden_out, normed_out, proj_out, normed_ref, proj_ref, hs, sems = refs[:7]
    wscr, sem = (pieces[0], None) if loaded else refs[7:]
    hidden_save = pltpu.make_async_copy(hs, hidden_out, sems.at[2])
    normed_save = pltpu.make_async_copy(normed_ref, normed_out, sems.at[0])
    proj_save = pltpu.make_async_copy(proj_ref, proj_out, sems.at[1])
    y = scal[0]
    micro, j, slot = place(scal, k)
    if not loaded:
        fetch_weights(scal, j, pieces, wscr, sem)
    chunk = hs.shape[2]
    rows, width = normed_ref.shape
    seq = rows // PAIR
    load_hidden(scal, ins, hs)
    hidden_save.start()
    normal, _ = standardize(whole(hs))
    normal = normal.reshape(PAIR, seq, width)
    normed = jnp.concatenate(
        [
            (1.0 + mods[slot, PAIR * micro + s, 1:2, :]) * normal[s]
            + mods[slot, PAIR * micro + s, 0:1, :]
            for s in range(PAIR)
        ],
        axis=0,
    ).astype(BF16)
    normed_ref[...] = normed
    normed_save.start()
    halves = wscr.shape[0]
    span = width // halves
    projected = nn(normed[:, :span], half_weights(wscr, sem, 0))
    for t in range(1, halves):
        projected += nn(normed[:, t * span : (t + 1) * span], half_weights(wscr, sem, t))
    proj_ref[...] = projected
    proj_save.start()
    if not send:
        normed_save.wait()
        hidden_save.wait()
        proj_save.wait()
        return
    own = hs[y].astype(F32)
    for s in range(PAIR):
        length = scal[3 + PAIR * micro + s]
        r = slice(s * seq, (s + 1) * seq)
        mixed = []
        for h in range(chunk // HDIM):
            lo = h * HDIM
            q, _ = unit(proj_ref[r, lo : lo + HDIM])
            key, _ = unit(proj_ref[r, chunk + lo : chunk + lo + HDIM])
            v = proj_ref[r, 2 * chunk + lo : 2 * chunk + lo + HDIM]
            mixed.append(nn(weights_of(q, key, length), v))
        mixture = jnp.concatenate(mixed, axis=1)
        gate = gates[slot, PAIR * micro + s]
        hs_rows = own[r] + gate * mixture
        if s == 0:
            first = hs_rows
    out_ref[...] = jnp.concatenate([first, hs_rows], axis=0).astype(BF16)
    normed_save.wait()
    hidden_save.wait()
    proj_save.wait()


def backward_kernel(k, n_in, n_w, loaded, send, scal, *refs):
    ins, refs = refs[:n_in], refs[n_in:]
    mods, gates, proj_ref, hidden = refs[:4]
    pieces, refs = refs[4 : 4 + n_w], refs[4 + n_w :]
    outs, refs = refs[: QUART * send], refs[QUART * send :]
    low_out, low_ref, hs, gs, dp, ds, sems = refs[:7]
    wscr, sem = (pieces[0], None) if loaded else refs[7:]
    low_save = pltpu.make_async_copy(low_ref, low_out, sems.at[0])
    y = scal[0]
    micro, j, slot = place(scal, k)
    if send:
        hidden_load = pltpu.make_async_copy(hidden, hs, sems.at[2])
        hidden_load.start()
        if not loaded:
            fetch_weights(scal, j, pieces, wscr, sem)
    rows, chunk = gs.shape
    width = chunk * QUART
    seq = rows // PAIR

    def total(parts):
        gs[...] = sum([part[...].astype(F32) for part in parts[1:]], parts[0][...].astype(F32))

    if n_in in (1, QUART):
        total(ins)
    else:

        @pl.when(scal[2] != 0)
        def _():
            total(ins[:1])

        @pl.when(scal[2] == 0)
        def _():
            total(ins[1:])

    root = 1.0 / math.sqrt(HDIM)
    for s in range(PAIR):
        length = scal[3 + PAIR * micro + s]
        r = slice(s * seq, (s + 1) * seq)
        for h in range(chunk // HDIM):
            lo = h * HDIM
            c = slice(lo, lo + HDIM)
            gate = gates[slot, PAIR * micro + s, :, c]
            dmix = gs[r, c] * gate
            q, rq = unit(proj_ref[r, lo : lo + HDIM])
            key, rk = unit(proj_ref[r, chunk + lo : chunk + lo + HDIM])
            v = proj_ref[r, 2 * chunk + lo : 2 * chunk + lo + HDIM]
            att = weights_of(q, key, length)
            datt = nt(dmix, v)
            dscore = att * (datt - jnp.sum(att * datt, axis=-1, keepdims=True)) * root
            dqn = nn(dscore, key)
            dkn = tn(dscore, q)
            dp[r, c] = rq * (dqn - q * jnp.mean(dqn * q, axis=-1, keepdims=True))
            dp[r, chunk + lo : chunk + lo + HDIM] = rk * (
                dkn - key * jnp.mean(dkn * key, axis=-1, keepdims=True)
            )
            dp[r, 2 * chunk + lo : 2 * chunk + lo + HDIM] = tn(att, dmix)
    low = dp[...].astype(BF16)
    low_ref[...] = low
    low_save.start()
    if not send:
        low_save.wait()
        return
    hidden_load.wait()
    normal, scale = standardize(whole(hs))
    halves = wscr.shape[0]
    norm_grad = jnp.concatenate([nt(low, half_weights(wscr, sem, t)) for t in range(halves)], axis=1)
    norm_grad = norm_grad.reshape(PAIR, seq, width)
    grad = jnp.concatenate(
        [(1.0 + mods[slot, PAIR * micro + s, 1:2, :]) * norm_grad[s] for s in range(PAIR)], axis=0
    )
    back = scale * (
        grad
        - jnp.mean(grad, axis=-1, keepdims=True)
        - normal * jnp.mean(grad * normal, axis=-1, keepdims=True)
    )
    for t in range(QUART):
        ds[t] = back[:, t * chunk : (t + 1) * chunk]
    ds[y] = ds[y] + gs[...]
    for d in range(QUART):
        outs[d][...] = ds[lax.rem(y + d, QUART)].astype(BF16)
    low_save.wait()


def weight_grad_kernel(scal, n0, n1, n2, g0, g1, g2, near, far, nscr, gscr, held, sems):
    c = scal[1]
    rows = n0.shape[0]

    def start(normed, grad):
        pltpu.make_async_copy(normed, nscr.at[0:rows], sems.at[0]).start()
        pltpu.make_async_copy(grad, gscr.at[0:rows], sems.at[1]).start()

    pltpu.make_async_copy(n1, nscr.at[rows : 2 * rows], sems.at[2]).start()
    pltpu.make_async_copy(g1, gscr.at[rows : 2 * rows], sems.at[3]).start()

    @pl.when(scal[2] == 0)
    def _():
        start(n0, g0)

    @pl.when(scal[2] != 0)
    def _():
        start(n2, g2)

    pltpu.make_async_copy(n0, nscr.at[0:rows], sems.at[0]).wait()
    pltpu.make_async_copy(g0, gscr.at[0:rows], sems.at[1]).wait()
    pltpu.make_async_copy(n1, nscr.at[rows : 2 * rows], sems.at[2]).wait()
    pltpu.make_async_copy(g1, gscr.at[rows : 2 * rows], sems.at[3]).wait()
    share = near.shape[2]
    depth = near.shape[0]
    steps, cores, count = held.shape[:3]
    per = cores * count * share
    right = gscr[...]
    saves = []
    for t in range(steps):
        value = tn(nscr[:, t * per : (t + 1) * per], right).astype(BF16)
        half, z = divmod(t * count, depth)
        for core in range(cores):
            for u in range(count):
                at = (u * cores + core) * share
                held[t, core, u] = value[at : at + share]
            sem = sems.at[4 + t * cores + core]

            def save(out):
                return pltpu.make_async_copy(held.at[t, core], out.at[z : z + count, half], sem)

            @pl.when(c == core)
            def _():
                save(near).start()

            @pl.when(c != core)
            def _():
                save(far).start()

            saves.append(save(near))
    for save in saves:
        save.wait()


def assemble_kernel(scal, *refs):
    parts, (out, held) = refs[: 2 * QUART], refs[2 * QUART :]
    y = scal[0]
    chunk = out.shape[1] // (3 * QUART)
    for dy in range(QUART):
        total = parts[dy][...].astype(F32) + parts[QUART + dy][...].astype(F32)
        held[lax.rem(y + QUART - dy, QUART)] = total
    for q in range(QUART):
        for i in range(3):
            at = (i * QUART + q) * chunk
            out[:, at : at + chunk] = held[q][:, i * chunk : (i + 1) * chunk]


def shards(latents, out_grad, w_qkv, mod_table, timesteps, text_len):
    y = lax.axis_index("y")
    p = lax.rem(lax.axis_index("xl") + y, 2)
    half = lax.axis_index("xh")
    core = lax.axis_index("c")
    halves = lax.axis_size("xh")
    depth = lax.axis_size("z")
    cores = lax.axis_size("c")
    count, _, seq, width = latents.shape
    share = w_qkv.shape[1]
    chunk = width // QUART
    cols = 3 * chunk
    rows = PAIR * seq
    nj = BLOCKS // 2
    count_z = max(384 // (cores * share), 1)
    strips = width // (cores * count_z * share)
    levels = mod_table.shape[1]

    def swap(value, axis):
        return lax.ppermute(value, axis, [(0, 1), (1, 0)])

    fine = ("y", "xl")

    def route(dy, back, group):
        pairs = []
        for yy in range(QUART):
            to = (yy + dy) % QUART
            if group is not None and to // 2 != group:
                continue
            for xx in range(2):
                there = (xx + (yy if back else to)) % 2
                pairs.append((yy * 2 + xx, to * 2 + there))
        return pairs

    def pick(stack, index):
        return lax.dynamic_index_in_dim(stack, index, 0, keepdims=False)

    quarters = w_qkv[0].reshape(share, 3, QUART, chunk).transpose(2, 0, 1, 3)
    quarters = quarters.reshape(QUART, share, cols)
    leaves = [pick(quarters, lax.rem(y + dy, QUART)) for dy in range(QUART)]
    arrived = jnp.stack(
        [lax.ppermute(leaves[dy], fine, route(dy, False, None)) for dy in range(QUART)]
    )
    gathered = []
    for g in range(nj // 2):
        mine = jnp.stack(
            [pick(arrived, lax.rem(y + QUART - j, QUART)) for j in (2 * g, 2 * g + 1)]
        )
        if g > 0:
            mine, _ = lax.optimization_barrier((mine, part))
        if halves == 2:
            other = swap(mine, "xh")
            mine = [jnp.where(half == h, mine, other) for h in range(2)]
            part = jnp.stack(mine, axis=1)
        else:
            part = mine[:, None]
        gathered.append(lax.all_gather(part, "z", axis=0))

    onehot = (timesteps[:, 0][:, None] == jnp.arange(levels, dtype=jnp.int32)[None, :]).astype(F32)
    table, _ = lax.optimization_barrier((mod_table, arrived))
    modulations = jnp.dot(
        onehot, table[0].reshape(levels, 3 * width), precision=lax.Precision.HIGHEST
    ).reshape(count, 3, width)
    mods = jnp.stack(
        [lax.ppermute(modulations, fine, route(dy, False, None)) for dy in range(QUART)]
    )
    gates = lax.dynamic_slice_in_dim(mods[:, :, 2:3, :], y * chunk, chunk, axis=3)
    scal = jnp.concatenate(
        [jnp.stack([y, core, p]).astype(jnp.int32), text_len[:, 0].astype(jnp.int32)]
    )
    entering = latents.reshape(count // PAIR, rows, width)
    leaving = lax.dynamic_slice_in_dim(
        out_grad.reshape(count // PAIR, rows, width), y * chunk, chunk, axis=2
    )

    first, mods, gates, entering = lax.optimization_barrier((gathered[0], mods, gates, entering))
    pieces = [(first, swap(first, "c"))]
    routes = [
        [
            (yy * 2 + xx, ((yy + d) % QUART) * 2 + (1 + xx + d) % 2)
            for yy in range(QUART)
            for xx in range(2)
        ]
        for d in range(QUART)
    ]

    def send(parts):
        return [lax.ppermute(parts[d], ("y", "xl"), routes[d]) for d in range(QUART)]

    wscr = pltpu.VMEM((halves, depth, cores, share, cols), BF16)
    params = pltpu.CompilerParams(vmem_limit_bytes=VMEM_LIMIT)

    def held(k):
        first, second = min(k // 2, nj - 1), max((k - 1) // 2, 0)
        first, second = first // 2, second // 2
        if first == second:
            return pieces[first]
        return pieces[first] + pieces[second]

    def shape(cols, kind):
        return jax.ShapeDtypeStruct((rows, cols), kind)

    def kept(dims, kind):
        return pltpu.HBM(dims, kind)

    def pinned(values):
        return [pltpu.with_memory_space_constraint(value, pltpu.HBM) for value in values]

    def load(k, after):
        upcoming, after = lax.optimization_barrier((list(held(k)), after))
        value = pl.pallas_call(
            functools.partial(load_kernel, k),
            out_shape=pltpu.VMEM((halves, depth, cores, share, cols), BF16),
            in_specs=[SM] + [HBM] * len(upcoming),
            out_specs=VM,
            scratch_shapes=[pltpu.SemaphoreType.DMA((halves,))],
            compiler_params=params,
            name="load_weights",
        )(scal, *pinned(upcoming))
        return value, after

    steps = BLOCKS + 1
    saved = []
    received = None
    for k in range(steps):
        if k == 0:
            ins = [entering[0]]
        elif k == 1:
            ins = [entering[1]] + received
        else:
            ins = received
        loaded = k > 0
        weights = [ready] if loaded else pinned(held(k))
        sending = k < steps - 1
        outs = [
            kept((QUART, rows, chunk), BF16),
            kept((rows, width), BF16),
            kept((rows, cols), F32),
        ]
        if sending:
            outs = [shape(chunk, BF16)] + outs
        result = pl.pallas_call(
            functools.partial(forward_kernel, k, len(ins), len(weights), loaded, sending),
            out_shape=outs,
            in_specs=[SM] + [VM] * (len(ins) + 2) + [VM if loaded else HBM] * len(weights),
            out_specs=[VM] * sending + [HBM] * 3,
            scratch_shapes=[
                pltpu.VMEM((rows, width), BF16),
                pltpu.VMEM((rows, cols), F32),
                pltpu.VMEM((QUART, rows, chunk), BF16),
                pltpu.SemaphoreType.DMA((3,)),
            ]
            + ([] if loaded else [wscr, pltpu.SemaphoreType.DMA((halves,))]),
            compiler_params=params,
            name="forward_step",
        )(scal, *ins, mods, gates, *weights)
        if sending:
            received = send([result[0]] * QUART)
            result = result[1:]
        if k == 3:
            second, _ = lax.optimization_barrier((gathered[1], result[1]))
            pieces.append((second, swap(second, "c")))
        if sending:
            ready, received[0] = load(k + 1, received[0])
        saved.append(result)

    lows = [None] * steps
    chips = [None] * nj
    rings = [None] * (nj // 2)
    received = None
    for k in reversed(range(steps)):
        if k == steps - 1:
            ins = [leaving[1]]
        elif k == steps - 2:
            ins = [leaving[0]] + received
        else:
            ins = received
        loaded = k > 0 and k % 2 == 0
        weights = [ready] if loaded else pinned(held(k))
        sending = k > 0
        outs = [shape(chunk, BF16)] * (QUART * sending) + [kept((rows, cols), BF16)]
        hidden, _, projected = saved[k]
        result = pl.pallas_call(
            functools.partial(backward_kernel, k, len(ins), len(weights), loaded, sending),
            out_shape=outs,
            in_specs=[SM] + [VM] * (len(ins) + 3) + [HBM] + [VM if loaded else HBM] * len(weights),
            out_specs=[VM] * (len(outs) - 1) + [HBM],
            scratch_shapes=[
                pltpu.VMEM((rows, cols), BF16),
                pltpu.VMEM((QUART, rows, chunk), BF16),
                pltpu.VMEM((rows, chunk), F32),
                pltpu.VMEM((rows, cols), F32),
                pltpu.VMEM((QUART, rows, chunk), F32),
                pltpu.SemaphoreType.DMA((3,)),
            ]
            + ([] if loaded else [wscr, pltpu.SemaphoreType.DMA((halves,))]),
            compiler_params=params,
            name="backward_step",
        )(scal, *ins, mods, gates, projected, *pinned([hidden]), *weights)
        lows[k] = result[-1]
        if sending:
            received = send(result[:-1])
            if k in (3, 5, 7):
                ready, received[0] = load(k - 1, received[0])
        if k % 2 == 0 and k < steps - 1:
            j = k // 2
            factors = [saved[k + i][1] for i in range(3)] + [lows[k + i] for i in range(3)]
            if sending:
                factors, received[0] = lax.optimization_barrier((factors, received[0]))
            partial = pl.pallas_call(
                weight_grad_kernel,
                out_shape=[kept((depth, halves, share, cols), BF16)] * cores,
                in_specs=[SM] + [HBM] * 6,
                out_specs=[HBM] * cores,
                scratch_shapes=[
                    pltpu.VMEM((2 * rows, width), BF16),
                    pltpu.VMEM((2 * rows, cols), BF16),
                    pltpu.VMEM((strips, cores, count_z, share, cols), BF16),
                    pltpu.SemaphoreType.DMA((4 + strips * cores,)),
                ],
                compiler_params=params,
                cost_estimate=pl.CostEstimate(
                    flops=4 * rows * width * cols,
                    bytes_accessed=4 * width * cols,
                    transcendentals=0,
                ),
                name="weight_grad",
            )(scal, *pinned(factors))
            if sending:
                partial, received[1] = lax.optimization_barrier((partial, received[1]))
            chips[j] = partial
        if k in (1, 3, 5):
            j = (k + 1) // 2
            chips[j], _ = lax.optimization_barrier((chips[j], lows[k]))
        if k in (0, 1, 3, 5):
            j = (k + 1) // 2
            chips[j] = (chips[j][0], swap(chips[j][1], "c"))
        if k == 4 and sending:
            keep, received[1] = lax.optimization_barrier((chips[3][1], received[1]))
            chips[3] = (chips[3][0], keep)
        if k in (0, 3):
            g = k // 3
            total = jnp.concatenate(
                [
                    (chips[i][0] + chips[i][1]).reshape(depth, halves * share, cols)
                    for i in (2 * g, 2 * g + 1)
                ],
                axis=1,
            )
            if sending:
                total, received[1] = lax.optimization_barrier((total, received[1]))
            else:
                total, rings[1] = lax.optimization_barrier((total, rings[1]))
            rings[g] = lax.psum_scatter(total, "z", scatter_dimension=0)

    def hand_back(g):
        ring = rings[g].reshape(2, halves, share, cols)
        ours = lax.dynamic_index_in_dim(ring, half, 1, keepdims=False)
        if halves == 2:
            theirs = swap(lax.dynamic_index_in_dim(ring, 1 - half, 1, keepdims=False), "xh")
            ours = (ours.astype(F32) + theirs.astype(F32)).astype(BF16)
        return [
            lax.ppermute(pick(ours, lax.rem(y + dy, 2)), fine, route(dy, True, g))
            for dy in range(QUART)
        ]

    upper = hand_back(1)
    rings[0], upper = lax.optimization_barrier((rings[0], upper))
    lower = hand_back(0)
    grads = pl.pallas_call(
        assemble_kernel,
        out_shape=jax.ShapeDtypeStruct((share, 3 * width), F32),
        in_specs=[SM] + [VM] * (2 * QUART),
        out_specs=VM,
        scratch_shapes=[pltpu.VMEM((QUART, share, cols), F32)],
        compiler_params=params,
        name="assemble",
    )(scal, *upper, *lower)
    return grads[None]


def solution(mesh):
    fine = Mesh(mesh.devices.reshape(4, 2, 2, 8, 2), ("y", "xl", "xh", "z", "c"))
    pipe = ("y", "xl")
    dp = ("xh", "z", "c")
    return jax.shard_map(
        shards,
        mesh=fine,
        in_specs=(
            P(None, dp, None, None),
            P(None, dp, None, None),
            P(pipe, dp, None),
            P(pipe, None, None, None),
            P(None, dp),
            P(None, dp),
        ),
        out_specs=P(pipe, dp, None),
        check_vma=False,
    )
```
